512 devices in a mesh: seq: 64 (over z_hi, y, core), head: 8 (over z_lo, x).
Axes of the slice: x: 4, y: 8, z: 8 (z_hi: 4, z_lo: 2; z = z_hi * 2 + z_lo), core: 2. Of those that a mesh axis runs over, the one named last changes fastest.
Arguments:
- queries: bfloat16 [16384, 8, 4, 128], P(('seq', 'head')), may hold values from -210 to 210
- keys: bfloat16 [16384, 8, 128], P(('seq', 'head')), may hold values from -6 to 6
- values: bfloat16 [16384, 8, 128], P(('seq', 'head')), may hold values from -6 to 6
- d_attended: bfloat16 [16384, 8, 4, 128], P(('seq', 'head')), may hold values from -12 to 12
- shift_amounts: int32 [8], replicated, may hold values from 0 to 1024, as said below
Outputs:
- attended: bfloat16 [16384, 8, 4, 128], P(('seq', 'head'))
- d_queries: bfloat16 [16384, 8, 4, 128], P(('seq', 'head'))
- d_keys: bfloat16 [16384, 8, 128], P(('seq', 'head'))
- d_values: bfloat16 [16384, 8, 128], P(('seq', 'head'))
The draws below stay inside these ranges and needn't reach their ends.
Inputs may be any that keep to these rules, and one draw needn't show every extreme that they name: `shift_amounts`: each head's shift is 0 or 1024, and exactly half of the 8 heads have 2048 // 2.
All inputs are finite; a program needn't handle non-finite values.
Results may differ from the reference program's by a relative error of at most 0.034.
Values may be sent and summed in bfloat16 or wider, within the bound.
No kernel may reach another device: no remote copies, remote signals or barrier semaphores. Data moves between devices by JAX's collectives and lax.ppermute only.
A program may use at most 64 MiB of HBM per device.

```python
import math
import jax
import jax.numpy as jnp
from jax import lax

HD = 128
KV_HEADS = 8
QPK = 4
GROUP = 2048
TOKENS = 16384


def base_keys(key):
    return jax.random.truncated_normal(key, -6.0, 6.0, (TOKENS, KV_HEADS, HD), jnp.float32)


def draw_keys(key, part):
    shared = base_keys(key)
    return shared.astype(jnp.bfloat16)


def draw_queries(key, part):
    key = jax.random.fold_in(key, 5)
    drawn = jax.random.truncated_normal(key, -6.0, 6.0, (TOKENS, KV_HEADS, QPK, HD), jnp.float32)
    return drawn.astype(jnp.bfloat16)


def draw_shift_amounts(key, part):
    key = jax.random.fold_in(key, 7)
    order = jax.random.permutation(key, KV_HEADS)
    return jnp.where(order < KV_HEADS // 2, GROUP // 2, 0).astype(jnp.int32)


def steps_of(stream_key, shape, cuts, low, high):
    def one(axis_at, shards_of):
        draws = jax.random.uniform(jax.random.fold_in(jax.random.fold_in(stream_key, 6), axis_at), (shards_of,), jnp.float32, low / len(cuts), high / len(cuts))
        return jnp.repeat(jnp.exp(draws), shape[axis_at] // shards_of).reshape((-1,) + (1,) * (len(shape) - axis_at - 1))

    loudness = one(*cuts[0])
    for cut in cuts[1:]:
        loudness = loudness * one(*cut)
    return loudness


def normal_values(rng, extent, width, reach, cuts=(), held_as=jnp.bfloat16):
    entries = jax.random.normal(rng, extent, jnp.float32) * width
    if len(cuts) > 0:
        entries = steps_of(rng, extent, cuts, -0.22, 0.18) * entries
    return jnp.clip(entries, min=-reach, max=reach).astype(held_as)


def setup_inputs(seed: int = 0) -> dict:
    streams_of = jax.random.split(jax.random.key(seed), 6)
    queries = draw_queries(jax.random.fold_in(streams_of[5], 71), 0)
    keys = draw_keys(jax.random.fold_in(streams_of[5], 71), 0)
    values = normal_values(streams_of[2], (TOKENS, KV_HEADS, HD), 1.0, 6.0, ((0, 512),))
    d_attended = normal_values(streams_of[3], (TOKENS, KV_HEADS, QPK, HD), 2.0, 12.0, ((0, 512),))
    shift_amounts = draw_shift_amounts(jax.random.fold_in(streams_of[5], 71), 0)
    return dict(queries=queries, keys=keys, values=values, d_attended=d_attended, shift_amounts=shift_amounts)


MASKED_LOGIT = -1e+30

def group_pass(block):
    q_block, k_block, v_block, d_block = block
    scaling = 1.0 / math.sqrt(HD)
    q_float = q_block.astype(jnp.float32)
    k_float = k_block.astype(jnp.float32)
    v_float = v_block.astype(jnp.float32)
    d_float = d_block.astype(jnp.float32)
    logits = jnp.einsum('tgd,ud->gtu', q_float, k_float) * scaling
    places = jnp.arange(GROUP, dtype=jnp.int32)
    causal = places[None, :] <= places[:, None]
    logits = jnp.where(causal[None], logits, MASKED_LOGIT)
    highest = lax.optimization_barrier(jnp.max(logits, axis=2, keepdims=True))
    lse = highest + jnp.log(lax.optimization_barrier(jnp.sum(jnp.exp(logits - highest), axis=2, keepdims=True)))
    exact_probs = jnp.exp(logits - lse)
    prob_rounded = lax.optimization_barrier(exact_probs.astype(jnp.bfloat16)).astype(jnp.float32)
    attended = jnp.einsum('gtu,ud->tgd', prob_rounded, v_float).astype(jnp.bfloat16)
    row_dot = lax.optimization_barrier(jnp.sum(d_float * attended.astype(jnp.float32), axis=2))
    d_probs = jnp.einsum('tgd,ud->gtu', d_float, v_float)
    d_scores = exact_probs * (d_probs - jnp.transpose(row_dot)[:, :, None])
    d_scores = lax.optimization_barrier(d_scores.astype(jnp.bfloat16)).astype(jnp.float32)
    d_queries = (jnp.einsum('gtu,ud->tgd', d_scores, k_float) * scaling).astype(jnp.bfloat16)
    d_keys = (jnp.einsum('gtu,tgd->ud', d_scores, q_float) * scaling).astype(jnp.bfloat16)
    d_values = jnp.einsum('gtu,tgd->ud', prob_rounded, d_float).astype(jnp.bfloat16)
    return (attended, d_queries, d_keys, d_values)

def head_pass(inputs):
    q_head, k_head, v_head, d_head, shift_value = inputs
    groups = TOKENS // GROUP
    rolled = [jnp.roll(item, -shift_value, axis=0) for item in (q_head, k_head, v_head, d_head)]
    shaped = [item.reshape((groups, GROUP) + item.shape[1:]) for item in rolled]
    results = lax.map(group_pass, tuple(shaped))
    return tuple((jnp.roll(item.reshape((TOKENS,) + item.shape[2:]), shift_value, axis=0) for item in results))

def reference(queries, keys, values, d_attended, shift_amounts):
    by_head = (jnp.moveaxis(queries, 1, 0), jnp.moveaxis(keys, 1, 0), jnp.moveaxis(values, 1, 0), jnp.moveaxis(d_attended, 1, 0), shift_amounts.astype(jnp.int32))
    attended, d_queries, d_keys, d_values = lax.map(head_pass, by_head)
    return (jnp.moveaxis(attended, 0, 1), jnp.moveaxis(d_queries, 0, 1), jnp.moveaxis(d_keys, 0, 1), jnp.moveaxis(d_values, 0, 1))
```

```python
import math

import jax
import jax.numpy as jnp
from jax import lax
from jax.experimental import pallas as pl
from jax.experimental.pallas import tpu as pltpu
from jax.sharding import PartitionSpec as P

GROUP = 2048
HEADS = 8
PER = 4
HD = 128
TOK = 256
SUB = 32
ROWS = TOK * PER
COLS = 512
LOG2E = 1.4426950408889634
NEG = -1e30
F32 = jnp.float32
BF16 = jnp.bfloat16
VM = pl.BlockSpec(memory_space=pltpu.VMEM)
SM = pl.BlockSpec(memory_space=pltpu.SMEM)
AXES = ("seq", "head")


def params():
    return pltpu.CompilerParams(vmem_limit_bytes=48 * 1024 * 1024)


def dot(a, b):
    return jnp.dot(a, b, preferred_element_type=F32)


def place_of_head(shift_ref, head):
    place = jnp.zeros(head.shape, jnp.int32)
    plain = jnp.int32(0)
    moved = jnp.int32(HEADS // 2)
    for h in range(HEADS):
        is_moved = (shift_ref[h] > 0).astype(jnp.int32)
        rank = jnp.where(is_moved == 1, moved, plain)
        place = jnp.where(head == h, rank, place)
        moved = moved + is_moved
        plain = plain + 1 - is_moved
    return place


def kv_order(shift_ref, back):
    local = lax.broadcasted_iota(jnp.int32, (TOK, TOK), 0 if back else 1)
    placed = lax.broadcasted_iota(jnp.int32, (TOK, TOK), 1 if back else 0)
    head = lax.broadcasted_iota(jnp.int32, (TOK, 1) if back else (1, TOK), 0 if back else 1) & 7
    place = place_of_head(shift_ref, head)
    hit = ((local >> 3) == (placed & 31)) & (place == (placed >> 5))
    return jnp.where(hit, 1.0, 0.0).astype(BF16)


def q_order(shift_ref, back):
    local = lax.broadcasted_iota(jnp.int32, (TOK, TOK), 0 if back else 1)
    placed = lax.broadcasted_iota(jnp.int32, (TOK, TOK), 1 if back else 0)
    head = lax.broadcasted_iota(jnp.int32, (TOK, 1) if back else (1, TOK), 0 if back else 1)
    place = place_of_head(shift_ref, (head >> 2) & 7)
    same = ((local >> 5) == ((placed & 31) >> 2)) & ((local & 3) == (placed & 3))
    return jnp.where(same & (place == (placed >> 5)), 1.0, 0.0).astype(BF16)


def pack_kv_kernel(shift_ref, k_ref, v_ref, out_ref):
    order = kv_order(shift_ref, False)
    for n, ref in enumerate((k_ref, v_ref)):
        moved = dot(order, ref[...]).astype(BF16)
        for h in range(HEADS):
            out_ref[h, n * SUB : (n + 1) * SUB, :] = moved[h * SUB : (h + 1) * SUB]


def pack_q_kernel(shift_ref, q_ref, d_ref, out_ref):
    order = q_order(shift_ref, False)
    for n, ref in enumerate((q_ref, d_ref)):
        for b in range(4):
            moved = dot(order, ref[b * TOK : (b + 1) * TOK, :]).astype(BF16)
            for h in range(HEADS):
                at = n * 128 + b * 32
                out_ref[h, at : at + 32, :] = moved[h * 32 : (h + 1) * 32]


def unpack_kv_kernel(shift_ref, in_ref, k_ref, v_ref):
    order = kv_order(shift_ref, True)
    for n, ref in enumerate((k_ref, v_ref)):
        held = in_ref[:, n * SUB : (n + 1) * SUB, :].reshape(TOK, HD)
        ref[...] = dot(order, held).astype(BF16)


def unpack_q_kernel(shift_ref, in_ref, o_ref, q_ref):
    order = q_order(shift_ref, True)
    for n, ref in enumerate((o_ref, q_ref)):
        for b in range(4):
            at = n * 128 + b * 32
            held = in_ref[:, at : at + 32, :].reshape(TOK, HD)
            ref[b * TOK : (b + 1) * TOK, :] = dot(order, held).astype(BF16)


def attend_kernel(
    where_ref, qd_ref, a0, a1, a2, a3, b0, b1, b2, b3,
    oq_ref, near_ref, far_ref,
    k_s, v_s, kt_s, vt_s, q_s, d_s, qt_s, dt_s, s_s, m_s, l_s, ot_s, dqt_s, dot_s,
):
    chips = where_ref[0]
    core = where_ref[1]
    scaling = 1.0 / math.sqrt(HD)
    exponent = scaling * LOG2E

    def stage(slot, ref):
        k = ref[:, 0:SUB, :].reshape(TOK, HD)
        v = ref[:, SUB : 2 * SUB, :].reshape(TOK, HD)
        k_s[slot] = k
        v_s[slot] = v
        kt_s[slot] = k.T
        vt_s[slot] = v.T

    q = qd_ref[:, 0:128, :].reshape(ROWS, HD)
    d = qd_ref[:, 128:256, :].reshape(ROWS, HD)
    q_s[...] = q
    d_s[...] = d
    qt_s[...] = q.T
    dt_s[...] = d.T
    for dist, (mine, other) in enumerate(((a0, b0), (a1, b1), (a2, b2), (a3, b3))):
        if dist == 0:
            stage(0, mine)
            stage(1, other)
        else:

            @pl.when(chips >= dist)
            def _():
                stage(2 * dist, mine)
                stage(2 * dist + 1, other)

            @pl.when(chips < dist)
            def _():
                near_ref[dist] = jnp.zeros((2, TOK, HD), BF16)
                far_ref[dist] = jnp.zeros((2, TOK, HD), BF16)

    @pl.when(core == 0)
    def _():
        far_ref[0] = jnp.zeros((2, TOK, HD), BF16)

    first = 2 - core
    last = 2 * (chips + 1)

    def fold(x, op):
        parts = x.reshape(TOK // 8, 8, COLS)
        return op(parts, axis=0)

    for c in range(ROWS // COLS):
        at = slice(c * COLS, (c + 1) * COLS)
        s = dot(k_s[0], qt_s[:, at])
        u = lax.broadcasted_iota(jnp.int32, (TOK, COLS), 0)
        t = (lax.broadcasted_iota(jnp.int32, (TOK, COLS), 1) + c * COLS) >> 2
        s = jnp.where(u <= t, s, NEG)
        s_s[0, :, at] = s
        m_s[:, at] = fold(s, jnp.max)

    def scores(b, _):
        for c in range(ROWS // COLS):
            at = slice(c * COLS, (c + 1) * COLS)
            s = dot(k_s[b], qt_s[:, at])
            s_s[b, :, at] = s
            m_s[:, at] = jnp.maximum(m_s[:, at], fold(s, jnp.max))
        return 0

    lax.fori_loop(first, last, scores, 0)
    m_s[...] = jnp.broadcast_to(jnp.max(m_s[...], axis=0, keepdims=True), (8, ROWS))
    l_s[...] = jnp.zeros((8, ROWS), F32)
    ot_s[...] = jnp.zeros((HD, ROWS), F32)

    def forward(b, _):
        for c in range(ROWS // COLS):
            at = slice(c * COLS, (c + 1) * COLS)
            p = jnp.exp2((s_s[b, :, at] - m_s[0:1, at]) * exponent)
            s_s[b, :, at] = p
            l_s[:, at] += fold(p, jnp.sum)
            ot_s[:, at] += dot(vt_s[b], p.astype(BF16))
        return 0

    forward(0, 0)
    lax.fori_loop(first, last, forward, 0)
    inv = 1.0 / jnp.sum(l_s[...], axis=0, keepdims=True)
    out_t = (ot_s[...] * inv).astype(BF16)
    l_s[...] = jnp.broadcast_to(inv, (8, ROWS))
    row_dot = jnp.sum(dt_s[...].astype(F32) * out_t.astype(F32), axis=0, keepdims=True)
    dot_s[...] = jnp.broadcast_to(row_dot, (8, ROWS))
    oq_ref[:, 0:128, :] = out_t.T.reshape(HEADS, 128, HD)
    dqt_s[...] = jnp.zeros((HD, ROWS), F32)

    def backward(b, _):
        dk = jnp.zeros((TOK, HD), F32)
        dv = jnp.zeros((TOK, HD), F32)
        for c in range(ROWS // COLS):
            at = slice(c * COLS, (c + 1) * COLS)
            p = s_s[b, :, at] * l_s[0:1, at]
            dp = dot(v_s[b], dt_s[:, at])
            ds = (p * (dp - dot_s[0:1, at])).astype(BF16)
            dqt_s[:, at] += dot(kt_s[b], ds)
            dk = dk + dot(ds, q_s[at, :])
            dv = dv + dot(p.astype(BF16), d_s[at, :])
        return (dk * scaling).astype(BF16), dv.astype(BF16)

    near_ref[0, 0], near_ref[0, 1] = backward(0, 0)

    @pl.when(core == 1)
    def _():
        far_ref[0, 0], far_ref[0, 1] = backward(1, 0)

    def pair(dist, _):
        near_ref[dist, 0], near_ref[dist, 1] = backward(2 * dist, 0)
        far_ref[dist, 0], far_ref[dist, 1] = backward(2 * dist + 1, 0)
        return 0

    lax.fori_loop(1, chips + 1, pair, 0)
    oq_ref[:, 128:256, :] = (dqt_s[...] * scaling).astype(BF16).T.reshape(HEADS, 128, HD)


def attend(where, qd, mine, other):
    f = pl.pallas_call(
        attend_kernel,
        out_shape=(
            jax.ShapeDtypeStruct((HEADS, 256, HD), BF16),
            jax.ShapeDtypeStruct((4, 2, TOK, HD), BF16),
            jax.ShapeDtypeStruct((4, 2, TOK, HD), BF16),
        ),
        in_specs=[SM] + [VM] * 9,
        out_specs=(VM, VM, VM),
        scratch_shapes=[
            pltpu.VMEM((8, TOK, HD), BF16),
            pltpu.VMEM((8, TOK, HD), BF16),
            pltpu.VMEM((8, HD, TOK), BF16),
            pltpu.VMEM((8, HD, TOK), BF16),
            pltpu.VMEM((ROWS, HD), BF16),
            pltpu.VMEM((ROWS, HD), BF16),
            pltpu.VMEM((HD, ROWS), BF16),
            pltpu.VMEM((HD, ROWS), BF16),
            pltpu.VMEM((8, TOK, ROWS), F32),
            pltpu.VMEM((8, ROWS), F32),
            pltpu.VMEM((8, ROWS), F32),
            pltpu.VMEM((HD, ROWS), F32),
            pltpu.VMEM((HD, ROWS), F32),
            pltpu.VMEM((8, ROWS), F32),
        ],
        compiler_params=params(),
    )
    return f(where, qd, *mine, *other)


def call(kernel, shapes, n_in):
    return pl.pallas_call(
        kernel,
        out_shape=tuple(jax.ShapeDtypeStruct(s, BF16) for s in shapes),
        in_specs=[SM] + [VM] * n_in,
        out_specs=tuple(VM for _ in shapes),
        compiler_params=params(),
    )


def rows_of_groups():
    rows = []
    for start in range(0, 64, 8):
        for core in range(2):
            for place in range(HEADS):
                moved = GROUP // 2 // TOK if place >= HEADS // 2 else 0
                rows.append([(start + moved + 2 * i + core) % 64 * 8 + place for i in range(4)])
    return rows


def local(queries, keys, values, d_attended, shift_amounts):
    seq_pos = lax.axis_index("seq")
    place = lax.axis_index("head")
    in_group = (seq_pos - jnp.where(place >= HEADS // 2, 4, 0)) & 7
    where = jnp.stack((in_group >> 1, in_group & 1)).astype(jnp.int32)
    rows = rows_of_groups()
    swap = [(s * 8 + h, (s ^ 1) * 8 + h) for s in range(64) for h in range(8)]

    (kv,) = call(pack_kv_kernel, [(HEADS, 2 * SUB, HD)], 2)(
        shift_amounts, keys.reshape(TOK, HD), values.reshape(TOK, HD)
    )
    own = lax.all_to_all(kv, "head", 0, 0, tiled=True)
    (qd,) = call(pack_q_kernel, [(HEADS, 256, HD)], 2)(
        shift_amounts, queries.reshape(ROWS, HD), d_attended.reshape(ROWS, HD)
    )
    mine = [own]
    for dist in (1, 2, 3):
        mine.append(lax.ppermute(own, AXES, [(r[i], r[i + dist]) for r in rows for i in range(4 - dist)]))
    qd_here = lax.all_to_all(qd, "head", 0, 0, tiled=True)
    other = [lax.ppermute(x, AXES, swap) for x in mine]
    oq, near, far = attend(where, qd_here, mine, other)
    got = lax.ppermute(far, AXES, swap)
    total = near[0].astype(F32) + got[0].astype(F32)
    for dist in (1, 2, 3):
        part = (near[dist].astype(F32) + got[dist].astype(F32)).astype(BF16)
        back = lax.ppermute(part, AXES, [(r[i + dist], r[i]) for r in rows for i in range(4 - dist)])
        total = total + back.astype(F32)
    oq_back = lax.all_to_all(oq, "head", 0, 0, tiled=True)
    grads = total.astype(BF16).reshape(2, HEADS, SUB, HD).transpose(1, 0, 2, 3).reshape(HEADS, 2 * SUB, HD)
    grads_back = lax.all_to_all(grads, "head", 0, 0, tiled=True)
    attended, d_queries = call(unpack_q_kernel, [(ROWS, HD)] * 2, 1)(shift_amounts, oq_back)
    d_keys, d_values = call(unpack_kv_kernel, [(TOK, HD)] * 2, 1)(shift_amounts, grads_back)
    return (
        attended.reshape(SUB, HEADS, PER, HD),
        d_queries.reshape(SUB, HEADS, PER, HD),
        d_keys.reshape(SUB, HEADS, HD),
        d_values.reshape(SUB, HEADS, HD),
    )


def solution(mesh):
    wide = P(("seq", "head"), None, None, None)
    flat = P(("seq", "head"), None, None)
    return jax.shard_map(
        local,
        mesh=mesh,
        in_specs=(wide, flat, flat, wide, P()),
        out_specs=(wide, wide, flat, flat),
        check_vma=False,
    )
```

```python
import math

import jax
import jax.numpy as jnp
from jax import lax
from jax.experimental import pallas as pl
from jax.experimental.pallas import tpu as pltpu
from jax.sharding import PartitionSpec as P

GROUP = 2048
HEADS = 8
PER = 4
HD = 128
TOK = 256
SUB = 32
ROWS = TOK * PER
COLS = 512
QAT = 64
WIDE = 320
LOG2E = 1.4426950408889634
NEG = -1e30
F32 = jnp.float32
BF16 = jnp.bfloat16
VM = pl.BlockSpec(memory_space=pltpu.VMEM)
SM = pl.BlockSpec(memory_space=pltpu.SMEM)
AXES = ("seq", "head")


LONG = pl.CostEstimate(flops=10_000_000_000, bytes_accessed=1 << 20, transcendentals=0)


def params():
    return pltpu.CompilerParams(vmem_limit_bytes=24 * 1024 * 1024)


def dot(a, b):
    return jnp.dot(a, b, preferred_element_type=F32)


def place_of_head(shift_ref, head):
    place = jnp.zeros(head.shape, jnp.int32)
    plain = jnp.int32(0)
    moved = jnp.int32(HEADS // 2)
    for h in range(HEADS):
        is_moved = (shift_ref[h] > 0).astype(jnp.int32)
        rank = jnp.where(is_moved == 1, moved, plain)
        place = jnp.where(head == h, rank, place)
        moved = moved + is_moved
        plain = plain + 1 - is_moved
    return place


def kv_order(shift_ref, back):
    local = lax.broadcasted_iota(jnp.int32, (TOK, TOK), 0 if back else 1)
    placed = lax.broadcasted_iota(jnp.int32, (TOK, TOK), 1 if back else 0)
    head = lax.broadcasted_iota(jnp.int32, (TOK, 1) if back else (1, TOK), 0 if back else 1) & 7
    place = place_of_head(shift_ref, head)
    hit = ((local >> 3) == (placed & 31)) & (place == (placed >> 5))
    return jnp.where(hit, 1.0, 0.0).astype(BF16)


def q_order(shift_ref, back):
    local = lax.broadcasted_iota(jnp.int32, (TOK, TOK), 0 if back else 1)
    placed = lax.broadcasted_iota(jnp.int32, (TOK, TOK), 1 if back else 0)
    head = lax.broadcasted_iota(jnp.int32, (TOK, 1) if back else (1, TOK), 0 if back else 1)
    place = place_of_head(shift_ref, (head >> 2) & 7)
    same = ((local >> 5) == ((placed & 31) >> 2)) & ((local & 3) == (placed & 3))
    return jnp.where(same & (place == (placed >> 5)), 1.0, 0.0).astype(BF16)


def pack_kernel(shift_hbm, k_hbm, v_hbm, q_hbm, d_hbm, out_ref, shift_ref, k_ref, v_ref, q_ref, d_ref, sems):
    copies = [
        pltpu.make_async_copy(src, dst, sems.at[n])
        for n, (src, dst) in enumerate(
            ((shift_hbm, shift_ref), (k_hbm, k_ref), (v_hbm, v_ref), (q_hbm, q_ref), (d_hbm, d_ref))
        )
    ]
    for copy in copies:
        copy.start()
    copies[0].wait()
    order = kv_order(shift_ref, False)
    wide_order = q_order(shift_ref, False)
    for n, ref in enumerate((k_ref, v_ref)):
        copies[n + 1].wait()
        moved = dot(order, ref[...]).astype(BF16)
        for h in range(HEADS):
            out_ref[h, n * SUB : (n + 1) * SUB, :] = moved[h * SUB : (h + 1) * SUB]
    for n, ref in enumerate((q_ref, d_ref)):
        copies[n + 3].wait()
        for b in range(4):
            moved = dot(wide_order, ref[b * TOK : (b + 1) * TOK, :]).astype(BF16)
            for h in range(HEADS):
                at = QAT + n * 128 + b * 32
                out_ref[h, at : at + 32, :] = moved[h * 32 : (h + 1) * 32]


def unpack_kernel(shift_ref, in_ref, o_ref, q_ref, k_ref, v_ref):
    order = kv_order(shift_ref, True)
    wide_order = q_order(shift_ref, True)
    for n, ref in enumerate((k_ref, v_ref)):
        held = in_ref[:, n * SUB : (n + 1) * SUB, :].reshape(TOK, HD)
        ref[...] = dot(order, held).astype(BF16)
    for n, ref in enumerate((o_ref, q_ref)):
        for b in range(4):
            at = QAT + n * 128 + b * 32
            held = in_ref[:, at : at + 32, :].reshape(TOK, HD)
            ref[b * TOK : (b + 1) * TOK, :] = dot(wide_order, held).astype(BF16)


def attend_kernel(
    where_ref, all_ref, b0, a1, a2, a3, b1, b2, b3,
    near_ref, far_ref, ds_ref, ot_ref,
    k_s, v_s, vt_s, q_s, d_s, qt_s, dt_s, s_s, m_s, l_s, ot_s, dot_s,
):
    chips = where_ref[0]
    core = where_ref[1]
    scaling = 1.0 / math.sqrt(HD)
    exponent = scaling * LOG2E

    def stage(slot, ref):
        k = ref[:, 0:SUB, :].reshape(TOK, HD)
        v = ref[:, SUB : 2 * SUB, :].reshape(TOK, HD)
        k_s[slot] = k
        v_s[slot] = v
        vt_s[slot] = v.T

    q = all_ref[:, QAT : QAT + 128, :].reshape(ROWS, HD)
    d = all_ref[:, QAT + 128 : QAT + 256, :].reshape(ROWS, HD)
    q_s[...] = q
    d_s[...] = d
    qt_s[...] = q.T
    dt_s[...] = d.T
    for dist, (mine, other) in enumerate(((all_ref, b0), (a1, b1), (a2, b2), (a3, b3))):
        if dist == 0:
            stage(0, mine)
            stage(1, other)
        else:

            @pl.when(chips >= dist)
            def _():
                stage(2 * dist, mine)
                stage(2 * dist + 1, other)

            @pl.when(chips < dist)
            def _():
                near_ref[dist] = jnp.zeros((HEADS, 2 * SUB, HD), BF16)
                far_ref[dist] = jnp.zeros((HEADS, 2 * SUB, HD), BF16)

    @pl.when(core == 0)
    def _():
        far_ref[0] = jnp.zeros((HEADS, 2 * SUB, HD), BF16)

    first = 2 - core
    last = 2 * (chips + 1)

    def fold(x, op):
        parts = x.reshape(TOK // 8, 8, COLS)
        return op(parts, axis=0)

    for c in range(ROWS // COLS):
        at = slice(c * COLS, (c + 1) * COLS)
        s = dot(k_s[0], qt_s[:, at])
        u = lax.broadcasted_iota(jnp.int32, (TOK, COLS), 0)
        t = (lax.broadcasted_iota(jnp.int32, (TOK, COLS), 1) + c * COLS) >> 2
        s = jnp.where(u <= t, s, NEG)
        s_s[0, :, at] = s
        m_s[:, at] = fold(s, jnp.max)

    def scores(b, _):
        for c in range(ROWS // COLS):
            at = slice(c * COLS, (c + 1) * COLS)
            s = dot(k_s[b], qt_s[:, at])
            s_s[b, :, at] = s
            m_s[:, at] = jnp.maximum(m_s[:, at], fold(s, jnp.max))
        return 0

    lax.fori_loop(first, last, scores, 0)
    m_s[...] = jnp.broadcast_to(jnp.max(m_s[...], axis=0, keepdims=True), (8, ROWS))
    l_s[...] = jnp.zeros((8, ROWS), F32)
    ot_s[...] = jnp.zeros((HD, ROWS), F32)

    def forward(b, _):
        for c in range(ROWS // COLS):
            at = slice(c * COLS, (c + 1) * COLS)
            p = jnp.exp2((s_s[b, :, at] - m_s[0:1, at]) * exponent)
            s_s[b, :, at] = p
            l_s[:, at] += fold(p, jnp.sum)
            ot_s[:, at] += dot(vt_s[b], p.astype(BF16))
        return 0

    forward(0, 0)
    lax.fori_loop(first, last, forward, 0)
    inv = 1.0 / jnp.sum(l_s[...], axis=0, keepdims=True)
    out_t = (ot_s[...] * inv).astype(BF16)
    l_s[...] = jnp.broadcast_to(inv, (8, ROWS))
    row_dot = jnp.sum(dt_s[...].astype(F32) * out_t.astype(F32), axis=0, keepdims=True)
    dot_s[...] = jnp.broadcast_to(row_dot, (8, ROWS))
    ot_ref[...] = out_t

    def backward(b, out_ref, dist):
        dk = jnp.zeros((TOK, HD), F32)
        dv = jnp.zeros((TOK, HD), F32)
        for c in range(ROWS // COLS):
            at = slice(c * COLS, (c + 1) * COLS)
            p = s_s[b, :, at] * l_s[0:1, at]
            dp = dot(v_s[b], dt_s[:, at])
            ds = (p * (dp - dot_s[0:1, at])).astype(BF16)
            ds_ref[b, :, at] = ds
            dk = dk + dot(ds, q_s[at, :])
            dv = dv + dot(p.astype(BF16), d_s[at, :])
        out_ref[dist, :, 0:SUB, :] = (dk * scaling).astype(BF16).reshape(HEADS, SUB, HD)
        out_ref[dist, :, SUB : 2 * SUB, :] = dv.astype(BF16).reshape(HEADS, SUB, HD)

    backward(0, near_ref, 0)

    @pl.when(core == 1)
    def _():
        backward(1, far_ref, 0)

    def pair(dist, _):
        backward(2 * dist, near_ref, dist)
        backward(2 * dist + 1, far_ref, dist)
        return 0

    lax.fori_loop(1, chips + 1, pair, 0)


def query_kernel(where_ref, ot_ref, ds_ref, all_ref, b0, a1, a2, a3, b1, b2, b3, oq_ref, dqt_s):
    chips = where_ref[0]
    core = where_ref[1]
    oq_ref[:, 0:128, :] = ot_ref[...].T.reshape(HEADS, 128, HD)

    def add(slot, ref, first=False):
        kt = ref[:, 0:SUB, :].reshape(TOK, HD).T
        for c in range(ROWS // COLS):
            at = slice(c * COLS, (c + 1) * COLS)
            part = dot(kt, ds_ref[slot, :, at])
            dqt_s[:, at] = part if first else dqt_s[:, at] + part

    add(0, all_ref, True)

    @pl.when(core == 1)
    def _():
        add(1, b0)

    for dist, mine, other in ((1, a1, b1), (2, a2, b2), (3, a3, b3)):

        @pl.when(chips >= dist)
        def _():
            add(2 * dist, mine)
            add(2 * dist + 1, other)

    grad = (dqt_s[...] * (1.0 / math.sqrt(HD))).astype(BF16)
    oq_ref[:, 128:256, :] = grad.T.reshape(HEADS, 128, HD)


def attend(where, *blocks):
    f = pl.pallas_call(
        attend_kernel,
        out_shape=(
            jax.ShapeDtypeStruct((4, HEADS, 2 * SUB, HD), BF16),
            jax.ShapeDtypeStruct((4, HEADS, 2 * SUB, HD), BF16),
            jax.ShapeDtypeStruct((8, TOK, ROWS), BF16),
            jax.ShapeDtypeStruct((HD, ROWS), BF16),
        ),
        in_specs=[SM] + [VM] * 8,
        out_specs=(VM, VM, VM, VM),
        scratch_shapes=[
            pltpu.VMEM((8, TOK, HD), BF16),
            pltpu.VMEM((8, TOK, HD), BF16),
            pltpu.VMEM((8, HD, TOK), BF16),
            pltpu.VMEM((ROWS, HD), BF16),
            pltpu.VMEM((ROWS, HD), BF16),
            pltpu.VMEM((HD, ROWS), BF16),
            pltpu.VMEM((HD, ROWS), BF16),
            pltpu.VMEM((8, TOK, ROWS), F32),
            pltpu.VMEM((8, ROWS), F32),
            pltpu.VMEM((8, ROWS), F32),
            pltpu.VMEM((HD, ROWS), F32),
            pltpu.VMEM((8, ROWS), F32),
        ],
        compiler_params=params(),
    )
    return f(where, *blocks)


def query_side(where, ot, ds, *blocks):
    f = pl.pallas_call(
        query_kernel,
        out_shape=jax.ShapeDtypeStruct((HEADS, 256, HD), BF16),
        in_specs=[SM] + [VM] * 10,
        out_specs=VM,
        scratch_shapes=[pltpu.VMEM((HD, ROWS), F32)],
        compiler_params=params(),
        cost_estimate=LONG,
    )
    return f(where, ot, ds, *blocks)


def shape(*dims):
    return jax.ShapeDtypeStruct(dims, BF16)


def run(kernel, outs, scratch, *operands, cost=None):
    return pl.pallas_call(
        kernel,
        out_shape=outs,
        in_specs=[SM] + [VM] * (len(operands) - 1),
        out_specs=tuple(VM for _ in outs),
        scratch_shapes=scratch,
        compiler_params=params(),
        cost_estimate=cost,
    )(*operands)


def pack(shift, k, v, q, d):
    return pl.pallas_call(
        pack_kernel,
        out_shape=shape(HEADS, WIDE, HD),
        in_specs=[pl.BlockSpec(memory_space=pl.ANY)] * 5,
        out_specs=VM,
        scratch_shapes=[
            pltpu.SMEM((HEADS,), jnp.int32),
            pltpu.VMEM((TOK, HD), BF16),
            pltpu.VMEM((TOK, HD), BF16),
            pltpu.VMEM((ROWS, HD), BF16),
            pltpu.VMEM((ROWS, HD), BF16),
            pltpu.SemaphoreType.DMA((5,)),
        ],
        compiler_params=pltpu.CompilerParams(vmem_limit_bytes=60 * 1024 * 1024),
    )(shift, k, v, q, d)


def rows_of_groups():
    rows = []
    for start in range(0, 64, 8):
        for core in range(2):
            for place in range(HEADS):
                moved = GROUP // 2 // TOK if place >= HEADS // 2 else 0
                rows.append([(start + moved + 2 * i + core) % 64 * 8 + place for i in range(4)])
    return rows


ALONG = rows_of_groups()
SWAP = [(s * 8 + h, (s ^ 1) * 8 + h) for s in range(64) for h in range(8)]


def ahead(x, dist):
    return lax.ppermute(x, AXES, [(r[i], r[i + dist]) for r in ALONG for i in range(4 - dist)])


def behind(x, dist):
    return lax.ppermute(x, AXES, [(r[i + dist], r[i]) for r in ALONG for i in range(4 - dist)])


def summed(near, far, ot):
    got = lax.ppermute(far, AXES, SWAP)
    parts = [(near[dist].astype(F32) + got[dist].astype(F32)).astype(BF16) for dist in (1, 2, 3)]
    total = near[0].astype(F32) + got[0].astype(F32)
    ot, *parts = lax.optimization_barrier((ot, *parts))
    for dist, part in zip((1, 2, 3), parts):
        total = total + behind(part, dist).astype(F32)
    return total.astype(BF16), ot


def local(queries, keys, values, d_attended, shift_amounts):
    seq_pos = lax.axis_index("seq")
    place = lax.axis_index("head")
    in_group = (seq_pos - jnp.where(place >= HEADS // 2, 4, 0)) & 7
    where = jnp.stack((in_group >> 1, in_group & 1)).astype(jnp.int32)
    packed = pack(
        shift_amounts,
        keys.reshape(TOK, HD),
        values.reshape(TOK, HD),
        queries.reshape(ROWS, HD),
        d_attended.reshape(ROWS, HD),
    )
    everything = lax.all_to_all(packed, "head", 0, 0, tiled=True)
    own = everything[:, 0 : 2 * SUB]
    a = [ahead(own, dist) for dist in (1, 2, 3)]
    blocks = [everything, *a] + [lax.ppermute(x, AXES, SWAP) for x in (own, *a)]
    blocks = [blocks[0], blocks[4], *blocks[1:4], *blocks[5:]]
    near, far, ds, ot = attend(where, *blocks)
    grads, ot = summed(near, far, ot)
    oq = query_side(where, ot, ds, *blocks)
    done = lax.all_to_all(jnp.concatenate((grads, oq), axis=1), "head", 0, 0, tiled=True)
    attended, d_queries, d_keys, d_values = run(
        unpack_kernel,
        (shape(ROWS, HD), shape(ROWS, HD), shape(TOK, HD), shape(TOK, HD)),
        [],
        shift_amounts,
        done,
    )
    return (
        attended.reshape(SUB, HEADS, PER, HD),
        d_queries.reshape(SUB, HEADS, PER, HD),
        d_keys.reshape(SUB, HEADS, HD),
        d_values.reshape(SUB, HEADS, HD),
    )


def solution(mesh):
    wide = P(("seq", "head"), None, None, None)
    flat = P(("seq", "head"), None, None)
    return jax.shard_map(
        local,
        mesh=mesh,
        in_specs=(wide, flat, flat, wide, P()),
        out_specs=(wide, wide, flat, flat),
        check_vma=False,
    )
```

```python
import math

import jax
import jax.numpy as jnp
from jax import lax
from jax.experimental import pallas as pl
from jax.experimental.pallas import tpu as pltpu
from jax.sharding import PartitionSpec as P

GROUP = 2048
HEADS = 8
PER = 4
HD = 128
TOK = 256
SUB = 32
ROWS = TOK * PER
COLS = 256
PAIR = 2 * TOK
STAGE_COST = 10_000_000_000
SUM_COST = 10_000_000_000
LOG2E = 1.4426950408889634
NEG = -1e30
F32 = jnp.float32
BF16 = jnp.bfloat16
VM = pl.BlockSpec(memory_space=pltpu.VMEM)
SM = pl.BlockSpec(memory_space=pltpu.SMEM)
AXES = ("seq", "head")


LONG = pl.CostEstimate(flops=10_000_000_000, bytes_accessed=1 << 20, transcendentals=0)


def params():
    return pltpu.CompilerParams(vmem_limit_bytes=24 * 1024 * 1024)


def dot(a, b):
    return jnp.dot(a, b, preferred_element_type=F32)


def place_of_head(shift_ref, head):
    place = jnp.zeros(head.shape, jnp.int32)
    plain = jnp.int32(0)
    moved = jnp.int32(HEADS // 2)
    for h in range(HEADS):
        is_moved = (shift_ref[h] > 0).astype(jnp.int32)
        rank = jnp.where(is_moved == 1, moved, plain)
        place = jnp.where(head == h, rank, place)
        moved = moved + is_moved
        plain = plain + 1 - is_moved
    return place


def kv_order(shift_ref, back):
    local = lax.broadcasted_iota(jnp.int32, (TOK, TOK), 0 if back else 1)
    placed = lax.broadcasted_iota(jnp.int32, (TOK, TOK), 1 if back else 0)
    head = lax.broadcasted_iota(jnp.int32, (TOK, 1) if back else (1, TOK), 0 if back else 1) & 7
    place = place_of_head(shift_ref, head)
    hit = ((local >> 3) == (placed & 31)) & (place == (placed >> 5))
    return jnp.where(hit, 1.0, 0.0).astype(BF16)


def q_order(shift_ref, back):
    local = lax.broadcasted_iota(jnp.int32, (TOK, TOK), 0 if back else 1)
    placed = lax.broadcasted_iota(jnp.int32, (TOK, TOK), 1 if back else 0)
    head = lax.broadcasted_iota(jnp.int32, (TOK, 1) if back else (1, TOK), 0 if back else 1)
    place = place_of_head(shift_ref, (head >> 2) & 7)
    same = ((local >> 5) == ((placed & 31) >> 2)) & ((local & 3) == (placed & 3))
    return jnp.where(same & (place == (placed >> 5)), 1.0, 0.0).astype(BF16)


def pack_kv_kernel(shift_hbm, k_hbm, v_hbm, out_ref, shift_ref, k_ref, v_ref, sems):
    copies = [
        pltpu.make_async_copy(src, dst, sems.at[n])
        for n, (src, dst) in enumerate(((shift_hbm, shift_ref), (k_hbm, k_ref), (v_hbm, v_ref)))
    ]
    for copy in copies:
        copy.start()
    copies[0].wait()
    order = kv_order(shift_ref, False)
    for n, ref in enumerate((k_ref, v_ref)):
        copies[n + 1].wait()
        moved = dot(order, ref[...]).astype(BF16)
        for h in range(HEADS):
            out_ref[h, n * SUB : (n + 1) * SUB, :] = moved[h * SUB : (h + 1) * SUB]


def pack_q_kernel(shift_ref, q_ref, d_ref, out_ref):
    order = q_order(shift_ref, False)
    for n, ref in enumerate((q_ref, d_ref)):
        for b in range(4):
            moved = dot(order, ref[b * TOK : (b + 1) * TOK, :]).astype(BF16)
            for h in range(HEADS):
                at = n * 128 + b * 32
                out_ref[h, at : at + 32, :] = moved[h * 32 : (h + 1) * 32]


def unpack_kv_kernel(shift_ref, in_ref, k_ref, v_ref):
    order = kv_order(shift_ref, True)
    for n, ref in enumerate((k_ref, v_ref)):
        held = in_ref[:, n * SUB : (n + 1) * SUB, :].reshape(TOK, HD)
        ref[...] = dot(order, held).astype(BF16)


def unpack_q_kernel(shift_ref, in_ref, o_ref, q_ref):
    order = q_order(shift_ref, True)
    for n, ref in enumerate((o_ref, q_ref)):
        for b in range(4):
            at = n * 128 + b * 32
            held = in_ref[:, at : at + 32, :].reshape(TOK, HD)
            ref[b * TOK : (b + 1) * TOK, :] = dot(order, held).astype(BF16)


def attend_kernel(
    where_ref, vt0_ref, qd_ref, a0, b0, a1, a2, a3, b1, b2, b3,
    near_ref, far_ref, ds_ref, ot_ref,
    k_s, v_s, vt_s, q_s, d_s, qt_s, dt_s, s_s, m_s, l_s, ot_s, dot_s,
):
    chips = where_ref[0]
    core = where_ref[1]
    scaling = 1.0 / math.sqrt(HD)
    exponent = scaling * LOG2E
    columns = [slice(c * COLS, (c + 1) * COLS) for c in range(ROWS // COLS)]

    def stage(dist, mine, other):
        for half, ref in enumerate((mine, other)):
            at = slice(half * TOK, (half + 1) * TOK)
            v = ref[:, SUB : 2 * SUB, :].reshape(TOK, HD)
            k_s[dist, at, :] = ref[:, 0:SUB, :].reshape(TOK, HD)
            v_s[dist, at, :] = v
            if dist > 0:
                vt_s[dist, :, at] = v.T

    q = qd_ref[:, 0:128, :].reshape(ROWS, HD)
    d = qd_ref[:, 128:256, :].reshape(ROWS, HD)
    q_s[...] = q
    d_s[...] = d
    qt_s[...] = q.T
    dt_s[...] = d.T
    stage(0, a0, b0)
    vt_s[0] = vt0_ref[...]
    for dist, mine, other in ((1, a1, b1), (2, a2, b2), (3, a3, b3)):

        @pl.when(chips >= dist)
        def _():
            stage(dist, mine, other)

        @pl.when(chips < dist)
        def _():
            near_ref[dist] = jnp.zeros((HEADS, 2 * SUB, HD), BF16)
            far_ref[dist] = jnp.zeros((HEADS, 2 * SUB, HD), BF16)

    def fold(x, op):
        return op(x.reshape(PAIR // 8, 8, COLS), axis=0)

    for c, at in enumerate(columns):
        s = dot(k_s[0], qt_s[:, at])
        u = lax.broadcasted_iota(jnp.int32, (PAIR, COLS), 0)
        t = (lax.broadcasted_iota(jnp.int32, (PAIR, COLS), 1) + c * COLS) >> 2
        limit = jnp.where(u < TOK, t, jnp.where(core == 1, PAIR, 0))
        s = jnp.where(u <= limit, s, NEG)
        s_s[0, :, at] = s
        m_s[:, at] = fold(s, jnp.max)

    def scores(b, _):
        for at in columns:
            s = dot(k_s[b], qt_s[:, at])
            s_s[b, :, at] = s
            m_s[:, at] = jnp.maximum(m_s[:, at], fold(s, jnp.max))
        return 0

    lax.fori_loop(1, chips + 1, scores, 0)
    m_s[...] = jnp.broadcast_to(jnp.max(m_s[...], axis=0, keepdims=True), (8, ROWS))
    l_s[...] = jnp.zeros((8, ROWS), F32)
    ot_s[...] = jnp.zeros((HD, ROWS), F32)

    def forward(b, _):
        for at in columns:
            p = jnp.exp2((s_s[b, :, at] - m_s[0:1, at]) * exponent)
            s_s[b, :, at] = p
            l_s[:, at] += fold(p, jnp.sum)
            ot_s[:, at] += dot(vt_s[b], p.astype(BF16))
        return 0

    lax.fori_loop(0, chips + 1, forward, 0)
    inv = 1.0 / jnp.sum(l_s[...], axis=0, keepdims=True)
    out_t = (ot_s[...] * inv).astype(BF16)
    l_s[...] = jnp.broadcast_to(inv, (8, ROWS))
    row_dot = jnp.sum(dt_s[...].astype(F32) * out_t.astype(F32), axis=0, keepdims=True)
    dot_s[...] = jnp.broadcast_to(row_dot, (8, ROWS))
    ot_ref[...] = out_t

    def backward(b, _):
        dk = jnp.zeros((PAIR, HD), F32)
        dv = jnp.zeros((PAIR, HD), F32)
        for at in columns:
            p = s_s[b, :, at] * l_s[0:1, at]
            dp = dot(v_s[b], dt_s[:, at])
            ds = (p * (dp - dot_s[0:1, at])).astype(BF16)
            ds_ref[b, :, at] = ds
            dk = dk + dot(ds, q_s[at, :])
            dv = dv + dot(p.astype(BF16), d_s[at, :])
        dk = (dk * scaling).astype(BF16)
        dv = dv.astype(BF16)
        for half, ref in enumerate((near_ref, far_ref)):
            at = slice(half * TOK, (half + 1) * TOK)
            ref[b, :, 0:SUB, :] = dk[at].reshape(HEADS, SUB, HD)
            ref[b, :, SUB : 2 * SUB, :] = dv[at].reshape(HEADS, SUB, HD)
        return 0

    lax.fori_loop(0, chips + 1, backward, 0)


def query_kernel(where_ref, ot_ref, ds_ref, a0, b0, a1, a2, a3, b1, b2, b3, oq_ref, dqt_s):
    chips = where_ref[0]
    oq_ref[:, 0:128, :] = ot_ref[...].T.reshape(HEADS, 128, HD)

    def add(dist, mine, other):
        kt = [ref[:, 0:SUB, :].reshape(TOK, HD).T for ref in (mine, other)]
        kt = jnp.concatenate(kt, axis=1)
        for c in range(ROWS // COLS):
            at = slice(c * COLS, (c + 1) * COLS)
            part = dot(kt, ds_ref[dist, :, at])
            dqt_s[:, at] = part if dist == 0 else dqt_s[:, at] + part

    add(0, a0, b0)
    for dist, mine, other in ((1, a1, b1), (2, a2, b2), (3, a3, b3)):

        @pl.when(chips >= dist)
        def _():
            add(dist, mine, other)

    grad = (dqt_s[...] * (1.0 / math.sqrt(HD))).astype(BF16)
    oq_ref[:, 128:256, :] = grad.T.reshape(HEADS, 128, HD)


def stage_kernel(a0, b0, vt_ref):
    for half, ref in enumerate((a0, b0)):
        vt_ref[:, half * TOK : (half + 1) * TOK] = ref[:, SUB : 2 * SUB, :].reshape(TOK, HD).T


def sum_kernel(near_ref, got_ref, c1, c2, c3, out_ref):
    total = near_ref[0].astype(F32) + got_ref[0].astype(F32)
    for ref in (c1, c2, c3):
        total = total + ref[...].astype(F32)
    out_ref[...] = total.astype(BF16)


def attend(where, *blocks):
    f = pl.pallas_call(
        attend_kernel,
        out_shape=(
            jax.ShapeDtypeStruct((4, HEADS, 2 * SUB, HD), BF16),
            jax.ShapeDtypeStruct((4, HEADS, 2 * SUB, HD), BF16),
            jax.ShapeDtypeStruct((4, PAIR, ROWS), BF16),
            jax.ShapeDtypeStruct((HD, ROWS), BF16),
        ),
        in_specs=[SM] + [VM] * 10,
        out_specs=(VM, VM, VM, VM),
        scratch_shapes=[
            pltpu.VMEM((4, PAIR, HD), BF16),
            pltpu.VMEM((4, PAIR, HD), BF16),
            pltpu.VMEM((4, HD, PAIR), BF16),
            pltpu.VMEM((ROWS, HD), BF16),
            pltpu.VMEM((ROWS, HD), BF16),
            pltpu.VMEM((HD, ROWS), BF16),
            pltpu.VMEM((HD, ROWS), BF16),
            pltpu.VMEM((4, PAIR, ROWS), F32),
            pltpu.VMEM((8, ROWS), F32),
            pltpu.VMEM((8, ROWS), F32),
            pltpu.VMEM((HD, ROWS), F32),
            pltpu.VMEM((8, ROWS), F32),
        ],
        compiler_params=params(),
    )
    return f(where, *blocks)


def query_side(where, ot, ds, *blocks):
    f = pl.pallas_call(
        query_kernel,
        out_shape=jax.ShapeDtypeStruct((HEADS, 256, HD), BF16),
        in_specs=[SM] + [VM] * 10,
        out_specs=VM,
        scratch_shapes=[pltpu.VMEM((HD, ROWS), F32)],
        compiler_params=params(),
    )
    return f(where, ot, ds, *blocks)


def shape(*dims):
    return jax.ShapeDtypeStruct(dims, BF16)


def cost_of(flops):
    return pl.CostEstimate(flops=flops, bytes_accessed=1 << 18, transcendentals=0)


def run(kernel, outs, *operands, first=VM, cost=None):
    return pl.pallas_call(
        kernel,
        out_shape=outs,
        in_specs=[first] + [VM] * (len(operands) - 1),
        out_specs=tuple(VM for _ in outs),
        compiler_params=params(),
        cost_estimate=cost,
    )(*operands)


def pack_kv(shift, k, v):
    return pl.pallas_call(
        pack_kv_kernel,
        out_shape=jax.ShapeDtypeStruct((HEADS, 2 * SUB, HD), BF16),
        in_specs=[pl.BlockSpec(memory_space=pl.ANY)] * 3,
        out_specs=VM,
        scratch_shapes=[
            pltpu.SMEM((HEADS,), jnp.int32),
            pltpu.VMEM((TOK, HD), BF16),
            pltpu.VMEM((TOK, HD), BF16),
            pltpu.SemaphoreType.DMA((3,)),
        ],
        compiler_params=pltpu.CompilerParams(vmem_limit_bytes=60 * 1024 * 1024),
    )(shift, k, v)


def rows_of_groups():
    rows = []
    for start in range(0, 64, 8):
        for core in range(2):
            for place in range(HEADS):
                moved = GROUP // 2 // TOK if place >= HEADS // 2 else 0
                rows.append([(start + moved + 2 * i + core) % 64 * 8 + place for i in range(4)])
    return rows


ALONG = rows_of_groups()
SWAP = [(s * 8 + h, (s ^ 1) * 8 + h) for s in range(64) for h in range(8)]


def ahead(x, dist):
    return lax.ppermute(x, AXES, [(r[i], r[i + dist]) for r in ALONG for i in range(4 - dist)])


def behind(x, dist):
    return lax.ppermute(x, AXES, [(r[i + dist], r[i]) for r in ALONG for i in range(4 - dist)])


def local(queries, keys, values, d_attended, shift_amounts):
    seq_pos = lax.axis_index("seq")
    place = lax.axis_index("head")
    in_group = (seq_pos - jnp.where(place >= HEADS // 2, 4, 0)) & 7
    where = jnp.stack((in_group >> 1, in_group & 1)).astype(jnp.int32)
    kv = pack_kv(shift_amounts, keys.reshape(TOK, HD), values.reshape(TOK, HD))
    own = lax.all_to_all(kv, "head", 0, 0, tiled=True)
    (qd,) = run(
        pack_q_kernel,
        (shape(HEADS, 256, HD),),
        shift_amounts, queries.reshape(ROWS, HD), d_attended.reshape(ROWS, HD),
        first=SM,
    )
    a = [ahead(own, dist) for dist in (1, 2, 3)]
    qd_here = lax.all_to_all(qd, "head", 0, 0, tiled=True)
    b = [lax.ppermute(x, AXES, SWAP) for x in (own, *a)]
    (vt0,) = run(stage_kernel, (shape(HD, PAIR),), own, b[0], cost=cost_of(STAGE_COST))
    blocks = [own, b[0], *a, *b[1:]]
    near, far, ds, ot = attend(where, vt0, qd_here, *blocks)

    got = lax.ppermute(far, AXES, SWAP)
    parts = [(near[dist].astype(F32) + got[dist].astype(F32)).astype(BF16) for dist in (1, 2, 3)]
    ot, *parts = lax.optimization_barrier((ot, *parts))
    back = [behind(part, dist) for dist, part in zip((1, 2, 3), parts)]
    oq = query_side(where, ot, ds, *blocks)
    oq_back = lax.all_to_all(oq, "head", 0, 0, tiled=True)
    (grads,) = run(sum_kernel, (shape(HEADS, 2 * SUB, HD),), near, got, *back, cost=cost_of(SUM_COST))
    grads, oq_back = lax.optimization_barrier((grads, oq_back))
    grads_back = lax.all_to_all(grads, "head", 0, 0, tiled=True)
    attended, d_queries = run(
        unpack_q_kernel, (shape(ROWS, HD), shape(ROWS, HD)), shift_amounts, oq_back, first=SM
    )
    d_keys, d_values = run(
        unpack_kv_kernel, (shape(TOK, HD), shape(TOK, HD)), shift_amounts, grads_back, first=SM
    )
    return (
        attended.reshape(SUB, HEADS, PER, HD),
        d_queries.reshape(SUB, HEADS, PER, HD),
        d_keys.reshape(SUB, HEADS, HD),
        d_values.reshape(SUB, HEADS, HD),
    )


def solution(mesh):
    wide = P(("seq", "head"), None, None, None)
    flat = P(("seq", "head"), None, None)
    return jax.shard_map(
        local,
        mesh=mesh,
        in_specs=(wide, flat, flat, wide, P()),
        out_specs=(wide, wide, flat, flat),
        check_vma=False,
    )
```

```python
import math

import jax
import jax.numpy as jnp
from jax import lax
from jax.experimental import pallas as pl
from jax.experimental.pallas import tpu as pltpu
from jax.sharding import PartitionSpec as P

GROUP = 2048
HEADS = 8
PER = 4
HD = 128
TOK = 256
SUB = 32
ROWS = TOK * PER
COLS = 256
PAIR = 2 * TOK
QAT = 64
WIDE = 320
LOG2E = 1.4426950408889634
NEG = -1e30
F32 = jnp.float32
BF16 = jnp.bfloat16
VM = pl.BlockSpec(memory_space=pltpu.VMEM)
SM = pl.BlockSpec(memory_space=pltpu.SMEM)
AXES = ("seq", "head")


LONG = pl.CostEstimate(flops=10_000_000_000, bytes_accessed=1 << 20, transcendentals=0)


def params():
    return pltpu.CompilerParams(vmem_limit_bytes=24 * 1024 * 1024)


def dot(a, b):
    return jnp.dot(a, b, preferred_element_type=F32)


def place_of_head(shift_ref, head):
    place = jnp.zeros(head.shape, jnp.int32)
    plain = jnp.int32(0)
    moved = jnp.int32(HEADS // 2)
    for h in range(HEADS):
        is_moved = (shift_ref[h] > 0).astype(jnp.int32)
        rank = jnp.where(is_moved == 1, moved, plain)
        place = jnp.where(head == h, rank, place)
        moved = moved + is_moved
        plain = plain + 1 - is_moved
    return place


def kv_order(shift_ref, back):
    local = lax.broadcasted_iota(jnp.int32, (TOK, TOK), 0 if back else 1)
    placed = lax.broadcasted_iota(jnp.int32, (TOK, TOK), 1 if back else 0)
    head = lax.broadcasted_iota(jnp.int32, (TOK, 1) if back else (1, TOK), 0 if back else 1) & 7
    place = place_of_head(shift_ref, head)
    hit = ((local >> 3) == (placed & 31)) & (place == (placed >> 5))
    return jnp.where(hit, 1.0, 0.0).astype(BF16)


def q_order(shift_ref, back):
    local = lax.broadcasted_iota(jnp.int32, (TOK, TOK), 0 if back else 1)
    placed = lax.broadcasted_iota(jnp.int32, (TOK, TOK), 1 if back else 0)
    head = lax.broadcasted_iota(jnp.int32, (TOK, 1) if back else (1, TOK), 0 if back else 1)
    place = place_of_head(shift_ref, (head >> 2) & 7)
    same = ((local >> 5) == ((placed & 31) >> 2)) & ((local & 3) == (placed & 3))
    return jnp.where(same & (place == (placed >> 5)), 1.0, 0.0).astype(BF16)


def pack_kernel(shift_hbm, k_hbm, v_hbm, q_hbm, d_hbm, out_ref, shift_ref, k_ref, v_ref, q_ref, d_ref, sems):
    copies = [
        pltpu.make_async_copy(src, dst, sems.at[n])
        for n, (src, dst) in enumerate(
            ((shift_hbm, shift_ref), (k_hbm, k_ref), (v_hbm, v_ref), (q_hbm, q_ref), (d_hbm, d_ref))
        )
    ]
    for copy in copies:
        copy.start()
    copies[0].wait()
    order = kv_order(shift_ref, False)
    wide_order = q_order(shift_ref, False)
    for n, ref in enumerate((k_ref, v_ref)):
        copies[n + 1].wait()
        moved = dot(order, ref[...]).astype(BF16)
        for h in range(HEADS):
            out_ref[h, n * SUB : (n + 1) * SUB, :] = moved[h * SUB : (h + 1) * SUB]
    for n, ref in enumerate((q_ref, d_ref)):
        copies[n + 3].wait()
        for b in range(4):
            moved = dot(wide_order, ref[b * TOK : (b + 1) * TOK, :]).astype(BF16)
            for h in range(HEADS):
                at = QAT + n * 128 + b * 32
                out_ref[h, at : at + 32, :] = moved[h * 32 : (h + 1) * 32]


def unpack_kernel(shift_ref, in_ref, o_ref, q_ref, k_ref, v_ref):
    order = kv_order(shift_ref, True)
    wide_order = q_order(shift_ref, True)
    for n, ref in enumerate((k_ref, v_ref)):
        held = in_ref[:, n * SUB : (n + 1) * SUB, :].reshape(TOK, HD)
        ref[...] = dot(order, held).astype(BF16)
    for n, ref in enumerate((o_ref, q_ref)):
        for b in range(4):
            at = QAT + n * 128 + b * 32
            held = in_ref[:, at : at + 32, :].reshape(TOK, HD)
            ref[b * TOK : (b + 1) * TOK, :] = dot(wide_order, held).astype(BF16)


def attend_kernel(
    where_ref, all_ref, b0, a1, b1, a23, b23,
    near_ref, far_ref, ds_ref, ot_ref,
    k_s, v_s, vt_s, q_s, d_s, qt_s, dt_s, s_s, m_s, l_s, ot_s, dot_s,
):
    chips = where_ref[0]
    core = where_ref[1]
    scaling = 1.0 / math.sqrt(HD)
    exponent = scaling * LOG2E
    columns = [slice(c * COLS, (c + 1) * COLS) for c in range(ROWS // COLS)]

    def stage(dist, mine, other):
        for half, ref in enumerate((mine, other)):
            at = slice(half * TOK, (half + 1) * TOK)
            v = ref[:, SUB : 2 * SUB, :].reshape(TOK, HD)
            k_s[dist, at, :] = ref[:, 0:SUB, :].reshape(TOK, HD)
            v_s[dist, at, :] = v
            vt_s[dist, :, at] = v.T

    q = all_ref[:, QAT : QAT + 128, :].reshape(ROWS, HD)
    d = all_ref[:, QAT + 128 : QAT + 256, :].reshape(ROWS, HD)
    q_s[...] = q
    d_s[...] = d
    qt_s[...] = q.T
    dt_s[...] = d.T
    stage(0, all_ref, b0)
    for dist, mine, other in ((1, a1, b1), (2, a23.at[0], b23.at[0]), (3, a23.at[1], b23.at[1])):

        @pl.when(chips >= dist)
        def _():
            stage(dist, mine, other)

        @pl.when(chips < dist)
        def _():
            near_ref[dist] = jnp.zeros((HEADS, 2 * SUB, HD), BF16)
            far_ref[dist] = jnp.zeros((HEADS, 2 * SUB, HD), BF16)

    def fold(x, op):
        return op(x.reshape(PAIR // 8, 8, COLS), axis=0)

    for c, at in enumerate(columns):
        s = dot(k_s[0], qt_s[:, at])
        u = lax.broadcasted_iota(jnp.int32, (PAIR, COLS), 0)
        t = (lax.broadcasted_iota(jnp.int32, (PAIR, COLS), 1) + c * COLS) >> 2
        limit = jnp.where(u < TOK, t, jnp.where(core == 1, PAIR, 0))
        s = jnp.where(u <= limit, s, NEG)
        s_s[0, :, at] = s
        m_s[:, at] = fold(s, jnp.max)

    def scores(b, _):
        for at in columns:
            s = dot(k_s[b], qt_s[:, at])
            s_s[b, :, at] = s
            m_s[:, at] = jnp.maximum(m_s[:, at], fold(s, jnp.max))
        return 0

    lax.fori_loop(1, chips + 1, scores, 0)
    m_s[...] = jnp.broadcast_to(jnp.max(m_s[...], axis=0, keepdims=True), (8, ROWS))
    l_s[...] = jnp.zeros((8, ROWS), F32)
    ot_s[...] = jnp.zeros((HD, ROWS), F32)

    def forward(b, _):
        for at in columns:
            p = jnp.exp2((s_s[b, :, at] - m_s[0:1, at]) * exponent)
            s_s[b, :, at] = p
            l_s[:, at] += fold(p, jnp.sum)
            ot_s[:, at] += dot(vt_s[b], p.astype(BF16))
        return 0

    lax.fori_loop(0, chips + 1, forward, 0)
    inv = 1.0 / jnp.sum(l_s[...], axis=0, keepdims=True)
    out_t = (ot_s[...] * inv).astype(BF16)
    l_s[...] = jnp.broadcast_to(inv, (8, ROWS))
    row_dot = jnp.sum(dt_s[...].astype(F32) * out_t.astype(F32), axis=0, keepdims=True)
    dot_s[...] = jnp.broadcast_to(row_dot, (8, ROWS))
    ot_ref[...] = out_t

    def backward(b, _):
        dk = jnp.zeros((PAIR, HD), F32)
        dv = jnp.zeros((PAIR, HD), F32)
        for at in columns:
            p = s_s[b, :, at] * l_s[0:1, at]
            dp = dot(v_s[b], dt_s[:, at])
            ds = (p * (dp - dot_s[0:1, at])).astype(BF16)
            ds_ref[b, :, at] = ds
            dk = dk + dot(ds, q_s[at, :])
            dv = dv + dot(p.astype(BF16), d_s[at, :])
        dk = (dk * scaling).astype(BF16)
        dv = dv.astype(BF16)
        for half, ref in enumerate((near_ref, far_ref)):
            at = slice(half * TOK, (half + 1) * TOK)
            ref[b, :, 0:SUB, :] = dk[at].reshape(HEADS, SUB, HD)
            ref[b, :, SUB : 2 * SUB, :] = dv[at].reshape(HEADS, SUB, HD)
        return 0

    lax.fori_loop(0, chips + 1, backward, 0)


def query_kernel(where_ref, ot_ref, ds_ref, all_ref, b0, a1, b1, a23, b23, oq_ref, dqt_s):
    chips = where_ref[0]
    oq_ref[:, 0:128, :] = ot_ref[...].T.reshape(HEADS, 128, HD)

    def add(dist, mine, other):
        kt = [ref[:, 0:SUB, :].reshape(TOK, HD).T for ref in (mine, other)]
        kt = jnp.concatenate(kt, axis=1)
        for c in range(ROWS // COLS):
            at = slice(c * COLS, (c + 1) * COLS)
            part = dot(kt, ds_ref[dist, :, at])
            dqt_s[:, at] = part if dist == 0 else dqt_s[:, at] + part

    add(0, all_ref, b0)
    for dist, mine, other in ((1, a1, b1), (2, a23.at[0], b23.at[0]), (3, a23.at[1], b23.at[1])):

        @pl.when(chips >= dist)
        def _():
            add(dist, mine, other)

    grad = (dqt_s[...] * (1.0 / math.sqrt(HD))).astype(BF16)
    oq_ref[:, 128:256, :] = grad.T.reshape(HEADS, 128, HD)


def attend(where, *blocks):
    f = pl.pallas_call(
        attend_kernel,
        out_shape=(
            jax.ShapeDtypeStruct((4, HEADS, 2 * SUB, HD), BF16),
            jax.ShapeDtypeStruct((4, HEADS, 2 * SUB, HD), BF16),
            jax.ShapeDtypeStruct((4, PAIR, ROWS), BF16),
            jax.ShapeDtypeStruct((HD, ROWS), BF16),
        ),
        in_specs=[SM] + [VM] * 6,
        out_specs=(VM, VM, VM, VM),
        scratch_shapes=[
            pltpu.VMEM((4, PAIR, HD), BF16),
            pltpu.VMEM((4, PAIR, HD), BF16),
            pltpu.VMEM((4, HD, PAIR), BF16),
            pltpu.VMEM((ROWS, HD), BF16),
            pltpu.VMEM((ROWS, HD), BF16),
            pltpu.VMEM((HD, ROWS), BF16),
            pltpu.VMEM((HD, ROWS), BF16),
            pltpu.VMEM((4, PAIR, ROWS), F32),
            pltpu.VMEM((8, ROWS), F32),
            pltpu.VMEM((8, ROWS), F32),
            pltpu.VMEM((HD, ROWS), F32),
            pltpu.VMEM((8, ROWS), F32),
        ],
        compiler_params=params(),
    )
    return f(where, *blocks)


def query_side(where, ot, ds, *blocks):
    f = pl.pallas_call(
        query_kernel,
        out_shape=jax.ShapeDtypeStruct((HEADS, 256, HD), BF16),
        in_specs=[SM] + [VM] * 8,
        out_specs=VM,
        scratch_shapes=[pltpu.VMEM((HD, ROWS), F32)],
        compiler_params=params(),
        cost_estimate=LONG,
    )
    return f(where, ot, ds, *blocks)


def shape(*dims):
    return jax.ShapeDtypeStruct(dims, BF16)


def run(kernel, outs, scratch, *operands, cost=None):
    return pl.pallas_call(
        kernel,
        out_shape=outs,
        in_specs=[SM] + [VM] * (len(operands) - 1),
        out_specs=tuple(VM for _ in outs),
        scratch_shapes=scratch,
        compiler_params=params(),
        cost_estimate=cost,
    )(*operands)


def pack(shift, k, v, q, d):
    return pl.pallas_call(
        pack_kernel,
        out_shape=shape(HEADS, WIDE, HD),
        in_specs=[pl.BlockSpec(memory_space=pl.ANY)] * 5,
        out_specs=VM,
        scratch_shapes=[
            pltpu.SMEM((HEADS,), jnp.int32),
            pltpu.VMEM((TOK, HD), BF16),
            pltpu.VMEM((TOK, HD), BF16),
            pltpu.VMEM((ROWS, HD), BF16),
            pltpu.VMEM((ROWS, HD), BF16),
            pltpu.SemaphoreType.DMA((5,)),
        ],
        compiler_params=pltpu.CompilerParams(vmem_limit_bytes=60 * 1024 * 1024),
    )(shift, k, v, q, d)


def rows_of_groups():
    rows = []
    for start in range(0, 64, 8):
        for core in range(2):
            for place in range(HEADS):
                moved = GROUP // 2 // TOK if place >= HEADS // 2 else 0
                rows.append([(start + moved + 2 * i + core) % 64 * 8 + place for i in range(4)])
    return rows


ALONG = rows_of_groups()
SWAP = [(s * 8 + h, (s ^ 1) * 8 + h) for s in range(64) for h in range(8)]


def ahead(x, dist):
    return lax.ppermute(x, AXES, [(r[i], r[i + dist]) for r in ALONG for i in range(4 - dist)])


def behind(x, dist):
    return lax.ppermute(x, AXES, [(r[i + dist], r[i]) for r in ALONG for i in range(4 - dist)])


def summed(near, far, ot):
    got = lax.ppermute(far, AXES, SWAP)
    parts = [(near[dist].astype(F32) + got[dist].astype(F32)).astype(BF16) for dist in (1, 2, 3)]
    total = near[0].astype(F32) + got[0].astype(F32)
    ot, *parts = lax.optimization_barrier((ot, *parts))
    for dist, part in zip((1, 2, 3), parts):
        total = total + behind(part, dist).astype(F32)
    return total.astype(BF16), ot


def local(queries, keys, values, d_attended, shift_amounts):
    seq_pos = lax.axis_index("seq")
    place = lax.axis_index("head")
    in_group = (seq_pos - jnp.where(place >= HEADS // 2, 4, 0)) & 7
    where = jnp.stack((in_group >> 1, in_group & 1)).astype(jnp.int32)
    packed = pack(
        shift_amounts,
        keys.reshape(TOK, HD),
        values.reshape(TOK, HD),
        queries.reshape(ROWS, HD),
        d_attended.reshape(ROWS, HD),
    )
    everything = lax.all_to_all(packed, "head", 0, 0, tiled=True)
    own = everything[:, 0 : 2 * SUB]
    a1, a2, a3 = (ahead(own, dist) for dist in (1, 2, 3))
    a23 = jnp.stack((a2, a3))
    b0, b1, b23 = (lax.ppermute(x, AXES, SWAP) for x in (own, a1, a23))
    blocks = (everything, b0, a1, b1, a23, b23)
    near, far, ds, ot = attend(where, *blocks)
    grads, ot = summed(near, far, ot)
    oq = query_side(where, ot, ds, *blocks)
    done = lax.all_to_all(jnp.concatenate((grads, oq), axis=1), "head", 0, 0, tiled=True)
    attended, d_queries, d_keys, d_values = run(
        unpack_kernel,
        (shape(ROWS, HD), shape(ROWS, HD), shape(TOK, HD), shape(TOK, HD)),
        [],
        shift_amounts,
        done,
    )
    return (
        attended.reshape(SUB, HEADS, PER, HD),
        d_queries.reshape(SUB, HEADS, PER, HD),
        d_keys.reshape(SUB, HEADS, HD),
        d_values.reshape(SUB, HEADS, HD),
    )


def solution(mesh):
    wide = P(("seq", "head"), None, None, None)
    flat = P(("seq", "head"), None, None)
    return jax.shard_map(
        local,
        mesh=mesh,
        in_specs=(wide, flat, flat, wide, P()),
        out_specs=(wide, wide, flat, flat),
        check_vma=False,
    )
```

```python
import math

import jax
import jax.numpy as jnp
from jax import lax
from jax.experimental import pallas as pl
from jax.experimental.pallas import tpu as pltpu
from jax.sharding import PartitionSpec as P

GROUP = 2048
HEADS = 8
PER = 4
HD = 128
TOK = 256
SUB = 32
ROWS = TOK * PER
COLS = 512
BOTH = 2 * ROWS
QAT = 64
WIDE = 320
LOG2E = 1.4426950408889634
NEG = -1e30
SCALING = 1.0 / math.sqrt(HD)
EXPONENT = SCALING * LOG2E
F32 = jnp.float32
BF16 = jnp.bfloat16
VM = pl.BlockSpec(memory_space=pltpu.VMEM)
SM = pl.BlockSpec(memory_space=pltpu.SMEM)
AXES = ("seq", "head")


LONG = pl.CostEstimate(flops=10_000_000_000, bytes_accessed=1 << 20, transcendentals=0)


def params():
    return pltpu.CompilerParams(vmem_limit_bytes=24 * 1024 * 1024)


def dot(a, b):
    return jnp.dot(a, b, preferred_element_type=F32)


def place_of_head(shift_ref, head):
    place = jnp.zeros(head.shape, jnp.int32)
    plain = jnp.int32(0)
    moved = jnp.int32(HEADS // 2)
    for h in range(HEADS):
        is_moved = (shift_ref[h] > 0).astype(jnp.int32)
        rank = jnp.where(is_moved == 1, moved, plain)
        place = jnp.where(head == h, rank, place)
        moved = moved + is_moved
        plain = plain + 1 - is_moved
    return place


def kv_order(shift_ref, back):
    local = lax.broadcasted_iota(jnp.int32, (TOK, TOK), 0 if back else 1)
    placed = lax.broadcasted_iota(jnp.int32, (TOK, TOK), 1 if back else 0)
    head = lax.broadcasted_iota(jnp.int32, (TOK, 1) if back else (1, TOK), 0 if back else 1) & 7
    place = place_of_head(shift_ref, head)
    hit = ((local >> 3) == (placed & 31)) & (place == (placed >> 5))
    return jnp.where(hit, 1.0, 0.0).astype(BF16)


def q_order(shift_ref, back):
    local = lax.broadcasted_iota(jnp.int32, (TOK, TOK), 0 if back else 1)
    placed = lax.broadcasted_iota(jnp.int32, (TOK, TOK), 1 if back else 0)
    head = lax.broadcasted_iota(jnp.int32, (TOK, 1) if back else (1, TOK), 0 if back else 1)
    place = place_of_head(shift_ref, (head >> 2) & 7)
    same = ((local >> 5) == ((placed & 31) >> 2)) & ((local & 3) == (placed & 3))
    return jnp.where(same & (place == (placed >> 5)), 1.0, 0.0).astype(BF16)


def pack_kernel(shift_hbm, k_hbm, v_hbm, q_hbm, d_hbm, out_ref, shift_ref, k_ref, v_ref, q_ref, d_ref, sems):
    copies = [
        pltpu.make_async_copy(src, dst, sems.at[n])
        for n, (src, dst) in enumerate(
            ((shift_hbm, shift_ref), (k_hbm, k_ref), (v_hbm, v_ref), (q_hbm, q_ref), (d_hbm, d_ref))
        )
    ]
    for copy in copies:
        copy.start()
    copies[0].wait()
    order = kv_order(shift_ref, False)
    wide_order = q_order(shift_ref, False)
    for n, ref in enumerate((k_ref, v_ref)):
        copies[n + 1].wait()
        moved = dot(order, ref[...]).astype(BF16)
        for h in range(HEADS):
            out_ref[h, n * SUB : (n + 1) * SUB, :] = moved[h * SUB : (h + 1) * SUB]
    for n, ref in enumerate((q_ref, d_ref)):
        copies[n + 3].wait()
        for b in range(4):
            moved = dot(wide_order, ref[b * TOK : (b + 1) * TOK, :]).astype(BF16)
            for h in range(HEADS):
                at = QAT + n * 128 + b * 32
                out_ref[h, at : at + 32, :] = moved[h * 32 : (h + 1) * 32]


def unpack_kernel(shift_ref, in_ref, o_ref, q_ref, k_ref, v_ref):
    order = kv_order(shift_ref, True)
    wide_order = q_order(shift_ref, True)
    for n, ref in enumerate((k_ref, v_ref)):
        held = in_ref[:, n * SUB : (n + 1) * SUB, :].reshape(TOK, HD)
        ref[...] = dot(order, held).astype(BF16)
    for n, ref in enumerate((o_ref, q_ref)):
        for b in range(4):
            at = QAT + n * 128 + b * 32
            held = in_ref[:, at : at + 32, :].reshape(TOK, HD)
            ref[b * TOK : (b + 1) * TOK, :] = dot(wide_order, held).astype(BF16)


def columns():
    return [slice(c * COLS, (c + 1) * COLS) for c in range(BOTH // COLS)]


def fold(x, op):
    return op(x.reshape(TOK // 8, 8, COLS), axis=0)


def rows_of(all_ref, swapped_ref, at):
    mine = all_ref[:, QAT + at : QAT + at + 128, :].reshape(ROWS, HD)
    return mine, swapped_ref[:, at : at + 128, :].reshape(ROWS, HD)


def first_kernel(where_ref, all_ref, swapped_ref, qt_ref, dt_ref, s_ref, dp_ref, m_ref):
    core = where_ref[1]
    for ref, at in ((qt_ref, 0), (dt_ref, 128)):
        mine, other = rows_of(all_ref, swapped_ref, at)
        ref[:, 0:ROWS] = mine.T
        ref[:, ROWS:BOTH] = other.T
    keys = all_ref[:, 0:SUB, :].reshape(TOK, HD)
    vals = all_ref[:, SUB : 2 * SUB, :].reshape(TOK, HD)
    for c, at in enumerate(columns()):
        s = dot(keys, qt_ref[:, at])
        u = lax.broadcasted_iota(jnp.int32, (TOK, COLS), 0)
        if c * COLS < ROWS:
            limit = (lax.broadcasted_iota(jnp.int32, (TOK, COLS), 1) + c * COLS) >> 2
        else:
            limit = jnp.where(core == 0, TOK, -1)
        s = jnp.where(u <= limit, s, NEG)
        s_ref[:, at] = s
        m_ref[:, at] = fold(s, jnp.max)
        dp_ref[:, at] = dot(vals, dt_ref[:, at])


def probs_kernel(where_ref, qt_ref, dt_ref, s0_ref, dp0_ref, m0_ref, a1, a2, a3, p_ref, dp_ref, stats_ref, k_s, v_s, m_s, l_s, r_s):
    chips = where_ref[0]
    for n, ref in enumerate((a1, a2, a3)):
        k_s[n] = ref[:, 0:SUB, :].reshape(TOK, HD)
        v_s[n] = ref[:, SUB : 2 * SUB, :].reshape(TOK, HD)
    m_s[...] = m0_ref[...]

    def scores(b, _):
        for at in columns():
            s = dot(k_s[b - 1], qt_ref[:, at])
            p_ref[b, :, at] = s
            m_s[:, at] = jnp.maximum(m_s[:, at], fold(s, jnp.max))
        return 0

    lax.fori_loop(1, chips + 1, scores, 0)
    top = jnp.max(m_s[...], axis=0, keepdims=True)
    m_s[...] = jnp.broadcast_to(top, (8, BOTH))

    for at in columns():
        p = jnp.exp2((s0_ref[:, at] - m_s[0:1, at]) * EXPONENT)
        p_ref[0, :, at] = p
        l_s[:, at] = fold(p, jnp.sum)
        r_s[:, at] = fold(p * dp0_ref[:, at], jnp.sum)

    def forward(b, _):
        for at in columns():
            p = jnp.exp2((p_ref[b, :, at] - m_s[0:1, at]) * EXPONENT)
            dp = dot(v_s[b - 1], dt_ref[:, at])
            p_ref[b, :, at] = p
            dp_ref[b - 1, :, at] = dp
            l_s[:, at] += fold(p, jnp.sum)
            r_s[:, at] += fold(p * dp, jnp.sum)
        return 0

    lax.fori_loop(1, chips + 1, forward, 0)
    stats_ref[0:1, :] = top
    stats_ref[1:2, :] = jnp.sum(l_s[...], axis=0, keepdims=True)
    stats_ref[2:3, :] = jnp.sum(r_s[...], axis=0, keepdims=True)
    stats_ref[3:8, :] = jnp.zeros((5, BOTH), F32)


def attended_kernel(where_ref, all_ref, a1, a2, a3, p_ref, o_ref, vt_s):
    chips = where_ref[0]
    for n, ref in enumerate((all_ref, a1, a2, a3)):
        vt_s[n] = ref[:, SUB : 2 * SUB, :].reshape(TOK, HD).T
    for at in columns():
        o_ref[:, at] = dot(vt_s[0], p_ref[0, :, at].astype(BF16))

    def add(b, _):
        for at in columns():
            o_ref[:, at] += dot(vt_s[b], p_ref[b, :, at].astype(BF16))
        return 0

    lax.fori_loop(1, chips + 1, add, 0)


def grads_kernel(
    where_ref, stats_ref, swapped_stats_ref, all_ref, swapped_ref, p_ref, dp0_ref, dp_ref,
    own_ref, c1, c2, c3, ds_ref, f_ref, q_s, d_s, g_s, r_s,
):
    chips = where_ref[0]
    q_s[0:ROWS, :], q_s[ROWS:BOTH, :] = rows_of(all_ref, swapped_ref, 0)
    d_s[0:ROWS, :], d_s[ROWS:BOTH, :] = rows_of(all_ref, swapped_ref, 128)
    for half in range(2):
        at = slice(half * ROWS, (half + 1) * ROWS)
        there = slice((1 - half) * ROWS, (2 - half) * ROWS)
        top = stats_ref[0:1, at]
        other_top = swapped_stats_ref[0:1, there]
        highest = jnp.maximum(top, other_top)
        f = jnp.exp2((top - highest) * EXPONENT)
        g = jnp.exp2((other_top - highest) * EXPONENT)
        inv = 1.0 / (stats_ref[1:2, at] * f + swapped_stats_ref[1:2, there] * g)
        row_dot = (stats_ref[2:3, at] * f + swapped_stats_ref[2:3, there] * g) * inv
        f_ref[:, at] = jnp.broadcast_to(f * inv, (8, ROWS))
        r_s[:, at] = jnp.broadcast_to(row_dot, (8, ROWS))

    def grads(b, dp):
        dk = jnp.zeros((TOK, HD), F32)
        dv = jnp.zeros((TOK, HD), F32)
        for at in columns():
            p = p_ref[b, :, at] * f_ref[0:1, at]
            ds = (p * (dp[:, at] - r_s[0:1, at])).astype(BF16)
            ds_ref[b, :, at] = ds
            dk = dk + dot(ds, q_s[at, :])
            dv = dv + dot(p.astype(BF16), d_s[at, :])
        return dk * SCALING, dv

    dk, dv = grads(0, dp0_ref)
    own_ref[:, 0:SUB, :] = dk.reshape(HEADS, SUB, HD)
    own_ref[:, SUB : 2 * SUB, :] = dv.reshape(HEADS, SUB, HD)

    def far(b, _):
        dk, dv = grads(b, dp_ref.at[b - 1])
        g_s[b - 1, :, 0:SUB, :] = dk.astype(BF16).reshape(HEADS, SUB, HD)
        g_s[b - 1, :, SUB : 2 * SUB, :] = dv.astype(BF16).reshape(HEADS, SUB, HD)
        return 0

    lax.fori_loop(1, chips + 1, far, 0)
    for dist, ref in ((1, c1), (2, c2), (3, c3)):

        @pl.when(chips >= dist)
        def _():
            ref[...] = g_s[dist - 1]

        @pl.when(chips < dist)
        def _():
            ref[...] = jnp.zeros((HEADS, 2 * SUB, HD), BF16)


def query_kernel(where_ref, all_ref, a1, a2, a3, ds_ref, o_ref, f_ref, mine_ref, other_ref, kt_s, g_s):
    chips = where_ref[0]
    for n, ref in enumerate((all_ref, a1, a2, a3)):
        kt_s[n] = ref[:, 0:SUB, :].reshape(TOK, HD).T
    for at in columns():
        g_s[:, at] = dot(kt_s[0], ds_ref[0, :, at])

    def add(b, _):
        for at in columns():
            g_s[:, at] += dot(kt_s[b], ds_ref[b, :, at])
        return 0

    lax.fori_loop(1, chips + 1, add, 0)
    for n, ref in enumerate((mine_ref, other_ref)):
        at = slice(n * ROWS, (n + 1) * ROWS)
        o = (o_ref[:, at] * f_ref[0:1, at]).T
        g = (g_s[:, at] * SCALING).T
        ref[:, 0:128, :] = o.reshape(HEADS, 128, HD).astype(ref.dtype)
        ref[:, 128:256, :] = g.reshape(HEADS, 128, HD).astype(ref.dtype)


def sum_kernel(own_ref, c1, c2, c3, out_ref):
    total = own_ref[...]
    for ref in (c1, c2, c3):
        total = total + ref[...].astype(F32)
    out_ref[...] = total.astype(BF16)


def shape(*dims, dtype=BF16):
    return jax.ShapeDtypeStruct(dims, dtype)


def run(kernel, outs, scratch, *operands, first=SM, cost=None):
    return pl.pallas_call(
        kernel,
        out_shape=outs,
        in_specs=[first] + [VM] * (len(operands) - 1),
        out_specs=tuple(VM for _ in outs),
        scratch_shapes=scratch,
        compiler_params=params(),
        cost_estimate=cost,
    )(*operands)


def pack(shift, k, v, q, d):
    return pl.pallas_call(
        pack_kernel,
        out_shape=shape(HEADS, WIDE, HD),
        in_specs=[pl.BlockSpec(memory_space=pl.ANY)] * 5,
        out_specs=VM,
        scratch_shapes=[
            pltpu.SMEM((HEADS,), jnp.int32),
            pltpu.VMEM((TOK, HD), BF16),
            pltpu.VMEM((TOK, HD), BF16),
            pltpu.VMEM((ROWS, HD), BF16),
            pltpu.VMEM((ROWS, HD), BF16),
            pltpu.SemaphoreType.DMA((5,)),
        ],
        compiler_params=pltpu.CompilerParams(vmem_limit_bytes=60 * 1024 * 1024),
    )(shift, k, v, q, d)


def rows_of_groups():
    rows = []
    for start in range(0, 64, 8):
        for core in range(2):
            for place in range(HEADS):
                moved = GROUP // 2 // TOK if place >= HEADS // 2 else 0
                rows.append([(start + moved + 2 * i + core) % 64 * 8 + place for i in range(4)])
    return rows


ALONG = rows_of_groups()
SWAP = [(s * 8 + h, (s ^ 1) * 8 + h) for s in range(64) for h in range(8)]


def ahead(x, dist):
    return lax.ppermute(x, AXES, [(r[i], r[i + dist]) for r in ALONG for i in range(4 - dist)])


def behind(x, dist):
    return lax.ppermute(x, AXES, [(r[i + dist], r[i]) for r in ALONG for i in range(4 - dist)])


def local(queries, keys, values, d_attended, shift_amounts):
    seq_pos = lax.axis_index("seq")
    place = lax.axis_index("head")
    in_group = (seq_pos - jnp.where(place >= HEADS // 2, 4, 0)) & 7
    where = jnp.stack((in_group >> 1, in_group & 1)).astype(jnp.int32)
    packed = pack(
        shift_amounts,
        keys.reshape(TOK, HD),
        values.reshape(TOK, HD),
        queries.reshape(ROWS, HD),
        d_attended.reshape(ROWS, HD),
    )
    everything = lax.all_to_all(packed, "head", 0, 0, tiled=True)
    own = everything[:, 0 : 2 * SUB]
    a = [ahead(own, dist) for dist in (1, 2, 3)]
    swapped = lax.ppermute(everything[:, QAT:WIDE], AXES, SWAP)
    rows = pltpu.VMEM((8, BOTH), F32)
    qt, dt, s0, dp0, m0 = run(
        first_kernel,
        (shape(HD, BOTH), shape(HD, BOTH), shape(TOK, BOTH, dtype=F32), shape(TOK, BOTH, dtype=F32), shape(8, BOTH, dtype=F32)),
        [],
        where, everything, swapped,
        cost=LONG,
    )
    probs, dp, stats = run(
        probs_kernel,
        (shape(4, TOK, BOTH, dtype=F32), shape(3, TOK, BOTH, dtype=F32), shape(8, BOTH, dtype=F32)),
        [pltpu.VMEM((3, TOK, HD), BF16), pltpu.VMEM((3, TOK, HD), BF16), rows, rows, rows],
        where, qt, dt, s0, dp0, m0, *a,
    )
    swapped_stats = lax.ppermute(stats, AXES, SWAP)
    (o,) = run(
        attended_kernel,
        (shape(HD, BOTH, dtype=F32),),
        [pltpu.VMEM((4, HD, TOK), BF16)],
        where, everything, *a, probs,
        cost=LONG,
    )
    block = shape(HEADS, 2 * SUB, HD)
    grads, c1, c2, c3, ds, f = run(
        grads_kernel,
        (shape(HEADS, 2 * SUB, HD, dtype=F32), block, block, block, shape(4, TOK, BOTH), shape(8, BOTH, dtype=F32)),
        [pltpu.VMEM((BOTH, HD), BF16), pltpu.VMEM((BOTH, HD), BF16), pltpu.VMEM((3, HEADS, 2 * SUB, HD), BF16), rows],
        where, stats, swapped_stats, everything, swapped, probs, dp0, dp,
    )
    back = [behind(part, dist) for dist, part in zip((1, 2, 3), (c1, c2, c3))]
    mine, other = run(
        query_kernel,
        (shape(HEADS, 256, HD, dtype=F32), shape(HEADS, 256, HD)),
        [pltpu.VMEM((4, HD, TOK), BF16), pltpu.VMEM((HD, BOTH), F32)],
        where, everything, *a, ds, o, f,
        cost=LONG,
    )
    oq = (mine + lax.ppermute(other, AXES, SWAP).astype(F32)).astype(BF16)
    (grads,) = run(sum_kernel, (block,), [], *(grads, *back), first=VM, cost=LONG)
    done = lax.all_to_all(jnp.concatenate((grads, oq), axis=1), "head", 0, 0, tiled=True)
    attended, d_queries, d_keys, d_values = run(
        unpack_kernel,
        (shape(ROWS, HD), shape(ROWS, HD), shape(TOK, HD), shape(TOK, HD)),
        [],
        shift_amounts,
        done,
    )
    return (
        attended.reshape(SUB, HEADS, PER, HD),
        d_queries.reshape(SUB, HEADS, PER, HD),
        d_keys.reshape(SUB, HEADS, HD),
        d_values.reshape(SUB, HEADS, HD),
    )


def solution(mesh):
    wide = P(("seq", "head"), None, None, None)
    flat = P(("seq", "head"), None, None)
    return jax.shard_map(
        local,
        mesh=mesh,
        in_specs=(wide, flat, flat, wide, P()),
        out_specs=(wide, wide, flat, flat),
        check_vma=False,
    )
```

```python
import math

import jax
import jax.numpy as jnp
from jax import lax
from jax.experimental import pallas as pl
from jax.experimental.pallas import tpu as pltpu
from jax.sharding import PartitionSpec as P

GROUP = 2048
HEADS = 8
PER = 4
HD = 128
TOK = 256
SUB = 32
ROWS = TOK * PER
COLS = 512
BOTH = 2 * ROWS
QAT = 64
WIDE = 320
LOG2E = 1.4426950408889634
NEG = -1e30
SCALING = 1.0 / math.sqrt(HD)
EXPONENT = SCALING * LOG2E
F32 = jnp.float32
BF16 = jnp.bfloat16
VM = pl.BlockSpec(memory_space=pltpu.VMEM)
SM = pl.BlockSpec(memory_space=pltpu.SMEM)
AXES = ("seq", "head")


LONG = pl.CostEstimate(flops=10_000_000_000, bytes_accessed=1 << 20, transcendentals=0)


def params():
    return pltpu.CompilerParams(vmem_limit_bytes=24 * 1024 * 1024)


def dot(a, b):
    return jnp.dot(a, b, preferred_element_type=F32)


def place_of_head(shift_ref, head):
    place = jnp.zeros(head.shape, jnp.int32)
    plain = jnp.int32(0)
    moved = jnp.int32(HEADS // 2)
    for h in range(HEADS):
        is_moved = (shift_ref[h] > 0).astype(jnp.int32)
        rank = jnp.where(is_moved == 1, moved, plain)
        place = jnp.where(head == h, rank, place)
        moved = moved + is_moved
        plain = plain + 1 - is_moved
    return place


def kv_order(shift_ref, back):
    local = lax.broadcasted_iota(jnp.int32, (TOK, TOK), 0 if back else 1)
    placed = lax.broadcasted_iota(jnp.int32, (TOK, TOK), 1 if back else 0)
    head = lax.broadcasted_iota(jnp.int32, (TOK, 1) if back else (1, TOK), 0 if back else 1) & 7
    place = place_of_head(shift_ref, head)
    hit = ((local >> 3) == (placed & 31)) & (place == (placed >> 5))
    return jnp.where(hit, 1.0, 0.0).astype(BF16)


def q_order(shift_ref, back):
    local = lax.broadcasted_iota(jnp.int32, (TOK, TOK), 0 if back else 1)
    placed = lax.broadcasted_iota(jnp.int32, (TOK, TOK), 1 if back else 0)
    head = lax.broadcasted_iota(jnp.int32, (TOK, 1) if back else (1, TOK), 0 if back else 1)
    place = place_of_head(shift_ref, (head >> 2) & 7)
    same = ((local >> 5) == ((placed & 31) >> 2)) & ((local & 3) == (placed & 3))
    return jnp.where(same & (place == (placed >> 5)), 1.0, 0.0).astype(BF16)


def pack_kernel(shift_hbm, k_hbm, v_hbm, q_hbm, d_hbm, out_ref, shift_ref, k_ref, v_ref, q_ref, d_ref, sems):
    copies = [
        pltpu.make_async_copy(src, dst, sems.at[n])
        for n, (src, dst) in enumerate(
            ((shift_hbm, shift_ref), (k_hbm, k_ref), (v_hbm, v_ref), (q_hbm, q_ref), (d_hbm, d_ref))
        )
    ]
    for copy in copies:
        copy.start()
    copies[0].wait()
    order = kv_order(shift_ref, False)
    wide_order = q_order(shift_ref, False)
    for n, ref in enumerate((k_ref, v_ref)):
        copies[n + 1].wait()
        moved = dot(order, ref[...]).astype(BF16)
        for h in range(HEADS):
            out_ref[h, n * SUB : (n + 1) * SUB, :] = moved[h * SUB : (h + 1) * SUB]
    for n, ref in enumerate((q_ref, d_ref)):
        copies[n + 3].wait()
        for b in range(4):
            moved = dot(wide_order, ref[b * TOK : (b + 1) * TOK, :]).astype(BF16)
            for h in range(HEADS):
                at = QAT + n * 128 + b * 32
                out_ref[h, at : at + 32, :] = moved[h * 32 : (h + 1) * 32]


def unpack_kernel(shift_ref, in_ref, o_ref, q_ref, k_ref, v_ref):
    order = kv_order(shift_ref, True)
    wide_order = q_order(shift_ref, True)
    for n, ref in enumerate((k_ref, v_ref)):
        held = in_ref[:, n * SUB : (n + 1) * SUB, :].reshape(TOK, HD)
        ref[...] = dot(order, held).astype(BF16)
    for n, ref in enumerate((o_ref, q_ref)):
        for b in range(4):
            at = QAT + n * 128 + b * 32
            held = in_ref[:, at : at + 32, :].reshape(TOK, HD)
            ref[b * TOK : (b + 1) * TOK, :] = dot(wide_order, held).astype(BF16)


def columns():
    return [slice(c * COLS, (c + 1) * COLS) for c in range(BOTH // COLS)]


def fold(x, op):
    return op(x.reshape(TOK // 8, 8, COLS), axis=0)


def rows_of(all_ref, swapped_ref, at):
    mine = all_ref[:, QAT + at : QAT + at + 128, :].reshape(ROWS, HD)
    return mine, swapped_ref[:, at : at + 128, :].reshape(ROWS, HD)


def first_kernel(where_ref, all_ref, swapped_ref, qt_ref, dt_ref, s_ref, dp_ref, m_ref, q_ref, d_ref):
    core = where_ref[1]
    for ref, rows_ref, at in ((qt_ref, q_ref, 0), (dt_ref, d_ref, 128)):
        mine, other = rows_of(all_ref, swapped_ref, at)
        rows_ref[0:ROWS, :] = mine
        rows_ref[ROWS:BOTH, :] = other
        ref[:, 0:ROWS] = mine.T
        ref[:, ROWS:BOTH] = other.T
    keys = all_ref[:, 0:SUB, :].reshape(TOK, HD)
    vals = all_ref[:, SUB : 2 * SUB, :].reshape(TOK, HD)
    for c, at in enumerate(columns()):
        s = dot(keys, qt_ref[:, at])
        u = lax.broadcasted_iota(jnp.int32, (TOK, COLS), 0)
        if c * COLS < ROWS:
            limit = (lax.broadcasted_iota(jnp.int32, (TOK, COLS), 1) + c * COLS) >> 2
        else:
            limit = jnp.where(core == 0, TOK, -1)
        s = jnp.where(u <= limit, s, NEG)
        s_ref[:, at] = s
        m_ref[:, at] = fold(s, jnp.max)
        dp_ref[:, at] = dot(vals, dt_ref[:, at])


def early_kernel(where_ref, qt_ref, dt_ref, a3, s_ref, dp_ref, m_ref):
    chips = where_ref[0]

    @pl.when(chips == 3)
    def _():
        keys = a3[:, 0:SUB, :].reshape(TOK, HD)
        vals = a3[:, SUB : 2 * SUB, :].reshape(TOK, HD)
        for at in columns():
            s = dot(keys, qt_ref[:, at])
            s_ref[:, at] = s
            m_ref[:, at] = fold(s, jnp.max)
            dp_ref[:, at] = dot(vals, dt_ref[:, at])

    @pl.when(chips < 3)
    def _():
        m_ref[...] = jnp.full((8, BOTH), NEG, F32)


def probs_kernel(
    where_ref, qt_ref, dt_ref, s0_ref, dp0_ref, m0_ref, s3_ref, dp3_ref, m3_ref, a1, a2,
    p_ref, dp_ref, stats_ref, k_s, v_s, m_s, l_s, r_s,
):
    chips = where_ref[0]
    last = jnp.minimum(chips, 2) + 1
    for n, ref in enumerate((a1, a2)):
        k_s[n] = ref[:, 0:SUB, :].reshape(TOK, HD)
        v_s[n] = ref[:, SUB : 2 * SUB, :].reshape(TOK, HD)
    m_s[...] = jnp.maximum(m0_ref[...], m3_ref[...])

    def scores(b, _):
        for at in columns():
            s = dot(k_s[b - 1], qt_ref[:, at])
            p_ref[b, :, at] = s
            m_s[:, at] = jnp.maximum(m_s[:, at], fold(s, jnp.max))
        return 0

    lax.fori_loop(1, last, scores, 0)
    top = jnp.max(m_s[...], axis=0, keepdims=True)
    m_s[...] = jnp.broadcast_to(top, (8, BOTH))

    for at in columns():
        p = jnp.exp2((s0_ref[:, at] - m_s[0:1, at]) * EXPONENT)
        p_ref[0, :, at] = p
        l_s[:, at] = fold(p, jnp.sum)
        r_s[:, at] = fold(p * dp0_ref[:, at], jnp.sum)

    def forward(b, _):
        for at in columns():
            p = jnp.exp2((p_ref[b, :, at] - m_s[0:1, at]) * EXPONENT)
            dp = dot(v_s[b - 1], dt_ref[:, at])
            p_ref[b, :, at] = p
            dp_ref[b - 1, :, at] = dp
            l_s[:, at] += fold(p, jnp.sum)
            r_s[:, at] += fold(p * dp, jnp.sum)
        return 0

    lax.fori_loop(1, last, forward, 0)

    @pl.when(chips == 3)
    def _():
        for at in columns():
            p = jnp.exp2((s3_ref[:, at] - m_s[0:1, at]) * EXPONENT)
            p_ref[3, :, at] = p
            l_s[:, at] += fold(p, jnp.sum)
            r_s[:, at] += fold(p * dp3_ref[:, at], jnp.sum)

    stats_ref[0:1, :] = top
    stats_ref[1:2, :] = jnp.sum(l_s[...], axis=0, keepdims=True)
    stats_ref[2:3, :] = jnp.sum(r_s[...], axis=0, keepdims=True)
    stats_ref[3:8, :] = jnp.zeros((5, BOTH), F32)


def attended_kernel(where_ref, all_ref, a1, a2, a3, p_ref, o_ref, vt_s):
    chips = where_ref[0]
    for n, ref in enumerate((all_ref, a1, a2, a3)):
        vt_s[n] = ref[:, SUB : 2 * SUB, :].reshape(TOK, HD).T
    for at in columns():
        o_ref[:, at] = dot(vt_s[0], p_ref[0, :, at].astype(BF16))

    def add(b, _):
        for at in columns():
            o_ref[:, at] += dot(vt_s[b], p_ref[b, :, at].astype(BF16))
        return 0

    lax.fori_loop(1, chips + 1, add, 0)


def key_grads(p_ref, dp_ref, ds_ref, f_ref, r_ref, q_ref, d_ref):
    dk = jnp.zeros((TOK, HD), F32)
    dv = jnp.zeros((TOK, HD), F32)
    for at in columns():
        p = p_ref[:, at] * f_ref[0:1, at]
        ds = (p * (dp_ref[:, at] - r_ref[0:1, at])).astype(BF16)
        ds_ref[:, at] = ds
        dk = dk + dot(ds, q_ref[at, :])
        dv = dv + dot(p.astype(BF16), d_ref[at, :])
    return dk * SCALING, dv


def grads_kernel(
    where_ref, stats_ref, swapped_stats_ref, q_s, d_s, p_ref, dp_ref, dp3_ref,
    c1, c2, c3, ds_ref, f_ref, r_s, g_s,
):
    chips = where_ref[0]
    for half in range(2):
        at = slice(half * ROWS, (half + 1) * ROWS)
        there = slice((1 - half) * ROWS, (2 - half) * ROWS)
        top = stats_ref[0:1, at]
        other_top = swapped_stats_ref[0:1, there]
        highest = jnp.maximum(top, other_top)
        f = jnp.exp2((top - highest) * EXPONENT)
        g = jnp.exp2((other_top - highest) * EXPONENT)
        inv = 1.0 / (stats_ref[1:2, at] * f + swapped_stats_ref[1:2, there] * g)
        row_dot = (stats_ref[2:3, at] * f + swapped_stats_ref[2:3, there] * g) * inv
        f_ref[:, at] = jnp.broadcast_to(f * inv, (8, ROWS))
        r_s[:, at] = jnp.broadcast_to(row_dot, (8, ROWS))

    def far(b, dp):
        dk, dv = key_grads(p_ref.at[b], dp, ds_ref.at[b - 1], f_ref, r_s, q_s, d_s)
        g_s[b - 1, :, 0:SUB, :] = dk.astype(BF16).reshape(HEADS, SUB, HD)
        g_s[b - 1, :, SUB : 2 * SUB, :] = dv.astype(BF16).reshape(HEADS, SUB, HD)
        return 0

    lax.fori_loop(1, jnp.minimum(chips, 2) + 1, lambda b, _: far(b, dp_ref.at[b - 1]), 0)

    @pl.when(chips == 3)
    def _():
        far(3, dp3_ref)

    for dist, ref in ((1, c1), (2, c2), (3, c3)):

        @pl.when(chips >= dist)
        def _():
            ref[...] = g_s[dist - 1]

        @pl.when(chips < dist)
        def _():
            ref[...] = jnp.zeros((HEADS, 2 * SUB, HD), BF16)


def query_kernel(
    where_ref, all_ref, a1, a2, a3, ds_ref, o_ref, f_ref, r_ref, q_ref, d_ref, p_ref, dp0_ref,
    mine_ref, other_ref, own_ref, kt_s, g_s, ds0_s,
):
    chips = where_ref[0]
    dk, dv = key_grads(p_ref.at[0], dp0_ref, ds0_s, f_ref, r_ref, q_ref, d_ref)
    own_ref[:, 0:SUB, :] = dk.reshape(HEADS, SUB, HD)
    own_ref[:, SUB : 2 * SUB, :] = dv.reshape(HEADS, SUB, HD)
    for n, ref in enumerate((all_ref, a1, a2, a3)):
        kt_s[n] = ref[:, 0:SUB, :].reshape(TOK, HD).T
    for at in columns():
        g_s[:, at] = dot(kt_s[0], ds0_s[:, at])

    def add(b, _):
        for at in columns():
            g_s[:, at] += dot(kt_s[b], ds_ref[b - 1, :, at])
        return 0

    lax.fori_loop(1, chips + 1, add, 0)
    for n, ref in enumerate((mine_ref, other_ref)):
        at = slice(n * ROWS, (n + 1) * ROWS)
        o = (o_ref[:, at] * f_ref[0:1, at]).T
        g = (g_s[:, at] * SCALING).T
        ref[:, 0:128, :] = o.reshape(HEADS, 128, HD).astype(ref.dtype)
        ref[:, 128:256, :] = g.reshape(HEADS, 128, HD).astype(ref.dtype)


def sum_kernel(own_ref, c1, c2, c3, out_ref):
    total = own_ref[...]
    for ref in (c1, c2, c3):
        total = total + ref[...].astype(F32)
    out_ref[...] = total.astype(BF16)


def shape(*dims, dtype=BF16):
    return jax.ShapeDtypeStruct(dims, dtype)


def run(kernel, outs, scratch, *operands, first=SM, cost=None):
    return pl.pallas_call(
        kernel,
        out_shape=outs,
        in_specs=[first] + [VM] * (len(operands) - 1),
        out_specs=tuple(VM for _ in outs),
        scratch_shapes=scratch,
        compiler_params=params(),
        cost_estimate=cost,
    )(*operands)


def pack(shift, k, v, q, d):
    return pl.pallas_call(
        pack_kernel,
        out_shape=shape(HEADS, WIDE, HD),
        in_specs=[pl.BlockSpec(memory_space=pl.ANY)] * 5,
        out_specs=VM,
        scratch_shapes=[
            pltpu.SMEM((HEADS,), jnp.int32),
            pltpu.VMEM((TOK, HD), BF16),
            pltpu.VMEM((TOK, HD), BF16),
            pltpu.VMEM((ROWS, HD), BF16),
            pltpu.VMEM((ROWS, HD), BF16),
            pltpu.SemaphoreType.DMA((5,)),
        ],
        compiler_params=pltpu.CompilerParams(vmem_limit_bytes=60 * 1024 * 1024),
    )(shift, k, v, q, d)


def rows_of_groups():
    rows = []
    for start in range(0, 64, 8):
        for core in range(2):
            for place in range(HEADS):
                moved = GROUP // 2 // TOK if place >= HEADS // 2 else 0
                rows.append([(start + moved + 2 * i + core) % 64 * 8 + place for i in range(4)])
    return rows


ALONG = rows_of_groups()
SWAP = [(s * 8 + h, (s ^ 1) * 8 + h) for s in range(64) for h in range(8)]


def ahead(x, dist):
    return lax.ppermute(x, AXES, [(r[i], r[i + dist]) for r in ALONG for i in range(4 - dist)])


def behind(x, dist):
    return lax.ppermute(x, AXES, [(r[i + dist], r[i]) for r in ALONG for i in range(4 - dist)])


def local(queries, keys, values, d_attended, shift_amounts):
    seq_pos = lax.axis_index("seq")
    place = lax.axis_index("head")
    in_group = (seq_pos - jnp.where(place >= HEADS // 2, 4, 0)) & 7
    where = jnp.stack((in_group >> 1, in_group & 1)).astype(jnp.int32)
    packed = pack(
        shift_amounts,
        keys.reshape(TOK, HD),
        values.reshape(TOK, HD),
        queries.reshape(ROWS, HD),
        d_attended.reshape(ROWS, HD),
    )
    everything = lax.all_to_all(packed, "head", 0, 0, tiled=True)
    own = everything[:, 0 : 2 * SUB]
    a = [ahead(own, dist) for dist in (1, 2, 3)]
    swapped = lax.ppermute(everything[:, QAT:WIDE], AXES, SWAP)
    rows = pltpu.VMEM((8, BOTH), F32)
    wide, tall, flat = shape(TOK, BOTH, dtype=F32), shape(BOTH, HD), shape(8, BOTH, dtype=F32)
    qt, dt, s0, dp0, m0, q_rows, d_rows = run(
        first_kernel,
        (shape(HD, BOTH), shape(HD, BOTH), wide, wide, flat, tall, tall),
        [],
        where, everything, swapped,
        cost=LONG,
    )
    s3, dp3, m3 = run(early_kernel, (wide, wide, flat), [], where, qt, dt, a[2], cost=LONG)
    held = pltpu.VMEM((2, TOK, HD), BF16)
    probs, dp, stats = run(
        probs_kernel,
        (shape(4, TOK, BOTH, dtype=F32), shape(2, TOK, BOTH, dtype=F32), flat),
        [held, held, rows, rows, rows],
        where, qt, dt, s0, dp0, m0, s3, dp3, m3, a[0], a[1],
    )
    swapped_stats = lax.ppermute(stats, AXES, SWAP)
    (o,) = run(
        attended_kernel,
        (shape(HD, BOTH, dtype=F32),),
        [pltpu.VMEM((4, HD, TOK), BF16)],
        where, everything, *a, probs,
        cost=LONG,
    )
    block = shape(HEADS, 2 * SUB, HD)
    c1, c2, c3, ds, f, row_dot = run(
        grads_kernel,
        (block, block, block, shape(3, TOK, BOTH), flat, flat),
        [pltpu.VMEM((3, HEADS, 2 * SUB, HD), BF16)],
        where, stats, swapped_stats, q_rows, d_rows, probs, dp, dp3,
    )
    back = [behind(part, dist) for dist, part in zip((1, 2, 3), (c1, c2, c3))]
    mine, other, grads = run(
        query_kernel,
        (shape(HEADS, 256, HD, dtype=F32), shape(HEADS, 256, HD), shape(HEADS, 2 * SUB, HD, dtype=F32)),
        [pltpu.VMEM((4, HD, TOK), BF16), pltpu.VMEM((HD, BOTH), F32), pltpu.VMEM((TOK, BOTH), BF16)],
        where, everything, *a, ds, o, f, row_dot, q_rows, d_rows, probs, dp0,
        cost=LONG,
    )
    oq = (mine + lax.ppermute(other, AXES, SWAP).astype(F32)).astype(BF16)
    (grads,) = run(sum_kernel, (block,), [], *(grads, *back), first=VM, cost=LONG)
    done = lax.all_to_all(jnp.concatenate((grads, oq), axis=1), "head", 0, 0, tiled=True)
    attended, d_queries, d_keys, d_values = run(
        unpack_kernel,
        (shape(ROWS, HD), shape(ROWS, HD), shape(TOK, HD), shape(TOK, HD)),
        [],
        shift_amounts,
        done,
    )
    return (
        attended.reshape(SUB, HEADS, PER, HD),
        d_queries.reshape(SUB, HEADS, PER, HD),
        d_keys.reshape(SUB, HEADS, HD),
        d_values.reshape(SUB, HEADS, HD),
    )


def solution(mesh):
    wide = P(("seq", "head"), None, None, None)
    flat = P(("seq", "head"), None, None)
    return jax.shard_map(
        local,
        mesh=mesh,
        in_specs=(wide, flat, flat, wide, P()),
        out_specs=(wide, wide, flat, flat),
        check_vma=False,
    )
```

```python
import math

import jax
import jax.numpy as jnp
from jax import lax
from jax.experimental import pallas as pl
from jax.experimental.pallas import tpu as pltpu
from jax.sharding import PartitionSpec as P

GROUP = 2048
HEADS = 8
PER = 4
HD = 128
TOK = 256
SUB = 32
ROWS = TOK * PER
COLS = 512
BOTH = 2 * ROWS
QAT = 64
WIDE = 320
LOG2E = 1.4426950408889634
NEG = -1e30
SCALING = 1.0 / math.sqrt(HD)
EXPONENT = SCALING * LOG2E
F32 = jnp.float32
BF16 = jnp.bfloat16
VM = pl.BlockSpec(memory_space=pltpu.VMEM)
SM = pl.BlockSpec(memory_space=pltpu.SMEM)
AXES = ("seq", "head")


LONG = pl.CostEstimate(flops=10_000_000_000, bytes_accessed=1 << 20, transcendentals=0)


def params():
    return pltpu.CompilerParams(vmem_limit_bytes=24 * 1024 * 1024)


def dot(a, b):
    return jnp.dot(a, b, preferred_element_type=F32)


def place_of_head(shift_ref, head):
    place = jnp.zeros(head.shape, jnp.int32)
    plain = jnp.int32(0)
    moved = jnp.int32(HEADS // 2)
    for h in range(HEADS):
        is_moved = (shift_ref[h] > 0).astype(jnp.int32)
        rank = jnp.where(is_moved == 1, moved, plain)
        place = jnp.where(head == h, rank, place)
        moved = moved + is_moved
        plain = plain + 1 - is_moved
    return place


def kv_order(shift_ref, back):
    local = lax.broadcasted_iota(jnp.int32, (TOK, TOK), 0 if back else 1)
    placed = lax.broadcasted_iota(jnp.int32, (TOK, TOK), 1 if back else 0)
    head = lax.broadcasted_iota(jnp.int32, (TOK, 1) if back else (1, TOK), 0 if back else 1) & 7
    place = place_of_head(shift_ref, head)
    hit = ((local >> 3) == (placed & 31)) & (place == (placed >> 5))
    return jnp.where(hit, 1.0, 0.0).astype(BF16)


def q_order(shift_ref, back):
    local = lax.broadcasted_iota(jnp.int32, (TOK, TOK), 0 if back else 1)
    placed = lax.broadcasted_iota(jnp.int32, (TOK, TOK), 1 if back else 0)
    head = lax.broadcasted_iota(jnp.int32, (TOK, 1) if back else (1, TOK), 0 if back else 1)
    place = place_of_head(shift_ref, (head >> 2) & 7)
    same = ((local >> 5) == ((placed & 31) >> 2)) & ((local & 3) == (placed & 3))
    return jnp.where(same & (place == (placed >> 5)), 1.0, 0.0).astype(BF16)


def pack_kernel(
    shift_hbm, k_hbm, v_hbm, q_hbm, d_hbm, out_hbm, shift_ref, k_ref, v_ref, q_ref, d_ref, kv_s, wide_s, sems
):
    copies = [
        pltpu.make_async_copy(src, dst, sems.at[n])
        for n, (src, dst) in enumerate(
            ((shift_hbm, shift_ref), (k_hbm, k_ref), (v_hbm, v_ref), (q_hbm, q_ref), (d_hbm, d_ref))
        )
    ]
    out = [pltpu.make_async_copy(kv_s, out_hbm.at[:, 0:QAT, :], sems.at[5])]
    for n in range(2):
        out.append(
            pltpu.make_async_copy(
                wide_s.at[n], out_hbm.at[:, QAT + n * 128 : QAT + n * 128 + 128, :], sems.at[6 + n]
            )
        )
    for copy in copies:
        copy.start()
    copies[0].wait()
    order = kv_order(shift_ref, False)
    wide_order = q_order(shift_ref, False)
    for n, ref in enumerate((k_ref, v_ref)):
        copies[n + 1].wait()
        moved = dot(order, ref[...]).astype(BF16)
        for h in range(HEADS):
            kv_s[h, n * SUB : (n + 1) * SUB, :] = moved[h * SUB : (h + 1) * SUB]
    out[0].start()
    for n, ref in enumerate((q_ref, d_ref)):
        copies[n + 3].wait()
        for b in range(4):
            moved = dot(wide_order, ref[b * TOK : (b + 1) * TOK, :]).astype(BF16)
            for h in range(HEADS):
                wide_s[n, h, b * 32 : b * 32 + 32, :] = moved[h * 32 : (h + 1) * 32]
        out[n + 1].start()
    for copy in out:
        copy.wait()


def unpack_kernel(shift_ref, in_ref, o_hbm, q_hbm, k_hbm, v_hbm, o_s, q_s, k_s, v_s, sems):
    order = kv_order(shift_ref, True)
    wide_order = q_order(shift_ref, True)
    copies = [
        pltpu.make_async_copy(src, dst, sems.at[n])
        for n, (src, dst) in enumerate(((o_s, o_hbm), (q_s, q_hbm), (k_s, k_hbm), (v_s, v_hbm)))
    ]
    for n, ref in enumerate((o_s, q_s)):
        for b in range(4):
            at = QAT + n * 128 + b * 32
            held = in_ref[:, at : at + 32, :].reshape(TOK, HD)
            ref[b * TOK : (b + 1) * TOK, :] = dot(wide_order, held).astype(BF16)
        copies[n].start()
    for n, ref in enumerate((k_s, v_s)):
        held = in_ref[:, n * SUB : (n + 1) * SUB, :].reshape(TOK, HD)
        ref[...] = dot(order, held).astype(BF16)
        copies[n + 2].start()
    for copy in copies:
        copy.wait()


def columns():
    return [slice(c * COLS, (c + 1) * COLS) for c in range(BOTH // COLS)]


def fold(x, op):
    return op(x.reshape(TOK // 8, 8, COLS), axis=0)


def rows_of(all_ref, swapped_ref, at):
    mine = all_ref[:, QAT + at : QAT + at + 128, :].reshape(ROWS, HD)
    return mine, swapped_ref[:, at : at + 128, :].reshape(ROWS, HD)


def first_kernel(where_ref, all_ref, swapped_ref, qt_ref, dt_ref, s_ref, dp_ref, m_ref, q_ref, d_ref):
    core = where_ref[1]
    for ref, rows_ref, at in ((qt_ref, q_ref, 0), (dt_ref, d_ref, 128)):
        mine, other = rows_of(all_ref, swapped_ref, at)
        rows_ref[0:ROWS, :] = mine
        rows_ref[ROWS:BOTH, :] = other
        ref[:, 0:ROWS] = mine.T
        ref[:, ROWS:BOTH] = other.T
    keys = all_ref[:, 0:SUB, :].reshape(TOK, HD)
    vals = all_ref[:, SUB : 2 * SUB, :].reshape(TOK, HD)
    for c, at in enumerate(columns()):
        s = dot(keys, qt_ref[:, at])
        u = lax.broadcasted_iota(jnp.int32, (TOK, COLS), 0)
        if c * COLS < ROWS:
            limit = (lax.broadcasted_iota(jnp.int32, (TOK, COLS), 1) + c * COLS) >> 2
        else:
            limit = jnp.where(core == 0, TOK, -1)
        s = jnp.where(u <= limit, s, NEG)
        s_ref[:, at] = s
        m_ref[:, at] = fold(s, jnp.max)
        dp_ref[:, at] = dot(vals, dt_ref[:, at])


def early_kernel(where_ref, qt_ref, dt_ref, a3, s_ref, dp_ref, m_ref):
    chips = where_ref[0]

    @pl.when(chips == 3)
    def _():
        keys = a3[:, 0:SUB, :].reshape(TOK, HD)
        vals = a3[:, SUB : 2 * SUB, :].reshape(TOK, HD)
        for at in columns():
            s = dot(keys, qt_ref[:, at])
            s_ref[:, at] = s
            m_ref[:, at] = fold(s, jnp.max)
            dp_ref[:, at] = dot(vals, dt_ref[:, at])

    @pl.when(chips < 3)
    def _():
        m_ref[...] = jnp.full((8, BOTH), NEG, F32)


def probs_kernel(
    where_ref, qt_ref, dt_ref, s0_ref, dp0_ref, m0_ref, s3_ref, dp3_ref, m3_ref, a1, a2,
    p_ref, dp_ref, stats_ref, k_s, v_s, m_s, l_s, r_s,
):
    chips = where_ref[0]
    last = jnp.minimum(chips, 2) + 1
    for n, ref in enumerate((a1, a2)):
        k_s[n] = ref[:, 0:SUB, :].reshape(TOK, HD)
        v_s[n] = ref[:, SUB : 2 * SUB, :].reshape(TOK, HD)
    m_s[...] = jnp.maximum(m0_ref[...], m3_ref[...])

    def scores(b, _):
        for at in columns():
            s = dot(k_s[b - 1], qt_ref[:, at])
            p_ref[b, :, at] = s
            m_s[:, at] = jnp.maximum(m_s[:, at], fold(s, jnp.max))
        return 0

    lax.fori_loop(1, last, scores, 0)
    top = jnp.max(m_s[...], axis=0, keepdims=True)
    m_s[...] = jnp.broadcast_to(top, (8, BOTH))

    for at in columns():
        p = jnp.exp2((s0_ref[:, at] - m_s[0:1, at]) * EXPONENT)
        p_ref[0, :, at] = p
        l_s[:, at] = fold(p, jnp.sum)
        r_s[:, at] = fold(p * dp0_ref[:, at], jnp.sum)

    def forward(b, _):
        for at in columns():
            p = jnp.exp2((p_ref[b, :, at] - m_s[0:1, at]) * EXPONENT)
            dp = dot(v_s[b - 1], dt_ref[:, at])
            p_ref[b, :, at] = p
            dp_ref[b - 1, :, at] = dp
            l_s[:, at] += fold(p, jnp.sum)
            r_s[:, at] += fold(p * dp, jnp.sum)
        return 0

    lax.fori_loop(1, last, forward, 0)

    @pl.when(chips == 3)
    def _():
        for at in columns():
            p = jnp.exp2((s3_ref[:, at] - m_s[0:1, at]) * EXPONENT)
            p_ref[3, :, at] = p
            l_s[:, at] += fold(p, jnp.sum)
            r_s[:, at] += fold(p * dp3_ref[:, at], jnp.sum)

    stats_ref[0:1, :] = top
    stats_ref[1:2, :] = jnp.sum(l_s[...], axis=0, keepdims=True)
    stats_ref[2:3, :] = jnp.sum(r_s[...], axis=0, keepdims=True)
    stats_ref[3:8, :] = jnp.zeros((5, BOTH), F32)


def attended_kernel(where_ref, all_ref, a1, a2, a3, p_ref, o_ref, vt_s):
    chips = where_ref[0]
    for n, ref in enumerate((all_ref, a1, a2, a3)):
        vt_s[n] = ref[:, SUB : 2 * SUB, :].reshape(TOK, HD).T
    for at in columns():
        o_ref[:, at] = dot(vt_s[0], p_ref[0, :, at].astype(BF16))

    def add(b, _):
        for at in columns():
            o_ref[:, at] += dot(vt_s[b], p_ref[b, :, at].astype(BF16))
        return 0

    lax.fori_loop(1, chips + 1, add, 0)


def key_grads(p_ref, dp_ref, ds_ref, f_ref, r_ref, q_ref, d_ref):
    dk = jnp.zeros((TOK, HD), F32)
    dv = jnp.zeros((TOK, HD), F32)
    for at in columns():
        p = p_ref[:, at] * f_ref[0:1, at]
        ds = (p * (dp_ref[:, at] - r_ref[0:1, at])).astype(BF16)
        ds_ref[:, at] = ds
        dk = dk + dot(ds, q_ref[at, :])
        dv = dv + dot(p.astype(BF16), d_ref[at, :])
    return dk * SCALING, dv


def grads_kernel(
    where_ref, stats_ref, swapped_stats_ref, q_s, d_s, p_ref, dp_ref, dp3_ref,
    c1, c2, c3, ds_ref, f_ref, r_s, g_s,
):
    chips = where_ref[0]
    for half in range(2):
        at = slice(half * ROWS, (half + 1) * ROWS)
        there = slice((1 - half) * ROWS, (2 - half) * ROWS)
        top = stats_ref[0:1, at]
        other_top = swapped_stats_ref[0:1, there]
        highest = jnp.maximum(top, other_top)
        f = jnp.exp2((top - highest) * EXPONENT)
        g = jnp.exp2((other_top - highest) * EXPONENT)
        inv = 1.0 / (stats_ref[1:2, at] * f + swapped_stats_ref[1:2, there] * g)
        row_dot = (stats_ref[2:3, at] * f + swapped_stats_ref[2:3, there] * g) * inv
        f_ref[:, at] = jnp.broadcast_to(f * inv, (8, ROWS))
        r_s[:, at] = jnp.broadcast_to(row_dot, (8, ROWS))

    def far(b, dp):
        dk, dv = key_grads(p_ref.at[b], dp, ds_ref.at[b - 1], f_ref, r_s, q_s, d_s)
        g_s[b - 1, :, 0:SUB, :] = dk.astype(BF16).reshape(HEADS, SUB, HD)
        g_s[b - 1, :, SUB : 2 * SUB, :] = dv.astype(BF16).reshape(HEADS, SUB, HD)
        return 0

    lax.fori_loop(1, jnp.minimum(chips, 2) + 1, lambda b, _: far(b, dp_ref.at[b - 1]), 0)

    @pl.when(chips == 3)
    def _():
        far(3, dp3_ref)

    for dist, ref in ((1, c1), (2, c2), (3, c3)):

        @pl.when(chips >= dist)
        def _():
            ref[...] = g_s[dist - 1]

        @pl.when(chips < dist)
        def _():
            ref[...] = jnp.zeros((HEADS, 2 * SUB, HD), BF16)


def query_kernel(
    where_ref, all_ref, a1, a2, a3, ds_ref, o_ref, f_ref, r_ref, q_ref, d_ref, p_ref, dp0_ref,
    mine_ref, other_ref, own_ref, kt_s, g_s, ds0_s,
):
    chips = where_ref[0]
    dk, dv = key_grads(p_ref.at[0], dp0_ref, ds0_s, f_ref, r_ref, q_ref, d_ref)
    own_ref[:, 0:SUB, :] = dk.reshape(HEADS, SUB, HD)
    own_ref[:, SUB : 2 * SUB, :] = dv.reshape(HEADS, SUB, HD)
    for n, ref in enumerate((all_ref, a1, a2, a3)):
        kt_s[n] = ref[:, 0:SUB, :].reshape(TOK, HD).T
    for at in columns():
        g_s[:, at] = dot(kt_s[0], ds0_s[:, at])

    def add(b, _):
        for at in columns():
            g_s[:, at] += dot(kt_s[b], ds_ref[b - 1, :, at])
        return 0

    lax.fori_loop(1, chips + 1, add, 0)
    for n, ref in enumerate((mine_ref, other_ref)):
        at = slice(n * ROWS, (n + 1) * ROWS)
        o = (o_ref[:, at] * f_ref[0:1, at]).T
        g = (g_s[:, at] * SCALING).T
        ref[:, 0:128, :] = o.reshape(HEADS, 128, HD).astype(ref.dtype)
        ref[:, 128:256, :] = g.reshape(HEADS, 128, HD).astype(ref.dtype)


def sum_kernel(own_ref, c1, c2, c3, out_ref):
    total = own_ref[...]
    for ref in (c1, c2, c3):
        total = total + ref[...].astype(F32)
    out_ref[...] = total.astype(BF16)


def shape(*dims, dtype=BF16):
    return jax.ShapeDtypeStruct(dims, dtype)


def run(kernel, outs, scratch, *operands, first=SM, out=VM, cost=None):
    return pl.pallas_call(
        kernel,
        out_shape=outs,
        in_specs=[first] + [VM] * (len(operands) - 1),
        out_specs=tuple(out for _ in outs),
        scratch_shapes=scratch,
        compiler_params=params(),
        cost_estimate=cost,
    )(*operands)


def pack(shift, k, v, q, d):
    return pl.pallas_call(
        pack_kernel,
        out_shape=shape(HEADS, WIDE, HD),
        in_specs=[pl.BlockSpec(memory_space=pl.ANY)] * 5,
        out_specs=pl.BlockSpec(memory_space=pl.ANY),
        scratch_shapes=[
            pltpu.SMEM((HEADS,), jnp.int32),
            pltpu.VMEM((TOK, HD), BF16),
            pltpu.VMEM((TOK, HD), BF16),
            pltpu.VMEM((ROWS, HD), BF16),
            pltpu.VMEM((ROWS, HD), BF16),
            pltpu.VMEM((HEADS, QAT, HD), BF16),
            pltpu.VMEM((2, HEADS, 128, HD), BF16),
            pltpu.SemaphoreType.DMA((8,)),
        ],
        compiler_params=pltpu.CompilerParams(vmem_limit_bytes=60 * 1024 * 1024),
    )(shift, k, v, q, d)


def rows_of_groups():
    rows = []
    for start in range(0, 64, 8):
        for core in range(2):
            for place in range(HEADS):
                moved = GROUP // 2 // TOK if place >= HEADS // 2 else 0
                rows.append([(start + moved + 2 * i + core) % 64 * 8 + place for i in range(4)])
    return rows


ALONG = rows_of_groups()
SWAP = [(s * 8 + h, (s ^ 1) * 8 + h) for s in range(64) for h in range(8)]


def ahead(x, dist):
    return lax.ppermute(x, AXES, [(r[i], r[i + dist]) for r in ALONG for i in range(4 - dist)])


def behind(x, dist):
    return lax.ppermute(x, AXES, [(r[i + dist], r[i]) for r in ALONG for i in range(4 - dist)])


def local(queries, keys, values, d_attended, shift_amounts):
    seq_pos = lax.axis_index("seq")
    place = lax.axis_index("head")
    in_group = (seq_pos - jnp.where(place >= HEADS // 2, 4, 0)) & 7
    where = jnp.stack((in_group >> 1, in_group & 1)).astype(jnp.int32)
    packed = pack(
        shift_amounts,
        keys.reshape(TOK, HD),
        values.reshape(TOK, HD),
        queries.reshape(ROWS, HD),
        d_attended.reshape(ROWS, HD),
    )
    everything = lax.all_to_all(packed, "head", 0, 0, tiled=True)
    own = everything[:, 0 : 2 * SUB]
    a = [ahead(own, dist) for dist in (1, 2, 3)]
    swapped = lax.ppermute(everything[:, QAT:WIDE], AXES, SWAP)
    rows = pltpu.VMEM((8, BOTH), F32)
    wide, tall, flat = shape(TOK, BOTH, dtype=F32), shape(BOTH, HD), shape(8, BOTH, dtype=F32)
    qt, dt, s0, dp0, m0, q_rows, d_rows = run(
        first_kernel,
        (shape(HD, BOTH), shape(HD, BOTH), wide, wide, flat, tall, tall),
        [],
        where, everything, swapped,
        cost=LONG,
    )
    s3, dp3, m3 = run(early_kernel, (wide, wide, flat), [], where, qt, dt, a[2], cost=LONG)
    held = pltpu.VMEM((2, TOK, HD), BF16)
    probs, dp, stats = run(
        probs_kernel,
        (shape(4, TOK, BOTH, dtype=F32), shape(2, TOK, BOTH, dtype=F32), flat),
        [held, held, rows, rows, rows],
        where, qt, dt, s0, dp0, m0, s3, dp3, m3, a[0], a[1],
    )
    swapped_stats = lax.ppermute(stats, AXES, SWAP)
    (o,) = run(
        attended_kernel,
        (shape(HD, BOTH, dtype=F32),),
        [pltpu.VMEM((4, HD, TOK), BF16)],
        where, everything, *a, probs,
        cost=LONG,
    )
    block = shape(HEADS, 2 * SUB, HD)
    c1, c2, c3, ds, f, row_dot = run(
        grads_kernel,
        (block, block, block, shape(3, TOK, BOTH), flat, flat),
        [pltpu.VMEM((3, HEADS, 2 * SUB, HD), BF16)],
        where, stats, swapped_stats, q_rows, d_rows, probs, dp, dp3,
    )
    back = [behind(part, dist) for dist, part in zip((1, 2, 3), (c1, c2, c3))]
    mine, other, grads = run(
        query_kernel,
        (shape(HEADS, 256, HD, dtype=F32), shape(HEADS, 256, HD), shape(HEADS, 2 * SUB, HD, dtype=F32)),
        [pltpu.VMEM((4, HD, TOK), BF16), pltpu.VMEM((HD, BOTH), F32), pltpu.VMEM((TOK, BOTH), BF16)],
        where, everything, *a, ds, o, f, row_dot, q_rows, d_rows, probs, dp0,
        cost=LONG,
    )
    oq = (mine + lax.ppermute(other, AXES, SWAP).astype(F32)).astype(BF16)
    (grads,) = run(sum_kernel, (block,), [], *(grads, *back), first=VM, cost=LONG)
    done = lax.all_to_all(jnp.concatenate((grads, oq), axis=1), "head", 0, 0, tiled=True)
    attended, d_queries, d_keys, d_values = run(
        unpack_kernel,
        (shape(ROWS, HD), shape(ROWS, HD), shape(TOK, HD), shape(TOK, HD)),
        [
            pltpu.VMEM((ROWS, HD), BF16),
            pltpu.VMEM((ROWS, HD), BF16),
            pltpu.VMEM((TOK, HD), BF16),
            pltpu.VMEM((TOK, HD), BF16),
            pltpu.SemaphoreType.DMA((4,)),
        ],
        shift_amounts,
        done,
        out=pl.BlockSpec(memory_space=pl.ANY),
    )
    return (
        attended.reshape(SUB, HEADS, PER, HD),
        d_queries.reshape(SUB, HEADS, PER, HD),
        d_keys.reshape(SUB, HEADS, HD),
        d_values.reshape(SUB, HEADS, HD),
    )


def solution(mesh):
    wide = P(("seq", "head"), None, None, None)
    flat = P(("seq", "head"), None, None)
    return jax.shard_map(
        local,
        mesh=mesh,
        in_specs=(wide, flat, flat, wide, P()),
        out_specs=(wide, wide, flat, flat),
        check_vma=False,
    )
```

```python
import math

import jax
import jax.numpy as jnp
from jax import lax
from jax.experimental import pallas as pl
from jax.experimental.pallas import tpu as pltpu
from jax.sharding import PartitionSpec as P

GROUP = 2048
HEADS = 8
PER = 4
HD = 128
TOK = 256
SUB = 32
ROWS = TOK * PER
COLS = 512
BOTH = 2 * ROWS
QAT = 64
WIDE = 320
LOG2E = 1.4426950408889634
NEG = -1e30
SCALING = 1.0 / math.sqrt(HD)
EXPONENT = SCALING * LOG2E
F32 = jnp.float32
BF16 = jnp.bfloat16
VM = pl.BlockSpec(memory_space=pltpu.VMEM)
SM = pl.BlockSpec(memory_space=pltpu.SMEM)
AXES = ("seq", "head")


LONG = pl.CostEstimate(flops=10_000_000_000, bytes_accessed=1 << 20, transcendentals=0)


def params():
    return pltpu.CompilerParams(vmem_limit_bytes=24 * 1024 * 1024)


def dot(a, b):
    return jnp.dot(a, b, preferred_element_type=F32)


def place_of_head(shift_ref, head):
    place = jnp.zeros(head.shape, jnp.int32)
    plain = jnp.int32(0)
    moved = jnp.int32(HEADS // 2)
    for h in range(HEADS):
        is_moved = (shift_ref[h] > 0).astype(jnp.int32)
        rank = jnp.where(is_moved == 1, moved, plain)
        place = jnp.where(head == h, rank, place)
        moved = moved + is_moved
        plain = plain + 1 - is_moved
    return place


def kv_order(shift_ref, back):
    local = lax.broadcasted_iota(jnp.int32, (TOK, TOK), 0 if back else 1)
    placed = lax.broadcasted_iota(jnp.int32, (TOK, TOK), 1 if back else 0)
    head = lax.broadcasted_iota(jnp.int32, (TOK, 1) if back else (1, TOK), 0 if back else 1) & 7
    place = place_of_head(shift_ref, head)
    hit = ((local >> 3) == (placed & 31)) & (place == (placed >> 5))
    return jnp.where(hit, 1.0, 0.0).astype(BF16)


def q_order(shift_ref, back):
    local = lax.broadcasted_iota(jnp.int32, (TOK, TOK), 0 if back else 1)
    placed = lax.broadcasted_iota(jnp.int32, (TOK, TOK), 1 if back else 0)
    head = lax.broadcasted_iota(jnp.int32, (TOK, 1) if back else (1, TOK), 0 if back else 1)
    place = place_of_head(shift_ref, (head >> 2) & 7)
    same = ((local >> 5) == ((placed & 31) >> 2)) & ((local & 3) == (placed & 3))
    return jnp.where(same & (place == (placed >> 5)), 1.0, 0.0).astype(BF16)


def pack_kernel(
    shift_hbm, k_hbm, v_hbm, q_hbm, d_hbm, out_hbm, shift_ref, k_ref, v_ref, q_ref, d_ref, kv_s, wide_s, sems
):
    copies = [
        pltpu.make_async_copy(src, dst, sems.at[n])
        for n, (src, dst) in enumerate(
            ((shift_hbm, shift_ref), (k_hbm, k_ref), (v_hbm, v_ref), (q_hbm, q_ref), (d_hbm, d_ref))
        )
    ]
    out = [pltpu.make_async_copy(kv_s, out_hbm.at[:, 0:QAT, :], sems.at[5])]
    for n in range(2):
        out.append(
            pltpu.make_async_copy(
                wide_s.at[n], out_hbm.at[:, QAT + n * 128 : QAT + n * 128 + 128, :], sems.at[6 + n]
            )
        )
    for copy in copies:
        copy.start()
    copies[0].wait()
    order = kv_order(shift_ref, False)
    wide_order = q_order(shift_ref, False)
    for n, ref in enumerate((k_ref, v_ref)):
        copies[n + 1].wait()
        moved = dot(order, ref[...]).astype(BF16)
        for h in range(HEADS):
            kv_s[h, n * SUB : (n + 1) * SUB, :] = moved[h * SUB : (h + 1) * SUB]
    out[0].start()
    for n, ref in enumerate((q_ref, d_ref)):
        copies[n + 3].wait()
        for b in range(4):
            moved = dot(wide_order, ref[b * TOK : (b + 1) * TOK, :]).astype(BF16)
            for h in range(HEADS):
                wide_s[n, h, b * 32 : b * 32 + 32, :] = moved[h * 32 : (h + 1) * 32]
        out[n + 1].start()
    for copy in out:
        copy.wait()


def unpack_kernel(shift_ref, in_ref, o_hbm, q_hbm, k_hbm, v_hbm, o_s, q_s, k_s, v_s, sems):
    order = kv_order(shift_ref, True)
    wide_order = q_order(shift_ref, True)
    copies = [
        pltpu.make_async_copy(src, dst, sems.at[n])
        for n, (src, dst) in enumerate(((o_s, o_hbm), (q_s, q_hbm), (k_s, k_hbm), (v_s, v_hbm)))
    ]
    for n, ref in enumerate((o_s, q_s)):
        for b in range(4):
            at = QAT + n * 128 + b * 32
            held = in_ref[:, at : at + 32, :].reshape(TOK, HD)
            ref[b * TOK : (b + 1) * TOK, :] = dot(wide_order, held).astype(BF16)
        copies[n].start()
    for n, ref in enumerate((k_s, v_s)):
        held = in_ref[:, n * SUB : (n + 1) * SUB, :].reshape(TOK, HD)
        ref[...] = dot(order, held).astype(BF16)
        copies[n + 2].start()
    for copy in copies:
        copy.wait()


def columns():
    return [slice(c * COLS, (c + 1) * COLS) for c in range(BOTH // COLS)]


def fold(x, op):
    return op(x.reshape(TOK // 8, 8, COLS), axis=0)


def halves():
    return [slice(c * COLS, (c + 1) * COLS) for c in range(ROWS // COLS)]


def past(at):
    return slice(ROWS + at.start, ROWS + at.stop)


def rows_at(all_ref, swapped_ref, at, which):
    start = at.start % ROWS // 128
    held = slice(start, start + COLS // 128)
    if at.start < ROWS:
        return all_ref[held, QAT + which : QAT + which + 128, :].reshape(COLS, HD)
    return swapped_ref[held, which : which + 128, :].reshape(COLS, HD)


def first_kernel(all_ref, qt_ref, dt_ref, s_ref, dp_ref, m_ref):
    for ref, at in ((qt_ref, QAT), (dt_ref, QAT + 128)):
        ref[...] = all_ref[:, at : at + 128, :].reshape(ROWS, HD).T
    keys = all_ref[:, 0:SUB, :].reshape(TOK, HD)
    vals = all_ref[:, SUB : 2 * SUB, :].reshape(TOK, HD)
    for at in halves():
        s = dot(keys, qt_ref[:, at])
        u = lax.broadcasted_iota(jnp.int32, (TOK, COLS), 0)
        t = (lax.broadcasted_iota(jnp.int32, (TOK, COLS), 1) + at.start) >> 2
        s = jnp.where(u <= t, s, NEG)
        s_ref[:, at] = s
        m_ref[:, at] = fold(s, jnp.max)
        dp_ref[:, at] = dot(vals, dt_ref[:, at])


def early_kernel(where_ref, qt_ref, dt_ref, a3, s_ref, dp_ref, m_ref):
    chips = where_ref[0]

    @pl.when(chips == 3)
    def _():
        keys = a3[:, 0:SUB, :].reshape(TOK, HD)
        vals = a3[:, SUB : 2 * SUB, :].reshape(TOK, HD)
        for at in halves():
            s = dot(keys, qt_ref[:, at])
            s_ref[:, at] = s
            m_ref[:, at] = fold(s, jnp.max)
            dp_ref[:, at] = dot(vals, dt_ref[:, at])

    @pl.when(chips < 3)
    def _():
        m_ref[...] = jnp.full((8, ROWS), NEG, F32)


def probs_kernel(
    where_ref, all_ref, sw_ref, qt_ref, dt_ref, s0_ref, dp0_ref, m0_ref, s3_ref, dp3_ref, m3_ref, a1, a2, a3,
    p_ref, dpm_ref, dpo_ref, stats_ref, k_s, v_s, qo_s, do_s, m_s, l_s, r_s,
):
    chips = where_ref[0]
    core = where_ref[1]
    last = jnp.minimum(chips, 2) + 1
    for n, ref in enumerate((all_ref, a1, a2, a3)):
        k_s[n] = ref[:, 0:SUB, :].reshape(TOK, HD)
        v_s[n] = ref[:, SUB : 2 * SUB, :].reshape(TOK, HD)
    qo_s[...] = sw_ref[:, 0:128, :].reshape(ROWS, HD).T
    do_s[...] = sw_ref[:, 128:256, :].reshape(ROWS, HD).T
    m_s[:, 0:ROWS] = jnp.maximum(m0_ref[...], m3_ref[...])
    for at in halves():
        s = jnp.where(core == 0, dot(k_s[0], qo_s[:, at]), NEG)
        p_ref[0, :, past(at)] = s
        m_s[:, past(at)] = fold(s, jnp.max)

    def scores(b, mine):
        for at in halves():
            if mine:
                s = dot(k_s[b], qt_ref[:, at])
                p_ref[b, :, at] = s
                m_s[:, at] = jnp.maximum(m_s[:, at], fold(s, jnp.max))
            s = dot(k_s[b], qo_s[:, at])
            p_ref[b, :, past(at)] = s
            m_s[:, past(at)] = jnp.maximum(m_s[:, past(at)], fold(s, jnp.max))
        return 0

    lax.fori_loop(1, last, lambda b, _: scores(b, True), 0)

    @pl.when(chips == 3)
    def _():
        scores(3, False)

    top = jnp.max(m_s[...], axis=0, keepdims=True)
    m_s[...] = jnp.broadcast_to(top, (8, BOTH))

    def probs(b, at, s, dp, begin=False):
        p = jnp.exp2((s - m_s[0:1, at]) * EXPONENT)
        p_ref[b, :, at] = p
        total = fold(p, jnp.sum)
        row = fold(p * dp, jnp.sum)
        l_s[:, at] = total if begin else l_s[:, at] + total
        r_s[:, at] = row if begin else r_s[:, at] + row

    def forward(b, mine, begin=False):
        for at in halves():
            if mine:
                dp = dot(v_s[b], dt_ref[:, at])
                dpm_ref[b - 1, :, at] = dp
                probs(b, at, p_ref[b, :, at], dp)
            dp = dot(v_s[b], do_s[:, at])
            dpo_ref[b, :, at] = dp
            probs(b, past(at), p_ref[b, :, past(at)], dp, begin)
        return 0

    for at in halves():
        probs(0, at, s0_ref[:, at], dp0_ref[:, at], True)
    forward(0, False, True)
    lax.fori_loop(1, last, lambda b, _: forward(b, True), 0)

    @pl.when(chips == 3)
    def _():
        forward(3, False)
        for at in halves():
            probs(3, at, s3_ref[:, at], dp3_ref[:, at])

    stats_ref[0:1, :] = top
    stats_ref[1:2, :] = jnp.sum(l_s[...], axis=0, keepdims=True)
    stats_ref[2:3, :] = jnp.sum(r_s[...], axis=0, keepdims=True)
    stats_ref[3:8, :] = jnp.zeros((5, BOTH), F32)


def attended_kernel(where_ref, all_ref, a1, a2, a3, p_ref, o_ref, vt_s):
    chips = where_ref[0]
    for n, ref in enumerate((all_ref, a1, a2, a3)):
        vt_s[n] = ref[:, SUB : 2 * SUB, :].reshape(TOK, HD).T
    for at in columns():
        o_ref[:, at] = dot(vt_s[0], p_ref[0, :, at].astype(BF16))

    def add(b, _):
        for at in columns():
            o_ref[:, at] += dot(vt_s[b], p_ref[b, :, at].astype(BF16))
        return 0

    lax.fori_loop(1, chips + 1, add, 0)


def key_grads(p_ref, dp_ref, dpo_ref, ds_ref, f_ref, r_ref, all_ref, sw_ref):
    dk = jnp.zeros((TOK, HD), F32)
    dv = jnp.zeros((TOK, HD), F32)
    for at in columns():
        dp = dp_ref[:, at] if at.start < ROWS else dpo_ref[:, at.start - ROWS : at.stop - ROWS]
        p = p_ref[:, at] * f_ref[0:1, at]
        ds = (p * (dp - r_ref[0:1, at])).astype(BF16)
        ds_ref[:, at] = ds
        dk = dk + dot(ds, rows_at(all_ref, sw_ref, at, 0))
        dv = dv + dot(p.astype(BF16), rows_at(all_ref, sw_ref, at, 128))
    return dk * SCALING, dv


def grads_kernel(
    where_ref, stats_ref, swapped_stats_ref, all_ref, sw_ref, p_ref, dp_ref, dp3_ref, dpo_ref,
    c1, c2, c3, ds_ref, f_ref, r_s, g_s,
):
    chips = where_ref[0]
    for half in range(2):
        at = slice(half * ROWS, (half + 1) * ROWS)
        there = slice((1 - half) * ROWS, (2 - half) * ROWS)
        top = stats_ref[0:1, at]
        other_top = swapped_stats_ref[0:1, there]
        highest = jnp.maximum(top, other_top)
        f = jnp.exp2((top - highest) * EXPONENT)
        g = jnp.exp2((other_top - highest) * EXPONENT)
        inv = 1.0 / (stats_ref[1:2, at] * f + swapped_stats_ref[1:2, there] * g)
        row_dot = (stats_ref[2:3, at] * f + swapped_stats_ref[2:3, there] * g) * inv
        f_ref[:, at] = jnp.broadcast_to(f * inv, (8, ROWS))
        r_s[:, at] = jnp.broadcast_to(row_dot, (8, ROWS))

    def far(b, dp):
        dk, dv = key_grads(
            p_ref.at[b], dp, dpo_ref.at[b], ds_ref.at[b - 1], f_ref, r_s, all_ref, sw_ref
        )
        g_s[b - 1, :, 0:SUB, :] = dk.astype(BF16).reshape(HEADS, SUB, HD)
        g_s[b - 1, :, SUB : 2 * SUB, :] = dv.astype(BF16).reshape(HEADS, SUB, HD)
        return 0

    lax.fori_loop(1, jnp.minimum(chips, 2) + 1, lambda b, _: far(b, dp_ref.at[b - 1]), 0)

    @pl.when(chips == 3)
    def _():
        far(3, dp3_ref)

    for dist, ref in ((1, c1), (2, c2), (3, c3)):

        @pl.when(chips >= dist)
        def _():
            ref[...] = g_s[dist - 1]

        @pl.when(chips < dist)
        def _():
            ref[...] = jnp.zeros((HEADS, 2 * SUB, HD), BF16)


def query_kernel(
    where_ref, all_ref, sw_ref, a1, a2, a3, ds_ref, o_ref, f_ref, r_ref, p_ref, dp0_ref, dpo_ref,
    mine_ref, other_ref, own_ref, kt_s, g_s, ds0_s,
):
    chips = where_ref[0]
    dk, dv = key_grads(p_ref.at[0], dp0_ref, dpo_ref.at[0], ds0_s, f_ref, r_ref, all_ref, sw_ref)
    own_ref[:, 0:SUB, :] = dk.reshape(HEADS, SUB, HD)
    own_ref[:, SUB : 2 * SUB, :] = dv.reshape(HEADS, SUB, HD)
    for n, ref in enumerate((all_ref, a1, a2, a3)):
        kt_s[n] = ref[:, 0:SUB, :].reshape(TOK, HD).T
    for at in columns():
        g_s[:, at] = dot(kt_s[0], ds0_s[:, at])

    def add(b, _):
        for at in columns():
            g_s[:, at] += dot(kt_s[b], ds_ref[b - 1, :, at])
        return 0

    lax.fori_loop(1, chips + 1, add, 0)
    for n, ref in enumerate((mine_ref, other_ref)):
        at = slice(n * ROWS, (n + 1) * ROWS)
        o = (o_ref[:, at] * f_ref[0:1, at]).T
        g = (g_s[:, at] * SCALING).T
        ref[:, 0:128, :] = o.reshape(HEADS, 128, HD).astype(ref.dtype)
        ref[:, 128:256, :] = g.reshape(HEADS, 128, HD).astype(ref.dtype)


def sum_kernel(own_ref, c1, c2, c3, out_ref):
    total = own_ref[...]
    for ref in (c1, c2, c3):
        total = total + ref[...].astype(F32)
    out_ref[...] = total.astype(BF16)


def shape(*dims, dtype=BF16):
    return jax.ShapeDtypeStruct(dims, dtype)


def run(kernel, outs, scratch, *operands, first=SM, out=VM, cost=None):
    return pl.pallas_call(
        kernel,
        out_shape=outs,
        in_specs=[first] + [VM] * (len(operands) - 1),
        out_specs=tuple(out for _ in outs),
        scratch_shapes=scratch,
        compiler_params=params(),
        cost_estimate=cost,
    )(*operands)


def pack(shift, k, v, q, d):
    return pl.pallas_call(
        pack_kernel,
        out_shape=shape(HEADS, WIDE, HD),
        in_specs=[pl.BlockSpec(memory_space=pl.ANY)] * 5,
        out_specs=pl.BlockSpec(memory_space=pl.ANY),
        scratch_shapes=[
            pltpu.SMEM((HEADS,), jnp.int32),
            pltpu.VMEM((TOK, HD), BF16),
            pltpu.VMEM((TOK, HD), BF16),
            pltpu.VMEM((ROWS, HD), BF16),
            pltpu.VMEM((ROWS, HD), BF16),
            pltpu.VMEM((HEADS, QAT, HD), BF16),
            pltpu.VMEM((2, HEADS, 128, HD), BF16),
            pltpu.SemaphoreType.DMA((8,)),
        ],
        compiler_params=pltpu.CompilerParams(vmem_limit_bytes=60 * 1024 * 1024),
    )(shift, k, v, q, d)


def rows_of_groups():
    rows = []
    for start in range(0, 64, 8):
        for core in range(2):
            for place in range(HEADS):
                moved = GROUP // 2 // TOK if place >= HEADS // 2 else 0
                rows.append([(start + moved + 2 * i + core) % 64 * 8 + place for i in range(4)])
    return rows


ALONG = rows_of_groups()
SWAP = [(s * 8 + h, (s ^ 1) * 8 + h) for s in range(64) for h in range(8)]


def ahead(x, dist):
    return lax.ppermute(x, AXES, [(r[i], r[i + dist]) for r in ALONG for i in range(4 - dist)])


def behind(x, dist):
    return lax.ppermute(x, AXES, [(r[i + dist], r[i]) for r in ALONG for i in range(4 - dist)])


def local(queries, keys, values, d_attended, shift_amounts):
    seq_pos = lax.axis_index("seq")
    place = lax.axis_index("head")
    in_group = (seq_pos - jnp.where(place >= HEADS // 2, 4, 0)) & 7
    where = jnp.stack((in_group >> 1, in_group & 1)).astype(jnp.int32)
    packed = pack(
        shift_amounts,
        keys.reshape(TOK, HD),
        values.reshape(TOK, HD),
        queries.reshape(ROWS, HD),
        d_attended.reshape(ROWS, HD),
    )
    everything = lax.all_to_all(packed, "head", 0, 0, tiled=True)
    own = everything[:, 0 : 2 * SUB]
    a = [ahead(own, dist) for dist in (1, 2, 3)]
    swapped = lax.ppermute(everything[:, QAT:WIDE], AXES, SWAP)
    rows = pltpu.VMEM((8, BOTH), F32)
    flat = shape(8, BOTH, dtype=F32)
    part, half, top = shape(TOK, ROWS, dtype=F32), shape(HD, ROWS), shape(8, ROWS, dtype=F32)
    qt, dt, s0, dp0, m0 = run(
        first_kernel, (half, half, part, part, top), [], everything, first=VM, cost=LONG
    )
    s3, dp3, m3 = run(early_kernel, (part, part, top), [], where, qt, dt, a[2], cost=LONG)
    held, turned = pltpu.VMEM((4, TOK, HD), BF16), pltpu.VMEM((HD, ROWS), BF16)
    probs, dp, dpo, stats = run(
        probs_kernel,
        (
            shape(4, TOK, BOTH, dtype=F32),
            shape(2, TOK, ROWS, dtype=F32),
            shape(4, TOK, ROWS, dtype=F32),
            flat,
        ),
        [held, held, turned, turned, rows, rows, rows],
        where, everything, swapped, qt, dt, s0, dp0, m0, s3, dp3, m3, *a,
    )
    swapped_stats = lax.ppermute(stats, AXES, SWAP)
    (o,) = run(
        attended_kernel,
        (shape(HD, BOTH, dtype=F32),),
        [pltpu.VMEM((4, HD, TOK), BF16)],
        where, everything, *a, probs,
        cost=LONG,
    )
    block = shape(HEADS, 2 * SUB, HD)
    c1, c2, c3, ds, f, row_dot = run(
        grads_kernel,
        (block, block, block, shape(3, TOK, BOTH), flat, flat),
        [pltpu.VMEM((3, HEADS, 2 * SUB, HD), BF16)],
        where, stats, swapped_stats, everything, swapped, probs, dp, dp3, dpo,
    )
    back = [behind(part, dist) for dist, part in zip((1, 2, 3), (c1, c2, c3))]
    mine, other, grads = run(
        query_kernel,
        (shape(HEADS, 256, HD, dtype=F32), shape(HEADS, 256, HD), shape(HEADS, 2 * SUB, HD, dtype=F32)),
        [pltpu.VMEM((4, HD, TOK), BF16), pltpu.VMEM((HD, BOTH), F32), pltpu.VMEM((TOK, BOTH), BF16)],
        where, everything, swapped, *a, ds, o, f, row_dot, probs, dp0, dpo,
        cost=LONG,
    )
    oq = (mine + lax.ppermute(other, AXES, SWAP).astype(F32)).astype(BF16)
    (grads,) = run(sum_kernel, (block,), [], *(grads, *back), first=VM, cost=LONG)
    done = lax.all_to_all(jnp.concatenate((grads, oq), axis=1), "head", 0, 0, tiled=True)
    attended, d_queries, d_keys, d_values = run(
        unpack_kernel,
        (shape(ROWS, HD), shape(ROWS, HD), shape(TOK, HD), shape(TOK, HD)),
        [
            pltpu.VMEM((ROWS, HD), BF16),
            pltpu.VMEM((ROWS, HD), BF16),
            pltpu.VMEM((TOK, HD), BF16),
            pltpu.VMEM((TOK, HD), BF16),
            pltpu.SemaphoreType.DMA((4,)),
        ],
        shift_amounts,
        done,
        out=pl.BlockSpec(memory_space=pl.ANY),
    )
    return (
        attended.reshape(SUB, HEADS, PER, HD),
        d_queries.reshape(SUB, HEADS, PER, HD),
        d_keys.reshape(SUB, HEADS, HD),
        d_values.reshape(SUB, HEADS, HD),
    )


def solution(mesh):
    wide = P(("seq", "head"), None, None, None)
    flat = P(("seq", "head"), None, None)
    return jax.shard_map(
        local,
        mesh=mesh,
        in_specs=(wide, flat, flat, wide, P()),
        out_specs=(wide, wide, flat, flat),
        check_vma=False,
    )
```

```python
import math

import jax
import jax.numpy as jnp
from jax import lax
from jax.experimental import pallas as pl
from jax.experimental.pallas import tpu as pltpu
from jax.sharding import PartitionSpec as P

GROUP = 2048
HEADS = 8
PER = 4
HD = 128
TOK = 256
SUB = 32
ROWS = TOK * PER
COLS = 512
BOTH = 2 * ROWS
QAT = 64
WIDE = 320
LOG2E = 1.4426950408889634
NEG = -1e30
SCALING = 1.0 / math.sqrt(HD)
EXPONENT = SCALING * LOG2E
F32 = jnp.float32
BF16 = jnp.bfloat16
VM = pl.BlockSpec(memory_space=pltpu.VMEM)
SM = pl.BlockSpec(memory_space=pltpu.SMEM)
AXES = ("seq", "head")


LONG = pl.CostEstimate(flops=10_000_000_000, bytes_accessed=1 << 20, transcendentals=0)


def params():
    return pltpu.CompilerParams(vmem_limit_bytes=24 * 1024 * 1024)


def dot(a, b):
    return jnp.dot(a, b, preferred_element_type=F32)


def place_of_head(shift_ref, head):
    place = jnp.zeros(head.shape, jnp.int32)
    plain = jnp.int32(0)
    moved = jnp.int32(HEADS // 2)
    for h in range(HEADS):
        is_moved = (shift_ref[h] > 0).astype(jnp.int32)
        rank = jnp.where(is_moved == 1, moved, plain)
        place = jnp.where(head == h, rank, place)
        moved = moved + is_moved
        plain = plain + 1 - is_moved
    return place


def kv_order(shift_ref, back):
    local = lax.broadcasted_iota(jnp.int32, (TOK, TOK), 0 if back else 1)
    placed = lax.broadcasted_iota(jnp.int32, (TOK, TOK), 1 if back else 0)
    head = lax.broadcasted_iota(jnp.int32, (TOK, 1) if back else (1, TOK), 0 if back else 1) & 7
    place = place_of_head(shift_ref, head)
    hit = ((local >> 3) == (placed & 31)) & (place == (placed >> 5))
    return jnp.where(hit, 1.0, 0.0).astype(BF16)


def q_order(shift_ref, back):
    local = lax.broadcasted_iota(jnp.int32, (TOK, TOK), 0 if back else 1)
    placed = lax.broadcasted_iota(jnp.int32, (TOK, TOK), 1 if back else 0)
    head = lax.broadcasted_iota(jnp.int32, (TOK, 1) if back else (1, TOK), 0 if back else 1)
    place = place_of_head(shift_ref, (head >> 2) & 7)
    same = ((local >> 5) == ((placed & 31) >> 2)) & ((local & 3) == (placed & 3))
    return jnp.where(same & (place == (placed >> 5)), 1.0, 0.0).astype(BF16)


def pack_kernel(
    shift_hbm, k_hbm, v_hbm, q_hbm, d_hbm, out_hbm, shift_ref, k_ref, v_ref, q_ref, d_ref, kv_s, wide_s, sems
):
    copies = [
        pltpu.make_async_copy(src, dst, sems.at[n])
        for n, (src, dst) in enumerate(
            ((shift_hbm, shift_ref), (k_hbm, k_ref), (v_hbm, v_ref), (q_hbm, q_ref), (d_hbm, d_ref))
        )
    ]
    out = [pltpu.make_async_copy(kv_s, out_hbm.at[:, 0:QAT, :], sems.at[5])]
    for n in range(2):
        out.append(
            pltpu.make_async_copy(
                wide_s.at[n], out_hbm.at[:, QAT + n * 128 : QAT + n * 128 + 128, :], sems.at[6 + n]
            )
        )
    for copy in copies:
        copy.start()
    copies[0].wait()
    order = kv_order(shift_ref, False)
    wide_order = q_order(shift_ref, False)
    for n, ref in enumerate((k_ref, v_ref)):
        copies[n + 1].wait()
        moved = dot(order, ref[...]).astype(BF16)
        for h in range(HEADS):
            kv_s[h, n * SUB : (n + 1) * SUB, :] = moved[h * SUB : (h + 1) * SUB]
    out[0].start()
    for n, ref in enumerate((q_ref, d_ref)):
        copies[n + 3].wait()
        for b in range(4):
            moved = dot(wide_order, ref[b * TOK : (b + 1) * TOK, :]).astype(BF16)
            for h in range(HEADS):
                wide_s[n, h, b * 32 : b * 32 + 32, :] = moved[h * 32 : (h + 1) * 32]
        out[n + 1].start()
    for copy in out:
        copy.wait()


def unpack_kernel(shift_ref, in_ref, o_hbm, q_hbm, k_hbm, v_hbm, o_s, q_s, k_s, v_s, sems):
    order = kv_order(shift_ref, True)
    wide_order = q_order(shift_ref, True)
    copies = [
        pltpu.make_async_copy(src, dst, sems.at[n])
        for n, (src, dst) in enumerate(((o_s, o_hbm), (q_s, q_hbm), (k_s, k_hbm), (v_s, v_hbm)))
    ]
    for n, ref in enumerate((o_s, q_s)):
        for b in range(4):
            at = QAT + n * 128 + b * 32
            held = in_ref[:, at : at + 32, :].reshape(TOK, HD)
            ref[b * TOK : (b + 1) * TOK, :] = dot(wide_order, held).astype(BF16)
        copies[n].start()
    for n, ref in enumerate((k_s, v_s)):
        held = in_ref[:, n * SUB : (n + 1) * SUB, :].reshape(TOK, HD)
        ref[...] = dot(order, held).astype(BF16)
        copies[n + 2].start()
    for copy in copies:
        copy.wait()


def columns():
    return [slice(c * COLS, (c + 1) * COLS) for c in range(BOTH // COLS)]


def fold(x, op):
    return op(x.reshape(TOK // 8, 8, COLS), axis=0)


def halves():
    return [slice(c * COLS, (c + 1) * COLS) for c in range(ROWS // COLS)]


def past(at):
    return slice(ROWS + at.start, ROWS + at.stop)


def rows_at(all_ref, swapped_ref, at, which):
    start = at.start % ROWS // 128
    held = slice(start, start + COLS // 128)
    if at.start < ROWS:
        return all_ref[held, QAT + which : QAT + which + 128, :].reshape(COLS, HD)
    return swapped_ref[held, which : which + 128, :].reshape(COLS, HD)


def first_kernel(all_ref, qt_ref, dt_ref, s_ref, dp_ref, m_ref):
    for ref, at in ((qt_ref, QAT), (dt_ref, QAT + 128)):
        ref[...] = all_ref[:, at : at + 128, :].reshape(ROWS, HD).T
    keys = all_ref[:, 0:SUB, :].reshape(TOK, HD)
    vals = all_ref[:, SUB : 2 * SUB, :].reshape(TOK, HD)
    for at in halves():
        s = dot(keys, qt_ref[:, at])
        u = lax.broadcasted_iota(jnp.int32, (TOK, COLS), 0)
        t = (lax.broadcasted_iota(jnp.int32, (TOK, COLS), 1) + at.start) >> 2
        s = jnp.where(u <= t, s, NEG)
        s_ref[:, at] = s
        m_ref[:, at] = fold(s, jnp.max)
        dp_ref[:, at] = dot(vals, dt_ref[:, at])


def other_kernel(where_ref, all_ref, sw_ref, qt_ref, dt_ref, s_ref, dp_ref, m_ref):
    core = where_ref[1]
    qt_ref[...] = sw_ref[:, 0:128, :].reshape(ROWS, HD).T
    dt_ref[...] = sw_ref[:, 128:256, :].reshape(ROWS, HD).T
    keys = all_ref[:, 0:SUB, :].reshape(TOK, HD)
    vals = all_ref[:, SUB : 2 * SUB, :].reshape(TOK, HD)
    for at in halves():
        s = jnp.where(core == 0, dot(keys, qt_ref[:, at]), NEG)
        s_ref[:, at] = s
        m_ref[:, at] = fold(s, jnp.max)
        dp_ref[:, at] = dot(vals, dt_ref[:, at])


def early_kernel(where_ref, qt_ref, dt_ref, a3, s_ref, dp_ref, m_ref):
    chips = where_ref[0]

    @pl.when(chips == 3)
    def _():
        keys = a3[:, 0:SUB, :].reshape(TOK, HD)
        vals = a3[:, SUB : 2 * SUB, :].reshape(TOK, HD)
        for at in halves():
            s = dot(keys, qt_ref[:, at])
            s_ref[:, at] = s
            m_ref[:, at] = fold(s, jnp.max)
            dp_ref[:, at] = dot(vals, dt_ref[:, at])

    @pl.when(chips < 3)
    def _():
        m_ref[...] = jnp.full((8, ROWS), NEG, F32)


def probs_kernel(
    where_ref, qt_ref, dt_ref, s0_ref, dp0_ref, m0_ref, s3_ref, dp3_ref, m3_ref,
    qo_s, do_s, s0o_ref, dp0o_ref, m0o_ref, a1, a2, a3,
    p_ref, dpm_ref, dpo_ref, stats_ref, k_s, v_s, m_s, l_s, r_s,
):
    chips = where_ref[0]
    last = jnp.minimum(chips, 2) + 1
    for n, ref in enumerate((a1, a2, a3)):
        k_s[n + 1] = ref[:, 0:SUB, :].reshape(TOK, HD)
        v_s[n + 1] = ref[:, SUB : 2 * SUB, :].reshape(TOK, HD)
    m_s[:, 0:ROWS] = jnp.maximum(m0_ref[...], m3_ref[...])
    m_s[:, ROWS:BOTH] = m0o_ref[...]

    def scores(b, mine):
        for at in halves():
            if mine:
                s = dot(k_s[b], qt_ref[:, at])
                p_ref[b, :, at] = s
                m_s[:, at] = jnp.maximum(m_s[:, at], fold(s, jnp.max))
            s = dot(k_s[b], qo_s[:, at])
            p_ref[b, :, past(at)] = s
            m_s[:, past(at)] = jnp.maximum(m_s[:, past(at)], fold(s, jnp.max))
        return 0

    lax.fori_loop(1, last, lambda b, _: scores(b, True), 0)

    @pl.when(chips == 3)
    def _():
        scores(3, False)

    top = jnp.max(m_s[...], axis=0, keepdims=True)
    m_s[...] = jnp.broadcast_to(top, (8, BOTH))

    def probs(b, at, s, dp, begin=False):
        p = jnp.exp2((s - m_s[0:1, at]) * EXPONENT)
        p_ref[b, :, at] = p
        total = fold(p, jnp.sum)
        row = fold(p * dp, jnp.sum)
        l_s[:, at] = total if begin else l_s[:, at] + total
        r_s[:, at] = row if begin else r_s[:, at] + row

    def forward(b, mine):
        for at in halves():
            if mine:
                dp = dot(v_s[b], dt_ref[:, at])
                dpm_ref[b - 1, :, at] = dp
                probs(b, at, p_ref[b, :, at], dp)
            dp = dot(v_s[b], do_s[:, at])
            dpo_ref[b, :, at] = dp
            probs(b, past(at), p_ref[b, :, past(at)], dp)
        return 0

    for at in halves():
        probs(0, at, s0_ref[:, at], dp0_ref[:, at], True)
        dpo_ref[0, :, at] = dp0o_ref[:, at]
        probs(0, past(at), s0o_ref[:, at], dp0o_ref[:, at], True)
    lax.fori_loop(1, last, lambda b, _: forward(b, True), 0)

    @pl.when(chips == 3)
    def _():
        forward(3, False)
        for at in halves():
            probs(3, at, s3_ref[:, at], dp3_ref[:, at])

    stats_ref[0:1, :] = top
    stats_ref[1:2, :] = jnp.sum(l_s[...], axis=0, keepdims=True)
    stats_ref[2:3, :] = jnp.sum(r_s[...], axis=0, keepdims=True)
    stats_ref[3:8, :] = jnp.zeros((5, BOTH), F32)


def attended_kernel(where_ref, all_ref, a1, a2, a3, p_ref, o_ref, vt_s):
    chips = where_ref[0]
    for n, ref in enumerate((all_ref, a1, a2, a3)):
        vt_s[n] = ref[:, SUB : 2 * SUB, :].reshape(TOK, HD).T
    for at in columns():
        o_ref[:, at] = dot(vt_s[0], p_ref[0, :, at].astype(BF16))

    def add(b, _):
        for at in columns():
            o_ref[:, at] += dot(vt_s[b], p_ref[b, :, at].astype(BF16))
        return 0

    lax.fori_loop(1, chips + 1, add, 0)


def key_grads(p_ref, dp_ref, dpo_ref, ds_ref, f_ref, r_ref, all_ref, sw_ref):
    dk = jnp.zeros((TOK, HD), F32)
    dv = jnp.zeros((TOK, HD), F32)
    for at in columns():
        dp = dp_ref[:, at] if at.start < ROWS else dpo_ref[:, at.start - ROWS : at.stop - ROWS]
        p = p_ref[:, at] * f_ref[0:1, at]
        ds = (p * (dp - r_ref[0:1, at])).astype(BF16)
        ds_ref[:, at] = ds
        dk = dk + dot(ds, rows_at(all_ref, sw_ref, at, 0))
        dv = dv + dot(p.astype(BF16), rows_at(all_ref, sw_ref, at, 128))
    return dk * SCALING, dv


def grads_kernel(
    where_ref, stats_ref, swapped_stats_ref, all_ref, sw_ref, p_ref, dp_ref, dp3_ref, dpo_ref,
    c1, c2, c3, ds_ref, f_ref, r_s, g_s,
):
    chips = where_ref[0]
    for half in range(2):
        at = slice(half * ROWS, (half + 1) * ROWS)
        there = slice((1 - half) * ROWS, (2 - half) * ROWS)
        top = stats_ref[0:1, at]
        other_top = swapped_stats_ref[0:1, there]
        highest = jnp.maximum(top, other_top)
        f = jnp.exp2((top - highest) * EXPONENT)
        g = jnp.exp2((other_top - highest) * EXPONENT)
        inv = 1.0 / (stats_ref[1:2, at] * f + swapped_stats_ref[1:2, there] * g)
        row_dot = (stats_ref[2:3, at] * f + swapped_stats_ref[2:3, there] * g) * inv
        f_ref[:, at] = jnp.broadcast_to(f * inv, (8, ROWS))
        r_s[:, at] = jnp.broadcast_to(row_dot, (8, ROWS))

    def far(b, dp):
        dk, dv = key_grads(
            p_ref.at[b], dp, dpo_ref.at[b], ds_ref.at[b - 1], f_ref, r_s, all_ref, sw_ref
        )
        g_s[b - 1, :, 0:SUB, :] = dk.astype(BF16).reshape(HEADS, SUB, HD)
        g_s[b - 1, :, SUB : 2 * SUB, :] = dv.astype(BF16).reshape(HEADS, SUB, HD)
        return 0

    lax.fori_loop(1, jnp.minimum(chips, 2) + 1, lambda b, _: far(b, dp_ref.at[b - 1]), 0)

    @pl.when(chips == 3)
    def _():
        far(3, dp3_ref)

    for dist, ref in ((1, c1), (2, c2), (3, c3)):

        @pl.when(chips >= dist)
        def _():
            ref[...] = g_s[dist - 1]

        @pl.when(chips < dist)
        def _():
            ref[...] = jnp.zeros((HEADS, 2 * SUB, HD), BF16)


def query_kernel(
    where_ref, all_ref, sw_ref, a1, a2, a3, ds_ref, o_ref, f_ref, r_ref, p_ref, dp0_ref, dpo_ref,
    mine_ref, other_ref, own_ref, kt_s, g_s, ds0_s,
):
    chips = where_ref[0]
    dk, dv = key_grads(p_ref.at[0], dp0_ref, dpo_ref.at[0], ds0_s, f_ref, r_ref, all_ref, sw_ref)
    own_ref[:, 0:SUB, :] = dk.reshape(HEADS, SUB, HD)
    own_ref[:, SUB : 2 * SUB, :] = dv.reshape(HEADS, SUB, HD)
    for n, ref in enumerate((all_ref, a1, a2, a3)):
        kt_s[n] = ref[:, 0:SUB, :].reshape(TOK, HD).T
    for at in columns():
        g_s[:, at] = dot(kt_s[0], ds0_s[:, at])

    def add(b, _):
        for at in columns():
            g_s[:, at] += dot(kt_s[b], ds_ref[b - 1, :, at])
        return 0

    lax.fori_loop(1, chips + 1, add, 0)
    for n, ref in enumerate((mine_ref, other_ref)):
        at = slice(n * ROWS, (n + 1) * ROWS)
        o = (o_ref[:, at] * f_ref[0:1, at]).T
        g = (g_s[:, at] * SCALING).T
        ref[:, 0:128, :] = o.reshape(HEADS, 128, HD).astype(ref.dtype)
        ref[:, 128:256, :] = g.reshape(HEADS, 128, HD).astype(ref.dtype)


def sum_kernel(own_ref, c1, c2, c3, out_ref):
    total = own_ref[...]
    for ref in (c1, c2, c3):
        total = total + ref[...].astype(F32)
    out_ref[...] = total.astype(BF16)


def shape(*dims, dtype=BF16):
    return jax.ShapeDtypeStruct(dims, dtype)


def run(kernel, outs, scratch, *operands, first=SM, out=VM, cost=None):
    return pl.pallas_call(
        kernel,
        out_shape=outs,
        in_specs=[first] + [VM] * (len(operands) - 1),
        out_specs=tuple(out for _ in outs),
        scratch_shapes=scratch,
        compiler_params=params(),
        cost_estimate=cost,
    )(*operands)


def pack(shift, k, v, q, d):
    return pl.pallas_call(
        pack_kernel,
        out_shape=shape(HEADS, WIDE, HD),
        in_specs=[pl.BlockSpec(memory_space=pl.ANY)] * 5,
        out_specs=pl.BlockSpec(memory_space=pl.ANY),
        scratch_shapes=[
            pltpu.SMEM((HEADS,), jnp.int32),
            pltpu.VMEM((TOK, HD), BF16),
            pltpu.VMEM((TOK, HD), BF16),
            pltpu.VMEM((ROWS, HD), BF16),
            pltpu.VMEM((ROWS, HD), BF16),
            pltpu.VMEM((HEADS, QAT, HD), BF16),
            pltpu.VMEM((2, HEADS, 128, HD), BF16),
            pltpu.SemaphoreType.DMA((8,)),
        ],
        compiler_params=pltpu.CompilerParams(vmem_limit_bytes=60 * 1024 * 1024),
    )(shift, k, v, q, d)


def rows_of_groups():
    rows = []
    for start in range(0, 64, 8):
        for core in range(2):
            for place in range(HEADS):
                moved = GROUP // 2 // TOK if place >= HEADS // 2 else 0
                rows.append([(start + moved + 2 * i + core) % 64 * 8 + place for i in range(4)])
    return rows


ALONG = rows_of_groups()
SWAP = [(s * 8 + h, (s ^ 1) * 8 + h) for s in range(64) for h in range(8)]


def ahead(x, dist):
    return lax.ppermute(x, AXES, [(r[i], r[i + dist]) for r in ALONG for i in range(4 - dist)])


def behind(x, dist):
    return lax.ppermute(x, AXES, [(r[i + dist], r[i]) for r in ALONG for i in range(4 - dist)])


def local(queries, keys, values, d_attended, shift_amounts):
    seq_pos = lax.axis_index("seq")
    place = lax.axis_index("head")
    in_group = (seq_pos - jnp.where(place >= HEADS // 2, 4, 0)) & 7
    where = jnp.stack((in_group >> 1, in_group & 1)).astype(jnp.int32)
    packed = pack(
        shift_amounts,
        keys.reshape(TOK, HD),
        values.reshape(TOK, HD),
        queries.reshape(ROWS, HD),
        d_attended.reshape(ROWS, HD),
    )
    everything = lax.all_to_all(packed, "head", 0, 0, tiled=True)
    own = everything[:, 0 : 2 * SUB]
    a = [ahead(own, dist) for dist in (1, 2, 3)]
    swapped = lax.ppermute(everything[:, QAT:WIDE], AXES, SWAP)
    rows = pltpu.VMEM((8, BOTH), F32)
    flat = shape(8, BOTH, dtype=F32)
    part, half, top = shape(TOK, ROWS, dtype=F32), shape(HD, ROWS), shape(8, ROWS, dtype=F32)
    qt, dt, s0, dp0, m0 = run(
        first_kernel, (half, half, part, part, top), [], everything, first=VM, cost=LONG
    )
    s3, dp3, m3 = run(early_kernel, (part, part, top), [], where, qt, dt, a[2], cost=LONG)
    qo, do, s0o, dp0o, m0o = run(
        other_kernel, (half, half, part, part, top), [], where, everything, swapped, cost=None
    )
    held, turned = pltpu.VMEM((4, TOK, HD), BF16), pltpu.VMEM((HD, ROWS), BF16)
    probs, dp, dpo, stats = run(
        probs_kernel,
        (
            shape(4, TOK, BOTH, dtype=F32),
            shape(2, TOK, ROWS, dtype=F32),
            shape(4, TOK, ROWS, dtype=F32),
            flat,
        ),
        [held, held, rows, rows, rows],
        where, qt, dt, s0, dp0, m0, s3, dp3, m3, qo, do, s0o, dp0o, m0o, *a,
    )
    swapped_stats = lax.ppermute(stats, AXES, SWAP)
    (o,) = run(
        attended_kernel,
        (shape(HD, BOTH, dtype=F32),),
        [pltpu.VMEM((4, HD, TOK), BF16)],
        where, everything, *a, probs,
        cost=LONG,
    )
    block = shape(HEADS, 2 * SUB, HD)
    c1, c2, c3, ds, f, row_dot = run(
        grads_kernel,
        (block, block, block, shape(3, TOK, BOTH), flat, flat),
        [pltpu.VMEM((3, HEADS, 2 * SUB, HD), BF16)],
        where, stats, swapped_stats, everything, swapped, probs, dp, dp3, dpo,
    )
    back = [behind(part, dist) for dist, part in zip((1, 2, 3), (c1, c2, c3))]
    mine, other, grads = run(
        query_kernel,
        (shape(HEADS, 256, HD, dtype=F32), shape(HEADS, 256, HD), shape(HEADS, 2 * SUB, HD, dtype=F32)),
        [pltpu.VMEM((4, HD, TOK), BF16), pltpu.VMEM((HD, BOTH), F32), pltpu.VMEM((TOK, BOTH), BF16)],
        where, everything, swapped, *a, ds, o, f, row_dot, probs, dp0, dpo,
        cost=LONG,
    )
    oq = (mine + lax.ppermute(other, AXES, SWAP).astype(F32)).astype(BF16)
    (grads,) = run(sum_kernel, (block,), [], *(grads, *back), first=VM, cost=LONG)
    done = lax.all_to_all(jnp.concatenate((grads, oq), axis=1), "head", 0, 0, tiled=True)
    attended, d_queries, d_keys, d_values = run(
        unpack_kernel,
        (shape(ROWS, HD), shape(ROWS, HD), shape(TOK, HD), shape(TOK, HD)),
        [
            pltpu.VMEM((ROWS, HD), BF16),
            pltpu.VMEM((ROWS, HD), BF16),
            pltpu.VMEM((TOK, HD), BF16),
            pltpu.VMEM((TOK, HD), BF16),
            pltpu.SemaphoreType.DMA((4,)),
        ],
        shift_amounts,
        done,
        out=pl.BlockSpec(memory_space=pl.ANY),
    )
    return (
        attended.reshape(SUB, HEADS, PER, HD),
        d_queries.reshape(SUB, HEADS, PER, HD),
        d_keys.reshape(SUB, HEADS, HD),
        d_values.reshape(SUB, HEADS, HD),
    )


def solution(mesh):
    wide = P(("seq", "head"), None, None, None)
    flat = P(("seq", "head"), None, None)
    return jax.shard_map(
        local,
        mesh=mesh,
        in_specs=(wide, flat, flat, wide, P()),
        out_specs=(wide, wide, flat, flat),
        check_vma=False,
    )
```

```python
import math

import jax
import jax.numpy as jnp
from jax import lax
from jax.experimental import pallas as pl
from jax.experimental.pallas import tpu as pltpu
from jax.sharding import PartitionSpec as P

GROUP = 2048
HEADS = 8
PER = 4
HD = 128
TOK = 256
SUB = 32
ROWS = TOK * PER
COLS = 512
BOTH = 2 * ROWS
QAT = 64
WIDE = 320
LOG2E = 1.4426950408889634
NEG = -1e30
SCALING = 1.0 / math.sqrt(HD)
EXPONENT = SCALING * LOG2E
F32 = jnp.float32
BF16 = jnp.bfloat16
VM = pl.BlockSpec(memory_space=pltpu.VMEM)
SM = pl.BlockSpec(memory_space=pltpu.SMEM)
AXES = ("seq", "head")


LONG = pl.CostEstimate(flops=10_000_000_000, bytes_accessed=1 << 20, transcendentals=0)


def params():
    return pltpu.CompilerParams(vmem_limit_bytes=24 * 1024 * 1024)


def dot(a, b):
    return jnp.dot(a, b, preferred_element_type=F32)


def place_of_head(shift_ref, head):
    place = jnp.zeros(head.shape, jnp.int32)
    plain = jnp.int32(0)
    moved = jnp.int32(HEADS // 2)
    for h in range(HEADS):
        is_moved = (shift_ref[h] > 0).astype(jnp.int32)
        rank = jnp.where(is_moved == 1, moved, plain)
        place = jnp.where(head == h, rank, place)
        moved = moved + is_moved
        plain = plain + 1 - is_moved
    return place


def kv_order(shift_ref, back):
    local = lax.broadcasted_iota(jnp.int32, (TOK, TOK), 0 if back else 1)
    placed = lax.broadcasted_iota(jnp.int32, (TOK, TOK), 1 if back else 0)
    head = lax.broadcasted_iota(jnp.int32, (TOK, 1) if back else (1, TOK), 0 if back else 1) & 7
    place = place_of_head(shift_ref, head)
    hit = ((local >> 3) == (placed & 31)) & (place == (placed >> 5))
    return jnp.where(hit, 1.0, 0.0).astype(BF16)


def q_order(shift_ref, back):
    local = lax.broadcasted_iota(jnp.int32, (TOK, TOK), 0 if back else 1)
    placed = lax.broadcasted_iota(jnp.int32, (TOK, TOK), 1 if back else 0)
    head = lax.broadcasted_iota(jnp.int32, (TOK, 1) if back else (1, TOK), 0 if back else 1)
    place = place_of_head(shift_ref, (head >> 2) & 7)
    same = ((local >> 5) == ((placed & 31) >> 2)) & ((local & 3) == (placed & 3))
    return jnp.where(same & (place == (placed >> 5)), 1.0, 0.0).astype(BF16)


def pack_kernel(
    shift_hbm, k_hbm, v_hbm, q_hbm, d_hbm, out_hbm, shift_ref, k_ref, v_ref, q_ref, d_ref, kv_s, wide_s, sems
):
    copies = [
        pltpu.make_async_copy(src, dst, sems.at[n])
        for n, (src, dst) in enumerate(
            ((shift_hbm, shift_ref), (k_hbm, k_ref), (v_hbm, v_ref), (q_hbm, q_ref), (d_hbm, d_ref))
        )
    ]
    out = [pltpu.make_async_copy(kv_s, out_hbm.at[:, 0:QAT, :], sems.at[5])]
    for n in range(2):
        out.append(
            pltpu.make_async_copy(
                wide_s.at[n], out_hbm.at[:, QAT + n * 128 : QAT + n * 128 + 128, :], sems.at[6 + n]
            )
        )
    for copy in copies:
        copy.start()
    copies[0].wait()
    order = kv_order(shift_ref, False)
    wide_order = q_order(shift_ref, False)
    for n, ref in enumerate((k_ref, v_ref)):
        copies[n + 1].wait()
        moved = dot(order, ref[...]).astype(BF16)
        for h in range(HEADS):
            kv_s[h, n * SUB : (n + 1) * SUB, :] = moved[h * SUB : (h + 1) * SUB]
    out[0].start()
    for n, ref in enumerate((q_ref, d_ref)):
        copies[n + 3].wait()
        for b in range(4):
            moved = dot(wide_order, ref[b * TOK : (b + 1) * TOK, :]).astype(BF16)
            for h in range(HEADS):
                wide_s[n, h, b * 32 : b * 32 + 32, :] = moved[h * 32 : (h + 1) * 32]
        out[n + 1].start()
    for copy in out:
        copy.wait()


def unpack_kernel(shift_ref, in_ref, o_hbm, q_hbm, k_hbm, v_hbm, o_s, q_s, k_s, v_s, sems):
    order = kv_order(shift_ref, True)
    wide_order = q_order(shift_ref, True)
    copies = [
        pltpu.make_async_copy(src, dst, sems.at[n])
        for n, (src, dst) in enumerate(((o_s, o_hbm), (q_s, q_hbm), (k_s, k_hbm), (v_s, v_hbm)))
    ]
    for n, ref in enumerate((o_s, q_s)):
        for b in range(4):
            at = QAT + n * 128 + b * 32
            held = in_ref[:, at : at + 32, :].reshape(TOK, HD)
            ref[b * TOK : (b + 1) * TOK, :] = dot(wide_order, held).astype(BF16)
        copies[n].start()
    for n, ref in enumerate((k_s, v_s)):
        held = in_ref[:, n * SUB : (n + 1) * SUB, :].reshape(TOK, HD)
        ref[...] = dot(order, held).astype(BF16)
        copies[n + 2].start()
    for copy in copies:
        copy.wait()


def columns():
    return [slice(c * COLS, (c + 1) * COLS) for c in range(BOTH // COLS)]


def fold(x, op):
    return op(x.reshape(TOK // 8, 8, COLS), axis=0)


def halves():
    return [slice(c * COLS, (c + 1) * COLS) for c in range(ROWS // COLS)]


def past(at):
    return slice(ROWS + at.start, ROWS + at.stop)


def rows_at(all_ref, swapped_ref, at, which):
    start = at.start % ROWS // 128
    held = slice(start, start + COLS // 128)
    if at.start < ROWS:
        return all_ref[held, QAT + which : QAT + which + 128, :].reshape(COLS, HD)
    return swapped_ref[held, which : which + 128, :].reshape(COLS, HD)


def first_kernel(all_ref, qt_ref, dt_ref, s_ref, dp_ref, m_ref):
    for ref, at in ((qt_ref, QAT), (dt_ref, QAT + 128)):
        ref[...] = all_ref[:, at : at + 128, :].reshape(ROWS, HD).T
    keys = all_ref[:, 0:SUB, :].reshape(TOK, HD)
    vals = all_ref[:, SUB : 2 * SUB, :].reshape(TOK, HD)
    for at in halves():
        s = dot(keys, qt_ref[:, at])
        u = lax.broadcasted_iota(jnp.int32, (TOK, COLS), 0)
        t = (lax.broadcasted_iota(jnp.int32, (TOK, COLS), 1) + at.start) >> 2
        s = jnp.where(u <= t, s, NEG)
        s_ref[:, at] = s
        m_ref[:, at] = fold(s, jnp.max)
        dp_ref[:, at] = dot(vals, dt_ref[:, at])


def other_kernel(where_ref, all_ref, sw_ref, qt_ref, dt_ref, s_ref, dp_ref, m_ref):
    core = where_ref[1]
    qt_ref[...] = sw_ref[:, 0:128, :].reshape(ROWS, HD).T
    dt_ref[...] = sw_ref[:, 128:256, :].reshape(ROWS, HD).T
    keys = all_ref[:, 0:SUB, :].reshape(TOK, HD)
    vals = all_ref[:, SUB : 2 * SUB, :].reshape(TOK, HD)
    for at in halves():
        s = jnp.where(core == 0, dot(keys, qt_ref[:, at]), NEG)
        s_ref[:, at] = s
        m_ref[:, at] = fold(s, jnp.max)
        dp_ref[:, at] = dot(vals, dt_ref[:, at])


def early_kernel(where_ref, qt_ref, dt_ref, a3, s_ref, dp_ref, m_ref):
    chips = where_ref[0]

    @pl.when(chips == 3)
    def _():
        keys = a3[:, 0:SUB, :].reshape(TOK, HD)
        vals = a3[:, SUB : 2 * SUB, :].reshape(TOK, HD)
        for at in halves():
            s = dot(keys, qt_ref[:, at])
            s_ref[:, at] = s
            m_ref[:, at] = fold(s, jnp.max)
            dp_ref[:, at] = dot(vals, dt_ref[:, at])

    @pl.when(chips < 3)
    def _():
        m_ref[...] = jnp.full((8, ROWS), NEG, F32)


def probs_kernel(
    where_ref, qt_ref, dt_ref, s0_ref, dp0_ref, m0_ref, s3_ref, dp3_ref, m3_ref,
    qo_s, do_s, s0o_ref, dp0o_ref, m0o_ref, s3o_ref, dp3o_ref, m3o_ref, a1, a2, a3,
    p_ref, dpm_ref, dpo_ref, stats_ref, k_s, v_s, m_s, l_s, r_s,
):
    chips = where_ref[0]
    last = jnp.minimum(chips, 2) + 1
    for n, ref in enumerate((a1, a2, a3)):
        k_s[n + 1] = ref[:, 0:SUB, :].reshape(TOK, HD)
        v_s[n + 1] = ref[:, SUB : 2 * SUB, :].reshape(TOK, HD)
    m_s[:, 0:ROWS] = jnp.maximum(m0_ref[...], m3_ref[...])
    m_s[:, ROWS:BOTH] = jnp.maximum(m0o_ref[...], m3o_ref[...])

    def scores(b, mine):
        for at in halves():
            if mine:
                s = dot(k_s[b], qt_ref[:, at])
                p_ref[b, :, at] = s
                m_s[:, at] = jnp.maximum(m_s[:, at], fold(s, jnp.max))
            s = dot(k_s[b], qo_s[:, at])
            p_ref[b, :, past(at)] = s
            m_s[:, past(at)] = jnp.maximum(m_s[:, past(at)], fold(s, jnp.max))
        return 0

    lax.fori_loop(1, last, lambda b, _: scores(b, True), 0)

    top = jnp.max(m_s[...], axis=0, keepdims=True)
    m_s[...] = jnp.broadcast_to(top, (8, BOTH))

    def probs(b, at, s, dp, begin=False):
        p = jnp.exp2((s - m_s[0:1, at]) * EXPONENT)
        p_ref[b, :, at] = p
        total = fold(p, jnp.sum)
        row = fold(p * dp, jnp.sum)
        l_s[:, at] = total if begin else l_s[:, at] + total
        r_s[:, at] = row if begin else r_s[:, at] + row

    def forward(b, mine):
        for at in halves():
            if mine:
                dp = dot(v_s[b], dt_ref[:, at])
                dpm_ref[b - 1, :, at] = dp
                probs(b, at, p_ref[b, :, at], dp)
            dp = dot(v_s[b], do_s[:, at])
            dpo_ref[b, :, at] = dp
            probs(b, past(at), p_ref[b, :, past(at)], dp)
        return 0

    for at in halves():
        probs(0, at, s0_ref[:, at], dp0_ref[:, at], True)
        dpo_ref[0, :, at] = dp0o_ref[:, at]
        probs(0, past(at), s0o_ref[:, at], dp0o_ref[:, at], True)
    lax.fori_loop(1, last, lambda b, _: forward(b, True), 0)

    @pl.when(chips == 3)
    def _():
        for at in halves():
            probs(3, at, s3_ref[:, at], dp3_ref[:, at])
            dpo_ref[3, :, at] = dp3o_ref[:, at]
            probs(3, past(at), s3o_ref[:, at], dp3o_ref[:, at])

    stats_ref[0:1, :] = top
    stats_ref[1:2, :] = jnp.sum(l_s[...], axis=0, keepdims=True)
    stats_ref[2:3, :] = jnp.sum(r_s[...], axis=0, keepdims=True)
    stats_ref[3:8, :] = jnp.zeros((5, BOTH), F32)


def attended_kernel(where_ref, all_ref, a1, a2, a3, p_ref, o_ref, vt_s):
    chips = where_ref[0]
    for n, ref in enumerate((all_ref, a1, a2, a3)):
        vt_s[n] = ref[:, SUB : 2 * SUB, :].reshape(TOK, HD).T
    for at in columns():
        o_ref[:, at] = dot(vt_s[0], p_ref[0, :, at].astype(BF16))

    def add(b, _):
        for at in columns():
            o_ref[:, at] += dot(vt_s[b], p_ref[b, :, at].astype(BF16))
        return 0

    lax.fori_loop(1, chips + 1, add, 0)


def key_grads(p_ref, dp_ref, dpo_ref, ds_ref, f_ref, r_ref, all_ref, sw_ref):
    dk = jnp.zeros((TOK, HD), F32)
    dv = jnp.zeros((TOK, HD), F32)
    for at in columns():
        dp = dp_ref[:, at] if at.start < ROWS else dpo_ref[:, at.start - ROWS : at.stop - ROWS]
        p = p_ref[:, at] * f_ref[0:1, at]
        ds = (p * (dp - r_ref[0:1, at])).astype(BF16)
        ds_ref[:, at] = ds
        dk = dk + dot(ds, rows_at(all_ref, sw_ref, at, 0))
        dv = dv + dot(p.astype(BF16), rows_at(all_ref, sw_ref, at, 128))
    return dk * SCALING, dv


def grads_kernel(
    where_ref, stats_ref, swapped_stats_ref, all_ref, sw_ref, p_ref, dp_ref, dp3_ref, dpo_ref,
    c1, c2, c3, ds_ref, f_ref, r_s, g_s,
):
    chips = where_ref[0]
    for half in range(2):
        at = slice(half * ROWS, (half + 1) * ROWS)
        there = slice((1 - half) * ROWS, (2 - half) * ROWS)
        top = stats_ref[0:1, at]
        other_top = swapped_stats_ref[0:1, there]
        highest = jnp.maximum(top, other_top)
        f = jnp.exp2((top - highest) * EXPONENT)
        g = jnp.exp2((other_top - highest) * EXPONENT)
        inv = 1.0 / (stats_ref[1:2, at] * f + swapped_stats_ref[1:2, there] * g)
        row_dot = (stats_ref[2:3, at] * f + swapped_stats_ref[2:3, there] * g) * inv
        f_ref[:, at] = jnp.broadcast_to(f * inv, (8, ROWS))
        r_s[:, at] = jnp.broadcast_to(row_dot, (8, ROWS))

    def far(b, dp):
        dk, dv = key_grads(
            p_ref.at[b], dp, dpo_ref.at[b], ds_ref.at[b - 1], f_ref, r_s, all_ref, sw_ref
        )
        g_s[b - 1, :, 0:SUB, :] = dk.astype(BF16).reshape(HEADS, SUB, HD)
        g_s[b - 1, :, SUB : 2 * SUB, :] = dv.astype(BF16).reshape(HEADS, SUB, HD)
        return 0

    lax.fori_loop(1, jnp.minimum(chips, 2) + 1, lambda b, _: far(b, dp_ref.at[b - 1]), 0)

    @pl.when(chips == 3)
    def _():
        far(3, dp3_ref)

    for dist, ref in ((1, c1), (2, c2), (3, c3)):

        @pl.when(chips >= dist)
        def _():
            ref[...] = g_s[dist - 1]

        @pl.when(chips < dist)
        def _():
            ref[...] = jnp.zeros((HEADS, 2 * SUB, HD), BF16)


def query_kernel(
    where_ref, all_ref, sw_ref, a1, a2, a3, ds_ref, o_ref, f_ref, r_ref, p_ref, dp0_ref, dpo_ref,
    mine_ref, other_ref, own_ref, kt_s, g_s, ds0_s,
):
    chips = where_ref[0]
    dk, dv = key_grads(p_ref.at[0], dp0_ref, dpo_ref.at[0], ds0_s, f_ref, r_ref, all_ref, sw_ref)
    own_ref[:, 0:SUB, :] = dk.reshape(HEADS, SUB, HD)
    own_ref[:, SUB : 2 * SUB, :] = dv.reshape(HEADS, SUB, HD)
    for n, ref in enumerate((all_ref, a1, a2, a3)):
        kt_s[n] = ref[:, 0:SUB, :].reshape(TOK, HD).T
    for at in columns():
        g_s[:, at] = dot(kt_s[0], ds0_s[:, at])

    def add(b, _):
        for at in columns():
            g_s[:, at] += dot(kt_s[b], ds_ref[b - 1, :, at])
        return 0

    lax.fori_loop(1, chips + 1, add, 0)
    for n, ref in enumerate((mine_ref, other_ref)):
        at = slice(n * ROWS, (n + 1) * ROWS)
        o = (o_ref[:, at] * f_ref[0:1, at]).T
        g = (g_s[:, at] * SCALING).T
        ref[:, 0:128, :] = o.reshape(HEADS, 128, HD).astype(ref.dtype)
        ref[:, 128:256, :] = g.reshape(HEADS, 128, HD).astype(ref.dtype)


def sum_kernel(own_ref, c1, c2, c3, out_ref):
    total = own_ref[...]
    for ref in (c1, c2, c3):
        total = total + ref[...].astype(F32)
    out_ref[...] = total.astype(BF16)


def shape(*dims, dtype=BF16):
    return jax.ShapeDtypeStruct(dims, dtype)


def run(kernel, outs, scratch, *operands, first=SM, out=VM, cost=None):
    return pl.pallas_call(
        kernel,
        out_shape=outs,
        in_specs=[first] + [VM] * (len(operands) - 1),
        out_specs=tuple(out for _ in outs),
        scratch_shapes=scratch,
        compiler_params=params(),
        cost_estimate=cost,
    )(*operands)


def pack(shift, k, v, q, d):
    return pl.pallas_call(
        pack_kernel,
        out_shape=shape(HEADS, WIDE, HD),
        in_specs=[pl.BlockSpec(memory_space=pl.ANY)] * 5,
        out_specs=pl.BlockSpec(memory_space=pl.ANY),
        scratch_shapes=[
            pltpu.SMEM((HEADS,), jnp.int32),
            pltpu.VMEM((TOK, HD), BF16),
            pltpu.VMEM((TOK, HD), BF16),
            pltpu.VMEM((ROWS, HD), BF16),
            pltpu.VMEM((ROWS, HD), BF16),
            pltpu.VMEM((HEADS, QAT, HD), BF16),
            pltpu.VMEM((2, HEADS, 128, HD), BF16),
            pltpu.SemaphoreType.DMA((8,)),
        ],
        compiler_params=pltpu.CompilerParams(vmem_limit_bytes=60 * 1024 * 1024),
    )(shift, k, v, q, d)


def rows_of_groups():
    rows = []
    for start in range(0, 64, 8):
        for core in range(2):
            for place in range(HEADS):
                moved = GROUP // 2 // TOK if place >= HEADS // 2 else 0
                rows.append([(start + moved + 2 * i + core) % 64 * 8 + place for i in range(4)])
    return rows


ALONG = rows_of_groups()
SWAP = [(s * 8 + h, (s ^ 1) * 8 + h) for s in range(64) for h in range(8)]


def ahead(x, dist):
    return lax.ppermute(x, AXES, [(r[i], r[i + dist]) for r in ALONG for i in range(4 - dist)])


def behind(x, dist):
    return lax.ppermute(x, AXES, [(r[i + dist], r[i]) for r in ALONG for i in range(4 - dist)])


def local(queries, keys, values, d_attended, shift_amounts):
    seq_pos = lax.axis_index("seq")
    place = lax.axis_index("head")
    in_group = (seq_pos - jnp.where(place >= HEADS // 2, 4, 0)) & 7
    where = jnp.stack((in_group >> 1, in_group & 1)).astype(jnp.int32)
    packed = pack(
        shift_amounts,
        keys.reshape(TOK, HD),
        values.reshape(TOK, HD),
        queries.reshape(ROWS, HD),
        d_attended.reshape(ROWS, HD),
    )
    everything = lax.all_to_all(packed, "head", 0, 0, tiled=True)
    own = everything[:, 0 : 2 * SUB]
    a = [ahead(own, dist) for dist in (1, 2, 3)]
    swapped = lax.ppermute(everything[:, QAT:WIDE], AXES, SWAP)
    rows = pltpu.VMEM((8, BOTH), F32)
    flat = shape(8, BOTH, dtype=F32)
    part, half, top = shape(TOK, ROWS, dtype=F32), shape(HD, ROWS), shape(8, ROWS, dtype=F32)
    qt, dt, s0, dp0, m0 = run(
        first_kernel, (half, half, part, part, top), [], everything, first=VM, cost=LONG
    )
    s3, dp3, m3 = run(early_kernel, (part, part, top), [], where, qt, dt, a[2], cost=LONG)
    qo, do, s0o, dp0o, m0o = run(
        other_kernel, (half, half, part, part, top), [], where, everything, swapped, cost=None
    )
    s3o, dp3o, m3o = run(early_kernel, (part, part, top), [], where, qo, do, a[2])
    held, turned = pltpu.VMEM((4, TOK, HD), BF16), pltpu.VMEM((HD, ROWS), BF16)
    probs, dp, dpo, stats = run(
        probs_kernel,
        (
            shape(4, TOK, BOTH, dtype=F32),
            shape(2, TOK, ROWS, dtype=F32),
            shape(4, TOK, ROWS, dtype=F32),
            flat,
        ),
        [held, held, rows, rows, rows],
        where, qt, dt, s0, dp0, m0, s3, dp3, m3, qo, do, s0o, dp0o, m0o, s3o, dp3o, m3o, *a,
    )
    swapped_stats = lax.ppermute(stats, AXES, SWAP)
    (o,) = run(
        attended_kernel,
        (shape(HD, BOTH, dtype=F32),),
        [pltpu.VMEM((4, HD, TOK), BF16)],
        where, everything, *a, probs,
        cost=LONG,
    )
    block = shape(HEADS, 2 * SUB, HD)
    c1, c2, c3, ds, f, row_dot = run(
        grads_kernel,
        (block, block, block, shape(3, TOK, BOTH), flat, flat),
        [pltpu.VMEM((3, HEADS, 2 * SUB, HD), BF16)],
        where, stats, swapped_stats, everything, swapped, probs, dp, dp3, dpo,
    )
    back = [behind(part, dist) for dist, part in zip((1, 2, 3), (c1, c2, c3))]
    mine, other, grads = run(
        query_kernel,
        (shape(HEADS, 256, HD, dtype=F32), shape(HEADS, 256, HD), shape(HEADS, 2 * SUB, HD, dtype=F32)),
        [pltpu.VMEM((4, HD, TOK), BF16), pltpu.VMEM((HD, BOTH), F32), pltpu.VMEM((TOK, BOTH), BF16)],
        where, everything, swapped, *a, ds, o, f, row_dot, probs, dp0, dpo,
        cost=LONG,
    )
    oq = (mine + lax.ppermute(other, AXES, SWAP).astype(F32)).astype(BF16)
    (grads,) = run(sum_kernel, (block,), [], *(grads, *back), first=VM, cost=LONG)
    done = lax.all_to_all(jnp.concatenate((grads, oq), axis=1), "head", 0, 0, tiled=True)
    attended, d_queries, d_keys, d_values = run(
        unpack_kernel,
        (shape(ROWS, HD), shape(ROWS, HD), shape(TOK, HD), shape(TOK, HD)),
        [
            pltpu.VMEM((ROWS, HD), BF16),
            pltpu.VMEM((ROWS, HD), BF16),
            pltpu.VMEM((TOK, HD), BF16),
            pltpu.VMEM((TOK, HD), BF16),
            pltpu.SemaphoreType.DMA((4,)),
        ],
        shift_amounts,
        done,
        out=pl.BlockSpec(memory_space=pl.ANY),
    )
    return (
        attended.reshape(SUB, HEADS, PER, HD),
        d_queries.reshape(SUB, HEADS, PER, HD),
        d_keys.reshape(SUB, HEADS, HD),
        d_values.reshape(SUB, HEADS, HD),
    )


def solution(mesh):
    wide = P(("seq", "head"), None, None, None)
    flat = P(("seq", "head"), None, None)
    return jax.shard_map(
        local,
        mesh=mesh,
        in_specs=(wide, flat, flat, wide, P()),
        out_specs=(wide, wide, flat, flat),
        check_vma=False,
    )
```
